768 devices in a mesh: lat: 48 (over z, x_hi, core), lon: 16 (over x_lo, y).
Axes of the slice: x: 4 (x_hi: 2, x_lo: 2; x = x_hi * 2 + x_lo), y: 8, z: 12, core: 2. Of those that a mesh axis runs over, the one named last changes fastest.
Arguments:
- elem_codes: int32 [768, 128, 256], P('lat', 'lon'), may hold values from 32 to 207, as said below
- block_exps: int32 [768, 128, 8], P('lat', 'lon'), may hold values from -2 to 1
- up_kernel: bfloat16 [4, 4, 256, 128], replicated, may hold values from -0.1875 to 0.1875
- up_bias: float32 [128], replicated, may hold values from -3 to 3
- mix_kernel: bfloat16 [3, 3, 128, 128], replicated, may hold values from -0.1875 to 0.1875
- cotangent: bfloat16 [1536, 256, 128], P('lat', 'lon'), may hold values from -6 to 6
Outputs:
- section_out: bfloat16 [1536, 256, 128], P('lat', 'lon')
- input_grad: float32 [768, 128, 256], P('lat', 'lon')
- up_grad: float32 [4, 4, 256, 128], P(None, None, 'lon')
- mix_grad: float32 [3, 3, 128, 128], P(None, None, 'lon')
The draws below stay inside these ranges and needn't reach their ends.
Inputs may be any that keep to these rules, and one draw needn't show every extreme that they name: `elem_codes`: every code has a sign bit of weight 128, a four-bit exponent field from 4 to 9 and a three-bit mantissa.
All inputs are finite; a program needn't handle non-finite values.
Results may differ from the reference program's by a relative error of at most 0.012.
Values may be sent and summed in bfloat16 or wider, within the bound.
A program may use at most 32 MiB of HBM per device.

```python
import math
import jax
import jax.numpy as jnp
from jax import lax

CIN = 256
COUT = 128
BLOCK = 32
IN_ROWS = 768
IN_COLS = 128
OUT_ROWS = 1536
OUT_COLS = 256
SB = 8


def draw_elem_codes(key, part):
    sign_key, exponent_key, mantissa_key = jax.random.split(key, 3)
    shape = (IN_ROWS, IN_COLS, CIN)
    sign_bit = jax.random.randint(sign_key, shape, 0, 2)
    exponent = jax.random.randint(exponent_key, shape, 4, 10)
    mantissa = jax.random.randint(mantissa_key, shape, 0, 8)
    return (sign_bit * 128 + exponent * 8 + mantissa).astype(jnp.int32)


def with_ends(array, key, smallest, top_value):
    longest = array.shape.index(max(array.shape))
    spots = []
    for shift in (0, 1):
        where = [jax.random.randint(jax.random.fold_in(key, axis), (), 0, length) for axis, length in enumerate(array.shape)]
        where[longest] = (where[longest] + shift) % array.shape[longest]
        spots.append(tuple(where))
    return array.at[spots[0]].set(smallest).at[spots[1]].set(top_value)


def levels(own_key, extent, pieces, low, top_value):
    def one(dim, blocks):
        steps = jax.random.uniform(jax.random.fold_in(jax.random.fold_in(own_key, 6), dim), (blocks,), jnp.float32, low / len(pieces), top_value / len(pieces))
        return jnp.repeat(jnp.exp(steps), extent[dim] // blocks).reshape((-1,) + (1,) * (len(extent) - dim - 1))

    level = one(*pieces[0])
    for cut in pieces[1:]:
        level = level * one(*cut)
    return level


def centred(stream_key, extent, width, limit, shards=(), dtype=jnp.bfloat16):
    entries = width * jax.random.normal(stream_key, extent, jnp.float32)
    if shards:
        entries = entries * levels(stream_key, extent, shards, -0.22, 0.18)
    return jnp.clip(entries, -limit, limit).astype(dtype)


def setup_inputs(seed: int = 0) -> dict:
    seeds = jax.random.split(jax.random.key(seed), 7)
    elem_codes = draw_elem_codes(jax.random.fold_in(seeds[6], 71), 0)
    block_exps = with_ends(jax.random.randint(seeds[1], (IN_ROWS, IN_COLS, SB), -2, 2), jax.random.fold_in(seeds[1], 1), -2, 1).astype(jnp.int32)
    up_kernel = centred(seeds[2], (4, 4, CIN, COUT), (4 * CIN) ** -0.5, 0.1875)
    up_bias = centred(seeds[3], (COUT,), 0.5, 3.0, (), jnp.float32)
    mix_kernel = centred(seeds[4], (3, 3, COUT, COUT), (9 * COUT) ** -0.5, 0.1875)
    cotangent = centred(seeds[5], (OUT_ROWS, OUT_COLS, COUT), 1.0, 6.0, ((0, 48), (1, 16)))
    return {"elem_codes": elem_codes, "block_exps": block_exps, "up_kernel": up_kernel, "up_bias": up_bias, "mix_kernel": mix_kernel, "cotangent": cotangent}


row_taps = (((1, 0), (3, -1)), ((0, 1), (2, 0)))

def decode(elem_codes, block_exps):
    sign_bit = elem_codes // 128
    exponent = elem_codes // 8 % 16
    mantissa = elem_codes % 8
    magnitude = jnp.exp2((exponent - 7).astype(jnp.float32)) * (1.0 + mantissa.astype(jnp.float32) / 8.0)
    signed = jnp.where(sign_bit == 1, -magnitude, magnitude)
    factor = jnp.repeat(jnp.exp2(block_exps.astype(jnp.float32)), BLOCK, axis=2)
    return (signed * factor).astype(jnp.bfloat16)

def extend(field, margin):
    widened = jnp.concatenate([field[:, -margin:], field, field[:, :margin]], axis=1)
    return jnp.pad(widened, ((margin, margin), (0, 0), (0, 0)))

def slope(pre_act):
    plain = pre_act.astype(jnp.float32)
    sigmoid_v = jax.nn.sigmoid(plain)
    return sigmoid_v * (1.0 + plain * (1.0 - sigmoid_v))

def matmul(left, right):
    return jnp.einsum('rcm,mn->rcn', left, right, precision=lax.Precision.HIGHEST)

def reference(elem_codes, block_exps, up_kernel, up_bias, mix_kernel, cotangent):
    inputs = decode(elem_codes, block_exps).astype(jnp.float32)
    up_wide = up_kernel.astype(jnp.float32)
    mix_wide = mix_kernel.astype(jnp.float32)
    grad_wide = cotangent.astype(jnp.float32)
    in_rows, in_cols = (inputs.shape[0], inputs.shape[1])
    out_rows, out_cols = (2 * in_rows, 2 * in_cols)
    padded_in = extend(inputs, 1)
    halves = []
    for row_par in range(2):
        lane_list = []
        for col_par in range(2):
            total = jnp.zeros((in_rows, in_cols, COUT), jnp.float32)
            for row_tap, row_off in row_taps[row_par]:
                for col_tap, col_off in row_taps[col_par]:
                    window = padded_in[1 + row_off:1 + row_off + in_rows, 1 + col_off:1 + col_off + in_cols]
                    total = total + matmul(window, up_wide[row_tap, col_tap])
            lane_list.append(total)
        halves.append(jnp.stack(lane_list, axis=2))
    raw = jnp.stack(halves, axis=1).reshape(out_rows, out_cols, COUT)
    pre_act = (raw + up_bias).astype(jnp.bfloat16)
    activated = jax.nn.silu(pre_act.astype(jnp.float32)).astype(jnp.bfloat16)
    act_pad = extend(activated.astype(jnp.float32), 1)
    grad_pad = extend(grad_wide, 1)
    grad_scale = 1.0 / math.sqrt(OUT_ROWS * OUT_COLS)
    total = jnp.zeros((out_rows, out_cols, COUT), jnp.float32)
    act_grad = jnp.zeros((out_rows, out_cols, COUT), jnp.float32)
    mix_list = []
    for row_tap in range(3):
        for col_tap in range(3):
            window = act_pad[row_tap:row_tap + out_rows, col_tap:col_tap + out_cols]
            total = total + matmul(window, mix_wide[row_tap, col_tap])
            flipped = grad_pad[2 - row_tap:2 - row_tap + out_rows, 2 - col_tap:2 - col_tap + out_cols]
            act_grad = act_grad + matmul(flipped, mix_wide[row_tap, col_tap].T)
            mix_list.append(jnp.einsum('rcm,rcn->mn', window, grad_wide, precision=lax.Precision.HIGHEST))
    section_out = total.astype(jnp.bfloat16)
    mix_grad = jnp.stack(mix_list, axis=0).reshape(3, 3, COUT, COUT) * grad_scale
    pre_grad = (act_grad * slope(pre_act)).astype(jnp.bfloat16)
    pre_pad = extend(pre_grad.astype(jnp.float32), 1)
    input_grad = jnp.zeros((in_rows, in_cols, CIN), jnp.float32)
    up_list = []
    for row_tap in range(4):
        for col_tap in range(4):
            window = pre_pad[row_tap:row_tap + 2 * in_rows:2, col_tap:col_tap + 2 * in_cols:2]
            input_grad = input_grad + matmul(window, up_wide[row_tap, col_tap].T)
            up_list.append(jnp.einsum('rcm,rcn->mn', inputs, window, precision=lax.Precision.HIGHEST))
    up_grad = jnp.stack(up_list, axis=0).reshape(4, 4, CIN, COUT) * grad_scale
    return (section_out, input_grad, up_grad, mix_grad)
```

```python
import functools
import math

import jax
import jax.numpy as jnp
from jax import lax
from jax.experimental import pallas as pl
from jax.experimental.pallas import tpu as pltpu
from jax.sharding import PartitionSpec as P

CIN = 256
COUT = 128
ROWS = 16
COLS = 8
PITCH = 10
CELLS = ROWS * COLS
TALL = CIN // COUT + 4
FLAT = 192
OUTER = 176
INNER = ROWS * PITCH
PARTS = 3
SPAN = 2 * COUT
TILES = 4 * PARTS
LON_ALL = 16
MESH = pl.DeviceIdType.MESH
F32 = jnp.float32
BF16 = jnp.bfloat16


def power_bits(value, bits):
    total = jnp.where(value & 1 != 0, 2.0, 1.0)
    for bit in range(1, bits):
        total = total * jnp.where(value & (1 << bit) != 0, float(1 << (1 << bit)), 1.0)
    return total


def decode(codes, exps):
    sign = jnp.where(codes >= 128, -(2.0**-9), 2.0**-9)
    fraction = (8 + (codes & 7)).astype(F32) * 0.125
    signed = sign * power_bits((codes >> 3) & 15, 4) * fraction
    factor = power_bits(exps + 2, 2).astype(BF16)
    blocks = exps.shape[1]
    channel = lax.broadcasted_iota(jnp.int32, (blocks, CIN), 1)
    block = lax.broadcasted_iota(jnp.int32, (blocks, CIN), 0)
    spread = jnp.where(channel // (CIN // blocks) == block, 1.0, 0.0).astype(BF16)
    return signed * jnp.dot(factor, spread, preferred_element_type=F32)


def halo_partners(lat, lon, lat_count, lon_count):
    up, down = lax.rem(lat + lat_count - 1, lat_count), lax.rem(lat + 1, lat_count)
    left, right = lax.rem(lon + lon_count - 1, lon_count), lax.rem(lon + 1, lon_count)
    return up, down, left, right


def halo_fill(codes, exps, cot, grid, own, cot_wide, row_out, col_out, corner_out):
    decoded = decode(codes[...], exps[...])
    for i in range(CIN // COUT):
        own[i] = decoded[:, i * COUT : (i + 1) * COUT]
    cot_wide[...] = cot[...].astype(F32)
    for r in range(ROWS):
        for s in range(2):
            for t in range(2):
                own[2 + 2 * s + t, r * COLS : (r + 1) * COLS, :] = cot_wide[
                    pl.ds((2 * r + s) * 2 * COLS + t, COLS, stride=2), :
                ]
    for side, r in enumerate((ROWS - 1, 0)):
        for i in range(TALL // 2):
            row_out[side, i] = jnp.concatenate(
                [own[j, r * COLS : (r + 1) * COLS, :] for j in (2 * i, 2 * i + 1)], axis=0
            ).astype(BF16)
    for side, c in enumerate((COLS - 1, 0)):
        for i in range(TALL):
            col_out[side, i] = own[i, pl.ds(c, ROWS, stride=COLS), :].astype(BF16)
    for corner, (r, c) in enumerate(((ROWS - 1, COLS - 1), (ROWS - 1, 0), (0, COLS - 1), (0, 0))):
        cell = r * COLS + c
        corner_out[corner] = jnp.zeros((8, COUT), F32)
        for i in range(TALL):
            corner_out[corner, i : i + 1, :] = own[i, cell : cell + 1, :]
    for r in range(ROWS):
        at = (r + 1) * PITCH + 1
        for i in range(TALL):
            grid[i, at : at + COLS, :] = own[i, r * COLS : (r + 1) * COLS, :]
    tail = (ROWS + 2) * PITCH
    for i in range(TALL):
        grid[i, tail:FLAT, :] = jnp.zeros((FLAT - tail, COUT), F32)


def halo_copies(partners, lat, lon, row_out, col_out, corner_out, row_in, col_in, corner_in, send, recv):
    up, down, left, right = partners
    plan = [
        (row_out.at[0], row_in.at[0], down, lon),
        (row_out.at[1], row_in.at[1], up, lon),
        (col_out.at[0], col_in.at[0], lat, right),
        (col_out.at[1], col_in.at[1], lat, left),
        (corner_out.at[0], corner_in.at[0], down, right),
        (corner_out.at[1], corner_in.at[1], down, left),
        (corner_out.at[2], corner_in.at[2], up, right),
        (corner_out.at[3], corner_in.at[3], up, left),
    ]
    return [
        pltpu.make_async_remote_copy(
            src_ref=src,
            dst_ref=dst,
            send_sem=send.at[i],
            recv_sem=recv.at[i],
            device_id=(to_lat, to_lon),
            device_id_type=MESH,
        )
        for i, (src, dst, to_lat, to_lon) in enumerate(plan)
    ]


def halo_place(lat, lat_count, grid, row_in, col_in, corner_in):
    above = (lat > 0).astype(F32)
    below = (lat < lat_count - 1).astype(F32)
    for side, (r, keep) in enumerate(((0, above), (ROWS + 1, below))):
        at = r * PITCH + 1
        for i in range(TALL // 2):
            part = row_in[side, i].astype(F32) * keep
            grid[2 * i, at : at + COLS, :] = part[:COLS]
            grid[2 * i + 1, at : at + COLS, :] = part[COLS:]
    for side, c in enumerate((0, COLS + 1)):
        for i in range(TALL):
            grid[i, pl.ds(PITCH + c, ROWS, stride=PITCH), :] = col_in[side, i].astype(F32)
    places = ((0, 0, above), (0, COLS + 1, above), (ROWS + 1, 0, below), (ROWS + 1, COLS + 1, below))
    for corner, (r, c, keep) in enumerate(places):
        cell = r * PITCH + c
        for i in range(TALL):
            grid[i, cell : cell + 1, :] = corner_in[corner, i : i + 1, :] * keep


def halo_kernel(
    lat_count,
    lon_count,
    codes,
    exps,
    cot,
    grid,
    own,
    cot_wide,
    row_out,
    col_out,
    corner_out,
    row_in,
    col_in,
    corner_in,
    send,
    recv,
):
    lat, lon = lax.axis_index("lat"), lax.axis_index("lon")
    partners = halo_partners(lat, lon, lat_count, lon_count)
    up, down, left, right = partners
    barrier = pltpu.get_barrier_semaphore()
    for to_lat in (up, lat, down):
        for to_lon in (left, lon, right):
            if to_lat is lat and to_lon is lon:
                continue
            pl.semaphore_signal(barrier, inc=1, device_id=(to_lat, to_lon), device_id_type=MESH)
    halo_fill(codes, exps, cot, grid, own, cot_wide, row_out, col_out, corner_out)
    pl.semaphore_wait(barrier, 8)
    copies = halo_copies(
        partners, lat, lon, row_out, col_out, corner_out, row_in, col_in, corner_in, send, recv
    )
    for copy in copies:
        copy.start()
    for copy in copies:
        copy.wait()
    halo_place(lat, lat_count, grid, row_in, col_in, corner_in)


OFFSETS = ((0, 0), (0, 1), (1, 0), (1, 1))


def positions(ref, length, low):
    found = {}
    for dr, dc in OFFSETS:
        for pr in range(2):
            for pc in range(2):
                found[2 * dr + pr, 2 * dc + pc] = ref[
                    low + 2 * pr + pc, pl.ds(dr * PITCH + dc, length), :
                ].astype(BF16)
    return found


def window(ref, start, length, low, high):
    return jnp.concatenate([ref[i, pl.ds(start, length), :] for i in range(low, high)], axis=1)


def keep_wide(ref, value):
    for i in range(4):
        ref[i, :OUTER, :] = value[:, i * COUT : (i + 1) * COUT]
        ref[i, OUTER:, :] = jnp.zeros((FLAT - OUTER, COUT), F32)


def patches(found, flipped):
    stacked = []
    for s in range(2):
        for t in range(2):
            pieces = []
            for ky in range(3):
                for kx in range(3):
                    at = (s - ky + 2, t - kx + 2) if flipped else (s + ky, t + kx)
                    pieces.append(found[at])
            stacked.append(jnp.concatenate(pieces, axis=1))
    return jnp.concatenate(stacked, axis=0)


def beside(array, rows):
    return jnp.concatenate([array[i * rows : (i + 1) * rows] for i in range(4)], axis=1)


def inner_mask(lanes):
    cell = lax.broadcasted_iota(jnp.int32, (INNER, lanes), 0)
    return lax.rem(cell, PITCH) < COLS


def compute_kernel(
    lat_count, grid, up_kernel, bias, mix_kernel, section, input_grad, sums, act, pre_grad, staged, out_wide, wide
):
    lat = lax.axis_index("lat")
    windows = [
        window(grid, dr * PITCH + dc, OUTER, 0, 2).astype(BF16) for dr, dc in OFFSETS
    ]
    forward = jnp.concatenate(
        [
            jnp.concatenate(
                [
                    up_kernel[(2 * (1 - dr) + pr) * 4 + 2 * (1 - dc) + pc]
                    for pr in range(2)
                    for pc in range(2)
                ],
                axis=1,
            )
            for dr, dc in OFFSETS
        ],
        axis=0,
    )
    raw = jnp.dot(jnp.concatenate(windows, axis=1), forward, preferred_element_type=F32)
    plain = (raw + jnp.concatenate([bias[...]] * 4, axis=1)).astype(BF16).astype(F32)
    sigmoid = jax.nn.sigmoid(plain)
    activated = (plain * sigmoid).astype(BF16).astype(F32)
    cell = lax.broadcasted_iota(jnp.int32, (OUTER, 4 * COUT), 0)
    lane = lax.broadcasted_iota(jnp.int32, (OUTER, 4 * COUT), 1)
    outside = ((cell < PITCH) & (lane < 2 * COUT) & (lat == 0)) | (
        (cell >= ROWS * PITCH) & (lane >= 2 * COUT) & (lat == lat_count - 1)
    )
    keep_wide(act, jnp.where(outside, 0.0, activated))

    act_patches = patches(positions(act, INNER, 0), False)
    cot_own = window(grid, PITCH + 1, INNER, 2, TALL)
    cot_own = jnp.where(inner_mask(4 * COUT), cot_own, 0.0).astype(BF16)
    cot_stacked = jnp.concatenate([cot_own[:, i * COUT : (i + 1) * COUT] for i in range(4)], axis=0)
    mix_sum = lax.dot_general(
        act_patches, cot_stacked, (((0,), (0,)), ((), ())), preferred_element_type=F32
    )
    for w in range(4):
        for slot in range(4):
            tap = slot * 4 + w
            at = (slot // 2) * COUT
            part = jnp.zeros((LON_ALL, 8, COUT), F32)
            if tap < 9:
                part = mix_sum[tap * COUT : (tap + 1) * COUT].reshape(LON_ALL, 8, COUT)
            wide[w // 2, 2, w % 2, :, slot % 2, :, at : at + COUT] = part

    backward = jnp.concatenate([mix_kernel[i] for i in range(9)], axis=1)
    act_grad = lax.dot_general(
        patches(positions(grid, OUTER, 2), True),
        backward,
        (((1,), (1,)), ((), ())),
        preferred_element_type=F32,
    )
    slope = sigmoid * (1.0 + plain * (1.0 - sigmoid))
    graded = (beside(act_grad, OUTER) * slope).astype(BF16).astype(F32)
    keep_wide(pre_grad, jnp.where(outside, 0.0, graded))
    grad_windows = jnp.concatenate(
        [window(pre_grad, dr * PITCH + dc, INNER, 0, 4).astype(BF16) for dr, dc in OFFSETS], axis=1
    )
    in_own = window(grid, PITCH + 1, INNER, 0, 2)
    in_own = jnp.where(inner_mask(CIN), in_own, 0.0).astype(BF16)
    up_sum = lax.dot_general(
        in_own, grad_windows, (((0,), (0,)), ((), ())), preferred_element_type=F32
    )
    for dr, dc in OFFSETS:
        for pr in range(2):
            for pc in range(2):
                source = ((2 * dr + dc) * 4 + 2 * pr + pc) * COUT
                at = pc * COUT
                wide[dr, dc, pr, :, :, :, at : at + COUT] = up_sum[
                    :, source : source + COUT
                ].reshape(LON_ALL, 2, 8, COUT)
    for core in range(2):
        for part in range(PARTS):
            for x_hi in range(2):
                sums[core, part, x_hi] = wide[core, part, x_hi].reshape(CIN, SPAN).astype(BF16)

    flat_mix = mix_kernel[...].reshape(9 * COUT, COUT)
    staged[...] = jnp.dot(act_patches, flat_mix, preferred_element_type=F32)
    for s in range(2):
        for t in range(2):
            for r in range(ROWS):
                out_wide[pl.ds((2 * r + s) * 2 * COLS + t, COLS, stride=2), :] = staged[
                    pl.ds((2 * s + t) * INNER + r * PITCH, COLS), :
                ]
    section[...] = out_wide[...].astype(BF16)
    back_up = jnp.concatenate(
        [
            up_kernel[(2 * dr + pr) * 4 + 2 * dc + pc]
            for dr, dc in OFFSETS
            for pr in range(2)
            for pc in range(2)
        ],
        axis=1,
    )
    spread = lax.dot_general(
        grad_windows, back_up, (((1,), (1,)), ((), ())), preferred_element_type=F32
    )
    for i in range(2):
        act[i, :INNER, :] = spread[:, i * COUT : (i + 1) * COUT]
        for r in range(ROWS):
            input_grad[r * COLS : (r + 1) * COLS, i * COUT : (i + 1) * COUT] = act[
                i, pl.ds(r * PITCH, COLS), :
            ]


def reduce_partners(lat, lon, z_count, y_count):
    core, x_hi, z = lax.rem(lat, 2), lax.rem(lat // 2, 2), lat // 4
    y, x_lo = lax.rem(lon, y_count), lon // y_count
    return core, x_hi, z, y, x_lo


def fetch(src, dst, send, recv, to):
    copy = pltpu.make_async_remote_copy(
        src_ref=src, dst_ref=dst, send_sem=send, recv_sem=recv, device_id=to, device_id_type=MESH
    )
    copy.start()


def await_bytes(ref, sem):
    pltpu.make_async_copy(ref, ref, sem).wait()


def reduce_kernel(
    z_count,
    y_count,
    scale,
    sums,
    final,
    core_in,
    x_out,
    x_in,
    y_out,
    y_in,
    z_out,
    z_in,
    z_all,
    core_sem,
    x_sem,
    y_sem,
    z_sem,
):
    lat, lon = lax.axis_index("lat"), lax.axis_index("lon")
    core, x_hi, z, y, x_lo = reduce_partners(lat, lon, z_count, y_count)
    x = 2 * x_hi + x_lo
    own = 2 * core + x_hi

    def across_x(step):
        other = lax.rem(x + step, 4)
        return (4 * z + 2 * (other // 2) + core, (other % 2) * y_count + y), other

    def across_y(step):
        other = lax.rem(y + step, y_count)
        return (lat, x_lo * y_count + other), other

    def across_z(step):
        other = lax.rem(z + step, z_count)
        return (4 * other + 2 * x_hi + core, lon), other

    def across_inner(step):
        other = lax.rem(own + step, 4)
        return (4 * z + 2 * (other % 2) + other // 2, lon), other

    barrier = pltpu.get_barrier_semaphore()

    def greet(to):
        pl.semaphore_signal(barrier, inc=1, device_id=to, device_id_type=MESH)

    total = 0
    for count, reach in ((4, across_x), (y_count, across_y), (z_count, across_z), (4, across_inner)):
        for step in range(1, count):
            greet(reach(step)[0])
        total += count - 1
    pl.semaphore_wait(barrier, total)

    partner = (lat + 1 - 2 * core, lon)
    for part in range(PARTS):
        fetch(sums.at[1 - core, part], core_in.at[part], core_sem.at[0, part], core_sem.at[1, part], partner)
    for part in range(PARTS):
        await_bytes(core_in.at[part], core_sem.at[1, part])
        x_out[part] = (
            (sums[core, part].astype(F32) + core_in[part].astype(F32))
            .astype(BF16)
            .reshape(x_out.shape[1:])
        )
        for step in range(1, 4):
            to, other = across_x(step)
            fetch(
                x_out.at[part, other // 2, other % 2],
                x_in.at[part, step - 1],
                x_sem.at[0, part],
                x_sem.at[1, part],
                to,
            )
    for part in range(PARTS):
        await_bytes(x_in.at[part], x_sem.at[1, part])
        total = x_out[part, x_hi, x_lo].astype(F32)
        for step in range(3):
            total = total + x_in[part, step].astype(F32)
        y_out[part] = total.astype(BF16).reshape(y_out.shape[1:])
        for step in range(1, y_count):
            to, other = across_y(step)
            fetch(y_out.at[part, other], y_in.at[part, step - 1], y_sem.at[0, part], y_sem.at[1, part], to)
    per = TILES // z_count
    for part in range(PARTS):
        await_bytes(y_in.at[part], y_sem.at[1, part])
        total = y_out[part, y].astype(F32)
        for step in range(y_count - 1):
            total = total + y_in[part, step].astype(F32)
        for i in range(2):
            for half in range(2):
                tile = part * 4 + i * 2 + half
                z_out[tile // per, tile % per] = total[half * 8 : half * 8 + 8, i * COUT : (i + 1) * COUT]
    for step in range(1, z_count):
        to, other = across_z(step)
        fetch(z_out.at[other], z_in.at[step - 1], z_sem.at[0], z_sem.at[1], to)
    await_bytes(z_in, z_sem.at[1])
    total = z_out[z]
    for step in range(z_count - 1):
        total = total + z_in[step]
    z_all[z] = total * scale
    for step in range(1, z_count):
        to, _ = across_z(step)
        fetch(z_all.at[z], z_all.at[z], z_sem.at[2], z_sem.at[3], to)
    await_bytes(z_all.at[pl.ds(0, z_count - 1)], z_sem.at[3])
    for step in range(1, 4):
        to, _ = across_inner(step)
        fetch(z_all, final.at[own], z_sem.at[4], z_sem.at[5], to)
    final[own] = z_all[...]
    for part in range(PARTS):
        await_bytes(core_in.at[part], core_sem.at[0, part])
        await_bytes(x_in.at[part], x_sem.at[0, part])
        await_bytes(y_in.at[part], y_sem.at[0, part])
    await_bytes(z_in, z_sem.at[0])
    await_bytes(z_all.at[pl.ds(0, z_count - 1)], z_sem.at[2])
    await_bytes(final.at[pl.ds(0, 3)], z_sem.at[4])
    await_bytes(final.at[pl.ds(0, 3)], z_sem.at[5])


def vmem(count):
    return [pl.BlockSpec(memory_space=pltpu.VMEM)] * count


def shards(elem_codes, block_exps, up_kernel, up_bias, mix_kernel, cotangent):
    lat_count, lon_count = lax.axis_size("lat"), lax.axis_size("lon")
    y_count, z_count = lon_count // 2, lat_count // 4
    per = TILES // z_count
    limit = 48 * 2**20
    grid = pl.pallas_call(
        functools.partial(halo_kernel, lat_count, lon_count),
        out_shape=jax.ShapeDtypeStruct((TALL, FLAT, COUT), F32),
        in_specs=vmem(3),
        out_specs=vmem(1)[0],
        scratch_shapes=[
            pltpu.VMEM((TALL, CELLS, COUT), F32),
            pltpu.VMEM((4 * CELLS, COUT), F32),
            pltpu.VMEM((2, TALL // 2, 2 * COLS, COUT), BF16),
            pltpu.VMEM((2, TALL, ROWS, COUT), BF16),
            pltpu.VMEM((4, 8, COUT), F32),
            pltpu.VMEM((2, TALL // 2, 2 * COLS, COUT), BF16),
            pltpu.VMEM((2, TALL, ROWS, COUT), BF16),
            pltpu.VMEM((4, 8, COUT), F32),
            pltpu.SemaphoreType.DMA((8,)),
            pltpu.SemaphoreType.DMA((8,)),
        ],
        compiler_params=pltpu.CompilerParams(
            collective_id=0, has_side_effects=True, vmem_limit_bytes=limit
        ),
    )(
        elem_codes.reshape(CELLS, CIN),
        block_exps.reshape(CELLS, CIN // 32),
        cotangent.reshape(4 * CELLS, COUT),
    )
    section, input_grad, sums = pl.pallas_call(
        functools.partial(compute_kernel, lat_count),
        out_shape=(
            jax.ShapeDtypeStruct((4 * CELLS, COUT), BF16),
            jax.ShapeDtypeStruct((CELLS, CIN), F32),
            jax.ShapeDtypeStruct((2, PARTS, 2, CIN, SPAN), BF16),
        ),
        in_specs=vmem(4),
        out_specs=vmem(3),
        scratch_shapes=[
            pltpu.VMEM((4, FLAT, COUT), F32),
            pltpu.VMEM((4, FLAT, COUT), F32),
            pltpu.VMEM((4 * INNER, COUT), F32),
            pltpu.VMEM((4 * CELLS, COUT), F32),
            pltpu.VMEM((2, PARTS, 2, LON_ALL, 2, 8, SPAN), F32),
        ],
        compiler_params=pltpu.CompilerParams(vmem_limit_bytes=limit),
    )(
        grid,
        up_kernel.reshape(16, CIN, COUT),
        up_bias.reshape(1, COUT),
        mix_kernel.reshape(9, COUT, COUT),
    )
    out_cells = 4 * CELLS * lat_count * lon_count
    final = pl.pallas_call(
        functools.partial(reduce_kernel, z_count, y_count, 1.0 / math.sqrt(out_cells)),
        out_shape=jax.ShapeDtypeStruct((4, z_count, per, 8, COUT), F32),
        in_specs=vmem(1),
        out_specs=vmem(1)[0],
        scratch_shapes=[
            pltpu.VMEM((PARTS, 2, CIN, SPAN), BF16),
            pltpu.VMEM((PARTS, 2, 2, CIN // 2, SPAN), BF16),
            pltpu.VMEM((PARTS, 3, CIN // 2, SPAN), BF16),
            pltpu.VMEM((PARTS, y_count, 16, SPAN), BF16),
            pltpu.VMEM((PARTS, y_count - 1, 16, SPAN), BF16),
            pltpu.VMEM((z_count, per, 8, COUT), F32),
            pltpu.VMEM((z_count - 1, per, 8, COUT), F32),
            pltpu.VMEM((z_count, per, 8, COUT), F32),
            pltpu.SemaphoreType.DMA((2, PARTS)),
            pltpu.SemaphoreType.DMA((2, PARTS)),
            pltpu.SemaphoreType.DMA((2, PARTS)),
            pltpu.SemaphoreType.DMA((6,)),
        ],
        compiler_params=pltpu.CompilerParams(
            collective_id=1, has_side_effects=True, vmem_limit_bytes=limit
        ),
    )(sums)
    final = final.reshape(4, TILES, 8, COUT)
    up_part = final[:, :8].reshape(4, 4, CIN // lon_count, COUT)
    mix_part = jnp.stack([final[tap % 4, 8 + tap // 4] for tap in range(9)])
    return (
        section.reshape(2 * ROWS, 2 * COLS, COUT),
        input_grad.reshape(ROWS, COLS, CIN),
        up_part,
        mix_part.reshape(3, 3, 8, COUT),
    )


def solution(mesh):
    placed = (P("lat", "lon", None), P("lat", "lon", None), P(), P(), P(), P("lat", "lon", None))
    return jax.shard_map(
        shards,
        mesh=mesh,
        in_specs=placed,
        out_specs=(
            P("lat", "lon", None),
            P("lat", "lon", None),
            P(None, None, "lon", None),
            P(None, None, "lon", None),
        ),
        check_vma=False,
    )
```

```python
import functools
import math

import jax
import jax.numpy as jnp
from jax import lax
from jax.experimental import pallas as pl
from jax.experimental.pallas import tpu as pltpu
from jax.sharding import PartitionSpec as P

CIN = 256
COUT = 128
BLOCK = 32
ROWS = 16
COLS = 8
PITCH = 10
CELLS = ROWS * COLS
TALL = CIN // COUT + 4
FLAT = 192
OUTER = 176
INNER = ROWS * PITCH
PARTS = 3
SPAN = 2 * COUT
MIX = 2
ORDER = (2, 0, 1)
LON_ALL = 16
MESH = pl.DeviceIdType.MESH
F32 = jnp.float32
BF16 = jnp.bfloat16


def power_bits(value, bits):
    total = jnp.where(value & 1 != 0, 2.0, 1.0)
    for bit in range(1, bits):
        total = total * jnp.where(value & (1 << bit) != 0, float(1 << (1 << bit)), 1.0)
    return total


def decode(codes, factor):
    sign = jnp.where(codes >= 128, -(2.0**-9), 2.0**-9)
    fraction = (8 + (codes & 7)).astype(F32) * 0.125
    return sign * power_bits((codes >> 3) & 15, 4) * fraction * factor


def block_factors(exps, own):
    factor = power_bits(exps + 2, 2).astype(BF16)
    count = exps.shape[0]
    lane = lax.broadcasted_iota(jnp.int32, (count, COLS * CIN), 1)
    row = lax.broadcasted_iota(jnp.int32, (count, COLS * CIN), 0)
    spread = jnp.where(lane // BLOCK == row, 1.0, 0.0).astype(BF16)
    wide = lax.dot_general(factor, spread, (((0,), (0,)), ((), ())), preferred_element_type=F32)
    for c in range(COLS):
        for i in range(CIN // COUT):
            at = c * CIN + i * COUT
            own[i, pl.ds(c, ROWS, stride=COLS), :] = wide[:, at : at + COUT]


def halo_partners(lat, lon, lat_count, lon_count):
    up, down = lax.rem(lat + lat_count - 1, lat_count), lax.rem(lat + 1, lat_count)
    left, right = lax.rem(lon + lon_count - 1, lon_count), lax.rem(lon + 1, lon_count)
    return up, down, left, right


def halo_fill(codes, exps, cot, grid, own, cot_wide, row_out, col_out, corner_out):
    block_factors(exps[...], own)
    for i in range(CIN // COUT):
        own[i] = decode(codes[:, i * COUT : (i + 1) * COUT], own[i])
    cot_wide[...] = cot[...].astype(F32)
    for r in range(ROWS):
        for s in range(2):
            for t in range(2):
                own[2 + 2 * s + t, r * COLS : (r + 1) * COLS, :] = cot_wide[
                    pl.ds((2 * r + s) * 2 * COLS + t, COLS, stride=2), :
                ]
    for side, r in enumerate((ROWS - 1, 0)):
        for i in range(TALL // 2):
            row_out[side, i] = jnp.concatenate(
                [own[j, r * COLS : (r + 1) * COLS, :] for j in (2 * i, 2 * i + 1)], axis=0
            ).astype(BF16)
    for side, c in enumerate((COLS - 1, 0)):
        for i in range(TALL):
            col_out[side, i] = own[i, pl.ds(c, ROWS, stride=COLS), :].astype(BF16)
    for corner, (r, c) in enumerate(((ROWS - 1, COLS - 1), (ROWS - 1, 0), (0, COLS - 1), (0, 0))):
        cell = r * COLS + c
        corner_out[corner] = jnp.zeros((8, COUT), F32)
        for i in range(TALL):
            corner_out[corner, i : i + 1, :] = own[i, cell : cell + 1, :]
    for r in range(ROWS):
        at = (r + 1) * PITCH + 1
        for i in range(TALL):
            grid[i, at : at + COLS, :] = own[i, r * COLS : (r + 1) * COLS, :]
    tail = (ROWS + 2) * PITCH
    for i in range(TALL):
        grid[i, tail:FLAT, :] = jnp.zeros((FLAT - tail, COUT), F32)


def halo_copies(partners, lat, lon, row_out, col_out, corner_out, row_in, col_in, corner_in, send, recv):
    up, down, left, right = partners
    plan = [
        (row_out.at[0], row_in.at[0], down, lon),
        (row_out.at[1], row_in.at[1], up, lon),
        (col_out.at[0], col_in.at[0], lat, right),
        (col_out.at[1], col_in.at[1], lat, left),
        (corner_out.at[0], corner_in.at[0], down, right),
        (corner_out.at[1], corner_in.at[1], down, left),
        (corner_out.at[2], corner_in.at[2], up, right),
        (corner_out.at[3], corner_in.at[3], up, left),
    ]
    return [
        pltpu.make_async_remote_copy(
            src_ref=src,
            dst_ref=dst,
            send_sem=send.at[i],
            recv_sem=recv.at[i],
            device_id=(to_lat, to_lon),
            device_id_type=MESH,
        )
        for i, (src, dst, to_lat, to_lon) in enumerate(plan)
    ]


def halo_place(lat, lat_count, grid, row_in, col_in, corner_in):
    above = (lat > 0).astype(F32)
    below = (lat < lat_count - 1).astype(F32)
    for side, (r, keep) in enumerate(((0, above), (ROWS + 1, below))):
        at = r * PITCH + 1
        for i in range(TALL // 2):
            part = row_in[side, i].astype(F32) * keep
            grid[2 * i, at : at + COLS, :] = part[:COLS]
            grid[2 * i + 1, at : at + COLS, :] = part[COLS:]
    for side, c in enumerate((0, COLS + 1)):
        for i in range(TALL):
            grid[i, pl.ds(PITCH + c, ROWS, stride=PITCH), :] = col_in[side, i].astype(F32)
    places = ((0, 0, above), (0, COLS + 1, above), (ROWS + 1, 0, below), (ROWS + 1, COLS + 1, below))
    for corner, (r, c, keep) in enumerate(places):
        cell = r * PITCH + c
        for i in range(TALL):
            grid[i, cell : cell + 1, :] = corner_in[corner, i : i + 1, :] * keep


OFFSETS = ((0, 0), (0, 1), (1, 0), (1, 1))


def positions(ref, length, low):
    found = {}
    for dr, dc in OFFSETS:
        for pr in range(2):
            for pc in range(2):
                found[2 * dr + pr, 2 * dc + pc] = ref[
                    low + 2 * pr + pc, pl.ds(dr * PITCH + dc, length), :
                ].astype(BF16)
    return found


def window(ref, start, length, low, high):
    return jnp.concatenate([ref[i, pl.ds(start, length), :] for i in range(low, high)], axis=1)


def keep_wide(ref, value):
    for i in range(4):
        ref[i, :OUTER, :] = value[:, i * COUT : (i + 1) * COUT]
        ref[i, OUTER:, :] = jnp.zeros((FLAT - OUTER, COUT), F32)


def patches(found, flipped):
    stacked = []
    for s in range(2):
        for t in range(2):
            pieces = []
            for ky in range(3):
                for kx in range(3):
                    at = (s - ky + 2, t - kx + 2) if flipped else (s + ky, t + kx)
                    pieces.append(found[at])
            stacked.append(jnp.concatenate(pieces, axis=1))
    return jnp.concatenate(stacked, axis=0)


def beside(array, rows):
    return jnp.concatenate([array[i * rows : (i + 1) * rows] for i in range(4)], axis=1)


def inner_mask(lanes):
    cell = lax.broadcasted_iota(jnp.int32, (INNER, lanes), 0)
    return lax.rem(cell, PITCH) < COLS


def merge_slots(even, odd):
    return jnp.concatenate([even, odd], axis=1).reshape(CIN, COUT).astype(BF16)


def forward_part(lat, lat_count, grid, up_kernel, bias, act):
    windows = [window(grid, dr * PITCH + dc, OUTER, 0, 2).astype(BF16) for dr, dc in OFFSETS]
    forward = jnp.concatenate(
        [
            jnp.concatenate(
                [
                    up_kernel[(2 * (1 - dr) + pr) * 4 + 2 * (1 - dc) + pc]
                    for pr in range(2)
                    for pc in range(2)
                ],
                axis=1,
            )
            for dr, dc in OFFSETS
        ],
        axis=0,
    )
    raw = jnp.dot(jnp.concatenate(windows, axis=1), forward, preferred_element_type=F32)
    plain = (raw + jnp.concatenate([bias[...]] * 4, axis=1)).astype(BF16).astype(F32)
    sigmoid = jax.nn.sigmoid(plain)
    activated = (plain * sigmoid).astype(BF16).astype(F32)
    cell = lax.broadcasted_iota(jnp.int32, (OUTER, 4 * COUT), 0)
    lane = lax.broadcasted_iota(jnp.int32, (OUTER, 4 * COUT), 1)
    outside = ((cell < PITCH) & (lane < 2 * COUT) & (lat == 0)) | (
        (cell >= ROWS * PITCH) & (lane >= 2 * COUT) & (lat == lat_count - 1)
    )
    keep_wide(act, jnp.where(outside, 0.0, activated))
    return sigmoid * (1.0 + plain * (1.0 - sigmoid)), outside


def mix_part_sums(grid, act_patches, sums):
    cot_own = window(grid, PITCH + 1, INNER, 2, TALL)
    cot_own = jnp.where(inner_mask(4 * COUT), cot_own, 0.0).astype(BF16)
    cot_stacked = jnp.concatenate([cot_own[:, i * COUT : (i + 1) * COUT] for i in range(4)], axis=0)
    mix_sum = lax.dot_general(
        act_patches, cot_stacked, (((0,), (0,)), ((), ())), preferred_element_type=F32
    )
    empty = jnp.zeros((LON_ALL, 8, COUT), F32)
    for w in range(4):
        slots = [empty] * 4
        for slot in range(4):
            tap = slot * 4 + w
            if tap < 9:
                slots[slot] = mix_sum[tap * COUT : (tap + 1) * COUT].reshape(LON_ALL, 8, COUT)
        for i in range(2):
            sums[w // 2, MIX, w % 2, :, i * COUT : (i + 1) * COUT] = merge_slots(
                slots[2 * i], slots[2 * i + 1]
            )


def backward_part(grid, mix_kernel, slope, outside, pre_grad):
    backward = jnp.concatenate([mix_kernel[i] for i in range(9)], axis=1)
    act_grad = lax.dot_general(
        patches(positions(grid, OUTER, 2), True),
        backward,
        (((1,), (1,)), ((), ())),
        preferred_element_type=F32,
    )
    graded = (beside(act_grad, OUTER) * slope).astype(BF16).astype(F32)
    keep_wide(pre_grad, jnp.where(outside, 0.0, graded))


def grad_window(pre_grad, dr, dc):
    return window(pre_grad, dr * PITCH + dc, INNER, 0, 4).astype(BF16)


def up_part_sums(grid, pre_grad, dc, sums):
    in_own = window(grid, PITCH + 1, INNER, 0, 2)
    in_own = jnp.where(inner_mask(CIN), in_own, 0.0).astype(BF16)
    for dr in range(2):
        up_sum = lax.dot_general(
            in_own,
            grad_window(pre_grad, dr, dc),
            (((0,), (0,)), ((), ())),
            preferred_element_type=F32,
        ).astype(BF16)
        for pr in range(2):
            sums[dr, dc, pr] = up_sum[:, pr * SPAN : (pr + 1) * SPAN]


def section_part(act_patches, mix_kernel, staged, out_wide, section):
    flat_mix = mix_kernel[...].reshape(9 * COUT, COUT)
    staged[...] = jnp.dot(act_patches, flat_mix, preferred_element_type=F32)
    for s in range(2):
        for t in range(2):
            for r in range(ROWS):
                out_wide[pl.ds((2 * r + s) * 2 * COLS + t, COLS, stride=2), :] = staged[
                    pl.ds((2 * s + t) * INNER + r * PITCH, COLS), :
                ]
    section[...] = out_wide[...].astype(BF16)


def input_part(pre_grad, up_kernel, act, input_grad):
    back_up = jnp.concatenate(
        [
            up_kernel[(2 * dr + pr) * 4 + 2 * dc + pc]
            for dr, dc in OFFSETS
            for pr in range(2)
            for pc in range(2)
        ],
        axis=1,
    )
    grad_windows = jnp.concatenate([grad_window(pre_grad, dr, dc) for dr, dc in OFFSETS], axis=1)
    spread = lax.dot_general(
        grad_windows, back_up, (((1,), (1,)), ((), ())), preferred_element_type=F32
    )
    for i in range(2):
        act[i, :INNER, :] = spread[:, i * COUT : (i + 1) * COUT]
        for r in range(ROWS):
            input_grad[r * COLS : (r + 1) * COLS, i * COUT : (i + 1) * COUT] = act[
                i, pl.ds(r * PITCH, COLS), :
            ]


def reduce_partners(lat, lon, z_count, y_count):
    core, x_hi, z = lax.rem(lat, 2), lax.rem(lat // 2, 2), lat // 4
    y, x_lo = lax.rem(lon, y_count), lon // y_count
    return core, x_hi, z, y, x_lo


def fetch(src, dst, send, recv, to):
    copy = pltpu.make_async_remote_copy(
        src_ref=src, dst_ref=dst, send_sem=send, recv_sem=recv, device_id=to, device_id_type=MESH
    )
    copy.start()


def await_bytes(ref, sem):
    pltpu.make_async_copy(ref, ref, sem).wait()


def z_plan(z_count):
    return 3, z_count // 3


def section_kernel(
    lat_count,
    lon_count,
    scale,
    codes_hbm,
    exps_hbm,
    cot_hbm,
    up_hbm,
    bias_hbm,
    mix_hbm,
    section,
    input_grad,
    up_out,
    mix_out,
    codes,
    exps,
    cot,
    up_kernel,
    bias,
    mix_kernel,
    load_sem,
    grid,
    own,
    cot_wide,
    row_out,
    col_out,
    corner_out,
    row_in,
    col_in,
    corner_in,
    halo_send,
    halo_recv,
    act,
    pre_grad,
    staged,
    out_wide,
    sums,
    core_in,
    x_out,
    xa_in,
    xb_in,
    y_out,
    y_in,
    far,
    near,
    final,
    core_sem,
    x_sem,
    y_sem,
    far_sem,
    near_sem,
    final_sem,
):
    z_count, y_count = lat_count // 4, lon_count // 2
    far_count, near_count = z_plan(z_count)
    lat, lon = lax.axis_index("lat"), lax.axis_index("lon")
    core, x_hi, z, y, x_lo = reduce_partners(lat, lon, z_count, y_count)
    x = 2 * x_hi + x_lo
    own_w = 2 * core + x_hi

    def at_x(step):
        other = lax.rem(x + step + 4, 4)
        return 4 * z + 2 * (other // 2) + core, lax.rem(other, 2) * y_count + y

    def at_y(step):
        return lat, x_lo * y_count + lax.rem(y + step, y_count)

    def at_z(step):
        return 4 * lax.rem(z + step + z_count, z_count) + 2 * x_hi + core, lon

    def at_inner(step):
        other = lax.rem(own_w + step, 4)
        return 4 * z + 2 * lax.rem(other, 2) + other // 2, lon

    partner = (lat + 1 - 2 * core, lon)
    far_steps = [near_count * i for i in range(1, far_count)]
    near_steps = [i if 2 * i <= near_count else i - near_count for i in range(1, near_count)]

    loads = [
        pltpu.make_async_copy(src, dst, load_sem.at[i])
        for i, (src, dst) in enumerate(
            (
                (exps_hbm, exps),
                (codes_hbm, codes),
                (cot_hbm, cot),
                (up_hbm, up_kernel),
                (mix_hbm, mix_kernel),
                (bias_hbm, bias),
            )
        )
    ]
    for load in loads:
        load.start()

    barrier = pltpu.get_barrier_semaphore()
    up, down, left, right = partners = halo_partners(lat, lon, lat_count, lon_count)
    greeted = [(a, b) for a in (up, down) for b in (left, lon, right)] + [(lat, left), (lat, right)]
    greeted += [partner, at_x(1), at_x(-1)]
    greeted += [at_y(step) for step in range(1, y_count)]
    for step in far_steps + near_steps:
        greeted += [at_z(step), at_z(-step)]
    greeted += [at_inner(step) for step in range(1, 4)]
    for to in greeted:
        pl.semaphore_signal(barrier, inc=1, device_id=to, device_id_type=MESH)
    for load in loads[:3]:
        load.wait()
    halo_fill(codes, exps, cot, grid, own, cot_wide, row_out, col_out, corner_out)
    pl.semaphore_wait(barrier, len(greeted))
    halo = halo_copies(
        partners, lat, lon, row_out, col_out, corner_out, row_in, col_in, corner_in, halo_send, halo_recv
    )
    for copy in halo:
        copy.start()
    for load in loads[3:]:
        load.wait()
    for copy in halo:
        copy.wait_recv()
    halo_place(lat, lat_count, grid, row_in, col_in, corner_in)

    def core_start(part):
        fetch(sums.at[1 - core, part], core_in.at[part], core_sem.at[0, part], core_sem.at[1, part], partner)

    half = CIN // 4

    def x_first(part):
        await_bytes(core_in.at[part], core_sem.at[1, part])
        merged = sums[core, part].astype(F32) + core_in[part].astype(F32)
        x_out[part] = merged.astype(BF16).reshape(x_out.shape[1:])
        across = lax.rem(x + 2, 4)
        for side, step in ((0, 1), (1, -1)):
            fetch(
                x_out.at[part, across, pl.ds(side * half, half)],
                xa_in.at[part, side],
                x_sem.at[0, part, side],
                x_sem.at[1, part, side],
                at_x(step),
            )

    def x_second(part):
        for side, step in ((0, 1), (1, -1)):
            await_bytes(xa_in.at[part, side], x_sem.at[1, part, side])
            beside_x = lax.rem(x + step + 4, 4)
            rows = pl.ds(side * half, half)
            merged = x_out[part, beside_x, rows].astype(F32) + xa_in[part, side].astype(F32)
            x_out[part, beside_x, rows] = merged.astype(BF16)
            fetch(
                x_out.at[part, beside_x],
                xb_in.at[part, side],
                x_sem.at[2, part, side],
                x_sem.at[3, part, side],
                at_x(step),
            )

    def y_start(part):
        for side in range(2):
            await_bytes(xb_in.at[part, side], x_sem.at[3, part, side])
        merged = x_out[part, x].astype(F32) + xb_in[part, 0].astype(F32) + xb_in[part, 1].astype(F32)
        y_out[part] = merged.astype(BF16).reshape(y_out.shape[1:])
        for step in range(1, y_count):
            fetch(
                y_out.at[part, lax.rem(y + step, y_count)],
                y_in.at[part, step - 1],
                y_sem.at[0, part],
                y_sem.at[1, part],
                at_y(step),
            )

    far_at, near_at = z // near_count, lax.rem(z, near_count)

    def far_start(part):
        await_bytes(y_in.at[part], y_sem.at[1, part])
        total = y_out[part, y].astype(F32)
        for step in range(y_count - 1):
            total = total + y_in[part, step].astype(F32)
        far[part, far_at] = total.astype(BF16)
        for step in far_steps:
            fetch(far.at[part, far_at], far.at[part, far_at], far_sem.at[0, part], far_sem.at[1, part], at_z(step))

    def near_start(part):
        await_bytes(far.at[part, pl.ds(0, far_count - 1)], far_sem.at[1, part])
        total = far[part, 0].astype(F32)
        for i in range(1, far_count):
            total = total + far[part, i].astype(F32)
        near[part, near_at] = total.astype(BF16)
        for step in near_steps:
            fetch(
                near.at[part, near_at], near.at[part, near_at], near_sem.at[0, part], near_sem.at[1, part], at_z(step)
            )

    def final_start(part):
        if near_count > 1:
            await_bytes(near.at[part, pl.ds(0, near_count - 1)], near_sem.at[1, part])
        total = near[part, 0].astype(F32)
        for i in range(1, near_count):
            total = total + near[part, i].astype(F32)
        final[part, own_w] = (total * scale).astype(BF16)
        for step in range(1, 4):
            fetch(
                final.at[part, own_w],
                final.at[part, own_w],
                final_sem.at[0, part],
                final_sem.at[1, part],
                at_inner(step),
            )

    def finish(part):
        await_bytes(final.at[part, pl.ds(0, 3)], final_sem.at[1, part])
        for w in range(4):
            total = final[part, w].astype(F32)
            for i in range(2):
                piece = total[:, i * COUT : (i + 1) * COUT]
                if part != MIX:
                    up_out[w, 2 * part + i] = piece
                    continue
                for slot in range(2):
                    tap = (2 * i + slot) * 4 + w
                    if tap < 9:
                        mix_out[tap] = piece[slot * 8 : slot * 8 + 8]

    slope, outside = forward_part(lat, lat_count, grid, up_kernel, bias, act)
    act_patches = patches(positions(act, INNER, 0), False)
    mix_part_sums(grid, act_patches, sums)
    core_start(MIX)
    backward_part(grid, mix_kernel, slope, outside, pre_grad)
    for dc in range(2):
        up_part_sums(grid, pre_grad, dc, sums)
        core_start(dc)
    for part in ORDER:
        x_first(part)
    x_second(ORDER[0])
    section_part(act_patches, mix_kernel, staged, out_wide, section)
    x_second(ORDER[1])
    x_second(ORDER[2])
    y_start(ORDER[0])
    input_part(pre_grad, up_kernel, act, input_grad)
    y_start(ORDER[1])
    far_start(ORDER[0])
    y_start(ORDER[2])
    far_start(ORDER[1])
    near_start(ORDER[0])
    far_start(ORDER[2])
    near_start(ORDER[1])
    final_start(ORDER[0])
    near_start(ORDER[2])
    final_start(ORDER[1])
    finish(ORDER[0])
    final_start(ORDER[2])
    finish(ORDER[1])
    for copy in halo:
        copy.wait_send()
    for part in range(PARTS):
        await_bytes(core_in.at[part], core_sem.at[0, part])
        for side in range(2):
            await_bytes(xa_in.at[part, side], x_sem.at[0, part, side])
            await_bytes(xb_in.at[part, side], x_sem.at[2, part, side])
        await_bytes(y_in.at[part], y_sem.at[0, part])
        await_bytes(far.at[part, pl.ds(0, far_count - 1)], far_sem.at[0, part])
        if near_count > 1:
            await_bytes(near.at[part, pl.ds(0, near_count - 1)], near_sem.at[0, part])
        await_bytes(final.at[part, pl.ds(0, 3)], final_sem.at[0, part])
    finish(ORDER[2])


def shards(elem_codes, block_exps, up_kernel, up_bias, mix_kernel, cotangent):
    lat_count, lon_count = lax.axis_size("lat"), lax.axis_size("lon")
    y_count, z_count = lon_count // 2, lat_count // 4
    far_count, near_count = z_plan(z_count)
    out_cells = 4 * CELLS * lat_count * lon_count
    operands = (
        elem_codes.reshape(CELLS, CIN),
        block_exps.transpose(1, 2, 0).reshape(COLS * CIN // BLOCK, ROWS),
        cotangent.reshape(4 * CELLS, COUT),
        up_kernel.reshape(16, CIN, COUT),
        up_bias.reshape(1, COUT),
        mix_kernel.reshape(9, COUT, COUT),
    )
    dma = pltpu.SemaphoreType.DMA
    section, input_grad, up_part, mix_part = pl.pallas_call(
        functools.partial(section_kernel, lat_count, lon_count, 1.0 / math.sqrt(out_cells)),
        out_shape=(
            jax.ShapeDtypeStruct((4 * CELLS, COUT), BF16),
            jax.ShapeDtypeStruct((CELLS, CIN), F32),
            jax.ShapeDtypeStruct((4, 4, LON_ALL, COUT), F32),
            jax.ShapeDtypeStruct((9, 8, COUT), F32),
        ),
        in_specs=[pl.BlockSpec(memory_space=pltpu.HBM)] * 6,
        out_specs=[pl.BlockSpec(memory_space=pltpu.VMEM)] * 4,
        scratch_shapes=[pltpu.VMEM(operand.shape, operand.dtype) for operand in operands]
        + [
            dma((6,)),
            pltpu.VMEM((TALL, FLAT, COUT), F32),
            pltpu.VMEM((TALL, CELLS, COUT), F32),
            pltpu.VMEM((4 * CELLS, COUT), F32),
            pltpu.VMEM((2, TALL // 2, 2 * COLS, COUT), BF16),
            pltpu.VMEM((2, TALL, ROWS, COUT), BF16),
            pltpu.VMEM((4, 8, COUT), F32),
            pltpu.VMEM((2, TALL // 2, 2 * COLS, COUT), BF16),
            pltpu.VMEM((2, TALL, ROWS, COUT), BF16),
            pltpu.VMEM((4, 8, COUT), F32),
            dma((8,)),
            dma((8,)),
            pltpu.VMEM((4, FLAT, COUT), F32),
            pltpu.VMEM((4, FLAT, COUT), F32),
            pltpu.VMEM((4 * INNER, COUT), F32),
            pltpu.VMEM((4 * CELLS, COUT), F32),
            pltpu.VMEM((2, PARTS, 2, CIN, SPAN), BF16),
            pltpu.VMEM((PARTS, 2, CIN, SPAN), BF16),
            pltpu.VMEM((PARTS, 4, CIN // 2, SPAN), BF16),
            pltpu.VMEM((PARTS, 2, CIN // 4, SPAN), BF16),
            pltpu.VMEM((PARTS, 2, CIN // 2, SPAN), BF16),
            pltpu.VMEM((PARTS, y_count, 16, SPAN), BF16),
            pltpu.VMEM((PARTS, y_count - 1, 16, SPAN), BF16),
            pltpu.VMEM((PARTS, far_count, 16, SPAN), BF16),
            pltpu.VMEM((PARTS, near_count, 16, SPAN), BF16),
            pltpu.VMEM((PARTS, 4, 16, SPAN), BF16),
            dma((2, PARTS)),
            dma((4, PARTS, 2)),
            dma((2, PARTS)),
            dma((2, PARTS)),
            dma((2, PARTS)),
            dma((2, PARTS)),
        ],
        compiler_params=pltpu.CompilerParams(
            collective_id=0, has_side_effects=True, vmem_limit_bytes=56 * 2**20
        ),
    )(*operands)
    return (
        section.reshape(2 * ROWS, 2 * COLS, COUT),
        input_grad.reshape(ROWS, COLS, CIN),
        up_part,
        mix_part.reshape(3, 3, 8, COUT),
    )


def solution(mesh):
    placed = (P("lat", "lon", None), P("lat", "lon", None), P(), P(), P(), P("lat", "lon", None))
    return jax.shard_map(
        shards,
        mesh=mesh,
        in_specs=placed,
        out_specs=(
            P("lat", "lon", None),
            P("lat", "lon", None),
            P(None, None, "lon", None),
            P(None, None, "lon", None),
        ),
        check_vma=False,
    )
```

```python
import functools
import math

import jax
import jax.numpy as jnp
from jax import lax
from jax.experimental import pallas as pl
from jax.experimental.pallas import tpu as pltpu
from jax.sharding import PartitionSpec as P

CIN = 256
COUT = 128
BLOCK = 32
ROWS = 16
COLS = 8
PITCH = 10
CELLS = ROWS * COLS
TALL = CIN // COUT + 4
FLAT = 192
OUTER = 176
INNER = ROWS * PITCH
PARTS = 3
SPAN = 2 * COUT
MIX = 2
ORDER = (2, 0, 1)
LON_ALL = 16
MESH = pl.DeviceIdType.MESH
F32 = jnp.float32
BF16 = jnp.bfloat16


def power_bits(value, bits):
    total = jnp.where(value & 1 != 0, 2.0, 1.0)
    for bit in range(1, bits):
        total = total * jnp.where(value & (1 << bit) != 0, float(1 << (1 << bit)), 1.0)
    return total


def decode(codes, factor):
    sign = jnp.where(codes >= 128, -(2.0**-9), 2.0**-9)
    fraction = (8 + (codes & 7)).astype(F32) * 0.125
    return sign * power_bits((codes >> 3) & 15, 4) * fraction * factor


def block_factors(exps, own):
    factor = power_bits(exps + 2, 2).astype(BF16)
    count = exps.shape[0]
    lane = lax.broadcasted_iota(jnp.int32, (count, COLS * CIN), 1)
    row = lax.broadcasted_iota(jnp.int32, (count, COLS * CIN), 0)
    spread = jnp.where(lane // BLOCK == row, 1.0, 0.0).astype(BF16)
    wide = lax.dot_general(factor, spread, (((0,), (0,)), ((), ())), preferred_element_type=F32)
    for c in range(COLS):
        for i in range(CIN // COUT):
            at = c * CIN + i * COUT
            own[i, pl.ds(c, ROWS, stride=COLS), :] = wide[:, at : at + COUT]


def halo_partners(lat, lon, lat_count, lon_count):
    up, down = lax.rem(lat + lat_count - 1, lat_count), lax.rem(lat + 1, lat_count)
    left, right = lax.rem(lon + lon_count - 1, lon_count), lax.rem(lon + 1, lon_count)
    return up, down, left, right


def halo_fill(codes, exps, cot, grid, own, cot_wide, row_out, col_out, corner_out):
    block_factors(exps[...], own)
    for i in range(CIN // COUT):
        own[i] = decode(codes[:, i * COUT : (i + 1) * COUT], own[i])
    cot_wide[...] = cot[...].astype(F32)
    for r in range(ROWS):
        for s in range(2):
            for t in range(2):
                own[2 + 2 * s + t, r * COLS : (r + 1) * COLS, :] = cot_wide[
                    pl.ds((2 * r + s) * 2 * COLS + t, COLS, stride=2), :
                ]
    for side, r in enumerate((ROWS - 1, 0)):
        for i in range(TALL // 2):
            row_out[side, i] = jnp.concatenate(
                [own[j, r * COLS : (r + 1) * COLS, :] for j in (2 * i, 2 * i + 1)], axis=0
            ).astype(BF16)
    for side, c in enumerate((COLS - 1, 0)):
        for i in range(TALL):
            col_out[side, i] = own[i, pl.ds(c, ROWS, stride=COLS), :].astype(BF16)
    for corner, (r, c) in enumerate(((ROWS - 1, COLS - 1), (ROWS - 1, 0), (0, COLS - 1), (0, 0))):
        cell = r * COLS + c
        corner_out[corner] = jnp.zeros((8, COUT), F32)
        for i in range(TALL):
            corner_out[corner, i : i + 1, :] = own[i, cell : cell + 1, :]
    for r in range(ROWS):
        at = (r + 1) * PITCH + 1
        for i in range(TALL):
            grid[i, at : at + COLS, :] = own[i, r * COLS : (r + 1) * COLS, :]
    tail = (ROWS + 2) * PITCH
    for i in range(TALL):
        grid[i, tail:FLAT, :] = jnp.zeros((FLAT - tail, COUT), F32)


def halo_copies(partners, lat, lon, row_out, col_out, corner_out, row_in, col_in, corner_in, send, recv):
    up, down, left, right = partners
    plan = [
        (row_out.at[0], row_in.at[0], down, lon),
        (row_out.at[1], row_in.at[1], up, lon),
        (col_out.at[0], col_in.at[0], lat, right),
        (col_out.at[1], col_in.at[1], lat, left),
        (corner_out.at[0], corner_in.at[0], down, right),
        (corner_out.at[1], corner_in.at[1], down, left),
        (corner_out.at[2], corner_in.at[2], up, right),
        (corner_out.at[3], corner_in.at[3], up, left),
    ]
    return [
        pltpu.make_async_remote_copy(
            src_ref=src,
            dst_ref=dst,
            send_sem=send.at[i],
            recv_sem=recv.at[i],
            device_id=(to_lat, to_lon),
            device_id_type=MESH,
        )
        for i, (src, dst, to_lat, to_lon) in enumerate(plan)
    ]


def halo_place(lat, lat_count, grid, row_in, col_in, corner_in):
    above = (lat > 0).astype(F32)
    below = (lat < lat_count - 1).astype(F32)
    for side, (r, keep) in enumerate(((0, above), (ROWS + 1, below))):
        at = r * PITCH + 1
        for i in range(TALL // 2):
            part = row_in[side, i].astype(F32) * keep
            grid[2 * i, at : at + COLS, :] = part[:COLS]
            grid[2 * i + 1, at : at + COLS, :] = part[COLS:]
    for side, c in enumerate((0, COLS + 1)):
        for i in range(TALL):
            grid[i, pl.ds(PITCH + c, ROWS, stride=PITCH), :] = col_in[side, i].astype(F32)
    places = ((0, 0, above), (0, COLS + 1, above), (ROWS + 1, 0, below), (ROWS + 1, COLS + 1, below))
    for corner, (r, c, keep) in enumerate(places):
        cell = r * PITCH + c
        for i in range(TALL):
            grid[i, cell : cell + 1, :] = corner_in[corner, i : i + 1, :] * keep


OFFSETS = ((0, 0), (0, 1), (1, 0), (1, 1))


def positions(ref, length, low):
    found = {}
    for dr, dc in OFFSETS:
        for pr in range(2):
            for pc in range(2):
                found[2 * dr + pr, 2 * dc + pc] = ref[
                    low + 2 * pr + pc, pl.ds(dr * PITCH + dc, length), :
                ].astype(BF16)
    return found


def window(ref, start, length, low, high):
    return jnp.concatenate([ref[i, pl.ds(start, length), :] for i in range(low, high)], axis=1)


def keep_wide(ref, value):
    for i in range(4):
        ref[i, :OUTER, :] = value[:, i * COUT : (i + 1) * COUT]
        ref[i, OUTER:, :] = jnp.zeros((FLAT - OUTER, COUT), F32)


def patches(found, flipped):
    stacked = []
    for s in range(2):
        for t in range(2):
            pieces = []
            for ky in range(3):
                for kx in range(3):
                    at = (s - ky + 2, t - kx + 2) if flipped else (s + ky, t + kx)
                    pieces.append(found[at])
            stacked.append(jnp.concatenate(pieces, axis=1))
    return jnp.concatenate(stacked, axis=0)


def beside(array, rows):
    return jnp.concatenate([array[i * rows : (i + 1) * rows] for i in range(4)], axis=1)


def inner_mask(lanes):
    cell = lax.broadcasted_iota(jnp.int32, (INNER, lanes), 0)
    return lax.rem(cell, PITCH) < COLS


def merge_slots(even, odd):
    return jnp.concatenate([even, odd], axis=1).reshape(CIN, COUT).astype(BF16)


def forward_part(lat, lat_count, grid, up_kernel, bias, act):
    windows = [window(grid, dr * PITCH + dc, OUTER, 0, 2).astype(BF16) for dr, dc in OFFSETS]
    forward = jnp.concatenate(
        [
            jnp.concatenate(
                [
                    up_kernel[(2 * (1 - dr) + pr) * 4 + 2 * (1 - dc) + pc]
                    for pr in range(2)
                    for pc in range(2)
                ],
                axis=1,
            )
            for dr, dc in OFFSETS
        ],
        axis=0,
    )
    raw = jnp.dot(jnp.concatenate(windows, axis=1), forward, preferred_element_type=F32)
    plain = (raw + jnp.concatenate([bias[...]] * 4, axis=1)).astype(BF16).astype(F32)
    sigmoid = jax.nn.sigmoid(plain)
    activated = (plain * sigmoid).astype(BF16).astype(F32)
    cell = lax.broadcasted_iota(jnp.int32, (OUTER, 4 * COUT), 0)
    lane = lax.broadcasted_iota(jnp.int32, (OUTER, 4 * COUT), 1)
    outside = ((cell < PITCH) & (lane < 2 * COUT) & (lat == 0)) | (
        (cell >= ROWS * PITCH) & (lane >= 2 * COUT) & (lat == lat_count - 1)
    )
    keep_wide(act, jnp.where(outside, 0.0, activated))
    return sigmoid * (1.0 + plain * (1.0 - sigmoid)), outside


def mix_part_sums(grid, act_patches, sums):
    cot_own = window(grid, PITCH + 1, INNER, 2, TALL)
    cot_own = jnp.where(inner_mask(4 * COUT), cot_own, 0.0).astype(BF16)
    cot_stacked = jnp.concatenate([cot_own[:, i * COUT : (i + 1) * COUT] for i in range(4)], axis=0)
    mix_sum = lax.dot_general(
        act_patches, cot_stacked, (((0,), (0,)), ((), ())), preferred_element_type=F32
    )
    empty = jnp.zeros((LON_ALL, 8, COUT), F32)
    for w in range(4):
        slots = [empty] * 4
        for slot in range(4):
            tap = slot * 4 + w
            if tap < 9:
                slots[slot] = mix_sum[tap * COUT : (tap + 1) * COUT].reshape(LON_ALL, 8, COUT)
        for i in range(2):
            sums[w // 2, MIX, w % 2, :, i * COUT : (i + 1) * COUT] = merge_slots(
                slots[2 * i], slots[2 * i + 1]
            )


def backward_part(grid, mix_kernel, slope, outside, pre_grad):
    backward = jnp.concatenate([mix_kernel[i] for i in range(9)], axis=1)
    act_grad = lax.dot_general(
        patches(positions(grid, OUTER, 2), True),
        backward,
        (((1,), (1,)), ((), ())),
        preferred_element_type=F32,
    )
    graded = (beside(act_grad, OUTER) * slope).astype(BF16).astype(F32)
    keep_wide(pre_grad, jnp.where(outside, 0.0, graded))


def grad_window(pre_grad, dr, dc):
    return window(pre_grad, dr * PITCH + dc, INNER, 0, 4).astype(BF16)


def up_part_sums(grid, pre_grad, dc, sums):
    in_own = window(grid, PITCH + 1, INNER, 0, 2)
    in_own = jnp.where(inner_mask(CIN), in_own, 0.0).astype(BF16)
    for dr in range(2):
        up_sum = lax.dot_general(
            in_own,
            grad_window(pre_grad, dr, dc),
            (((0,), (0,)), ((), ())),
            preferred_element_type=F32,
        ).astype(BF16)
        for pr in range(2):
            sums[dr, dc, pr] = up_sum[:, pr * SPAN : (pr + 1) * SPAN]


def section_part(act_patches, mix_kernel, staged, out_wide, section):
    flat_mix = mix_kernel[...].reshape(9 * COUT, COUT)
    staged[...] = jnp.dot(act_patches, flat_mix, preferred_element_type=F32)
    for s in range(2):
        for t in range(2):
            for r in range(ROWS):
                out_wide[pl.ds((2 * r + s) * 2 * COLS + t, COLS, stride=2), :] = staged[
                    pl.ds((2 * s + t) * INNER + r * PITCH, COLS), :
                ]
    section[...] = out_wide[...].astype(BF16)


def input_part(pre_grad, up_kernel, act, input_grad):
    back_up = jnp.concatenate(
        [
            up_kernel[(2 * dr + pr) * 4 + 2 * dc + pc]
            for dr, dc in OFFSETS
            for pr in range(2)
            for pc in range(2)
        ],
        axis=1,
    )
    grad_windows = jnp.concatenate([grad_window(pre_grad, dr, dc) for dr, dc in OFFSETS], axis=1)
    spread = lax.dot_general(
        grad_windows, back_up, (((1,), (1,)), ((), ())), preferred_element_type=F32
    )
    for i in range(2):
        act[i, :INNER, :] = spread[:, i * COUT : (i + 1) * COUT]
        for r in range(ROWS):
            input_grad[r * COLS : (r + 1) * COLS, i * COUT : (i + 1) * COUT] = act[
                i, pl.ds(r * PITCH, COLS), :
            ]


def reduce_partners(lat, lon, z_count, y_count):
    core, x_hi, z = lax.rem(lat, 2), lax.rem(lat // 2, 2), lat // 4
    y, x_lo = lax.rem(lon, y_count), lon // y_count
    return core, x_hi, z, y, x_lo


def fetch(src, dst, send, recv, to):
    copy = pltpu.make_async_remote_copy(
        src_ref=src, dst_ref=dst, send_sem=send, recv_sem=recv, device_id=to, device_id_type=MESH
    )
    copy.start()


def await_bytes(ref, sem):
    pltpu.make_async_copy(ref, ref, sem).wait()


def z_plan(z_count):
    return 3, z_count // 3


def section_kernel(
    lat_count,
    lon_count,
    scale,
    codes_hbm,
    exps_hbm,
    cot_hbm,
    up_hbm,
    bias_hbm,
    mix_hbm,
    section,
    input_grad,
    up_out,
    mix_out,
    codes,
    exps,
    cot,
    up_kernel,
    bias,
    mix_kernel,
    load_sem,
    grid,
    own,
    cot_wide,
    row_out,
    col_out,
    corner_out,
    row_in,
    col_in,
    corner_in,
    halo_send,
    halo_recv,
    act,
    pre_grad,
    staged,
    out_wide,
    sums,
    core_in,
    x_out,
    xa_in,
    xb_in,
    y_out,
    y_in,
    far,
    near,
    final,
    core_sem,
    x_sem,
    y_sem,
    far_sem,
    near_sem,
    final_sem,
):
    z_count, y_count = lat_count // 4, lon_count // 2
    far_count, near_count = z_plan(z_count)
    lat, lon = lax.axis_index("lat"), lax.axis_index("lon")
    core, x_hi, z, y, x_lo = reduce_partners(lat, lon, z_count, y_count)
    x = 2 * x_hi + x_lo

    def at_x(step):
        other = lax.rem(x + step + 4, 4)
        return 4 * z + 2 * (other // 2) + core, lax.rem(other, 2) * y_count + y

    def at_y(step):
        return lat, x_lo * y_count + lax.rem(y + step, y_count)

    def at_z(step, row):
        return 4 * lax.rem(z + step + z_count, z_count) + 2 * row + core, lon

    partner = (lat + 1 - 2 * core, lon)
    far_steps = [near_count * i for i in range(1, far_count)]
    near_steps = [i if 2 * i <= near_count else i - near_count for i in range(1, near_count)]

    loads = [
        pltpu.make_async_copy(src, dst, load_sem.at[i])
        for i, (src, dst) in enumerate(
            (
                (exps_hbm, exps),
                (codes_hbm, codes),
                (cot_hbm, cot),
                (up_hbm, up_kernel),
                (mix_hbm, mix_kernel),
                (bias_hbm, bias),
            )
        )
    ]
    for load in loads:
        load.start()

    barrier = pltpu.get_barrier_semaphore()
    up, down, left, right = partners = halo_partners(lat, lon, lat_count, lon_count)
    greeted = [(a, b) for a in (up, down) for b in (left, lon, right)] + [(lat, left), (lat, right)]
    greeted += [partner, at_x(1), at_x(-1)]
    greeted += [at_y(step) for step in range(1, y_count)]
    far_all = sorted({step % z_count for base in far_steps for step in (base, -base)})
    near_all = sorted({step % z_count for base in near_steps for step in (base, -base)})
    greeted += [at_z(step, x_hi) for step in far_all + near_all]
    greeted += [at_z(step, 1 - x_hi) for step in [0] + near_all]
    for to in greeted:
        pl.semaphore_signal(barrier, inc=1, device_id=to, device_id_type=MESH)
    for load in loads[:3]:
        load.wait()
    halo_fill(codes, exps, cot, grid, own, cot_wide, row_out, col_out, corner_out)
    pl.semaphore_wait(barrier, len(greeted))
    halo = halo_copies(
        partners, lat, lon, row_out, col_out, corner_out, row_in, col_in, corner_in, halo_send, halo_recv
    )
    for copy in halo:
        copy.start()
    for load in loads[3:]:
        load.wait()
    for copy in halo:
        copy.wait_recv()
    halo_place(lat, lat_count, grid, row_in, col_in, corner_in)

    def core_start(part):
        fetch(sums.at[1 - core, part], core_in.at[part], core_sem.at[0, part], core_sem.at[1, part], partner)

    half = CIN // 4

    def x_first(part):
        await_bytes(core_in.at[part], core_sem.at[1, part])
        merged = sums[core, part].astype(F32) + core_in[part].astype(F32)
        x_out[part] = merged.astype(BF16).reshape(x_out.shape[1:])
        across = lax.rem(x + 2, 4)
        for side, step in ((0, 1), (1, -1)):
            fetch(
                x_out.at[part, across, pl.ds(side * half, half)],
                xa_in.at[part, side],
                x_sem.at[0, part, side],
                x_sem.at[1, part, side],
                at_x(step),
            )

    def x_second(part):
        for side, step in ((0, 1), (1, -1)):
            await_bytes(xa_in.at[part, side], x_sem.at[1, part, side])
            beside_x = lax.rem(x + step + 4, 4)
            rows = pl.ds(side * half, half)
            merged = x_out[part, beside_x, rows].astype(F32) + xa_in[part, side].astype(F32)
            x_out[part, beside_x, rows] = merged.astype(BF16)
            fetch(
                x_out.at[part, beside_x],
                xb_in.at[part, side],
                x_sem.at[2, part, side],
                x_sem.at[3, part, side],
                at_x(step),
            )

    def y_start(part):
        for side in range(2):
            await_bytes(xb_in.at[part, side], x_sem.at[3, part, side])
        merged = x_out[part, x].astype(F32) + xb_in[part, 0].astype(F32) + xb_in[part, 1].astype(F32)
        y_out[part] = merged.astype(BF16).reshape(y_out.shape[1:])
        for step in range(1, y_count):
            fetch(
                y_out.at[part, lax.rem(y + step, y_count)],
                y_in.at[part, step - 1],
                y_sem.at[0, part],
                y_sem.at[1, part],
                at_y(step),
            )

    far_at, near_at = z // near_count, lax.rem(z, near_count)

    def far_start(part):
        await_bytes(y_in.at[part], y_sem.at[1, part])
        total = y_out[part, y].astype(F32)
        for step in range(y_count - 1):
            total = total + y_in[part, step].astype(F32)
        far[part, far_at] = total.astype(BF16)
        for step in far_steps:
            fetch(far.at[part, far_at], far.at[part, far_at], far_sem.at[0, part], far_sem.at[1, part], at_z(step, x_hi))

    def near_start(part):
        await_bytes(far.at[part, pl.ds(0, far_count - 1)], far_sem.at[1, part])
        total = far[part, 0].astype(F32)
        for i in range(1, far_count):
            total = total + far[part, i].astype(F32)
        slot = 2 * near_at + x_hi
        near[part, slot] = total.astype(BF16)
        for to in [at_z(step, 1 - x_hi) for step in [0] + near_steps] + [at_z(step, x_hi) for step in near_steps]:
            fetch(near.at[part, slot], near.at[part, slot], near_sem.at[0, part], near_sem.at[1, part], to)

    def final_start(part):
        await_bytes(near.at[part, pl.ds(0, 2 * near_count - 1)], near_sem.at[1, part])
        for row in range(2):
            total = near[part, row].astype(F32)
            for i in range(1, near_count):
                total = total + near[part, 2 * i + row].astype(F32)
            final[part, core, row] = total * scale
        fetch(
            final.at[part, core], final.at[part, core], final_sem.at[0, part], final_sem.at[1, part], partner
        )

    def finish(part):
        await_bytes(final.at[part, 0], final_sem.at[1, part])
        for w in range(4):
            for i in range(2):
                piece = final[part, w // 2, w % 2, :, i * COUT : (i + 1) * COUT]
                if part != MIX:
                    up_out[w, 2 * part + i] = piece
                    continue
                for slot in range(2):
                    tap = (2 * i + slot) * 4 + w
                    if tap < 9:
                        mix_out[tap] = piece[slot * 8 : slot * 8 + 8]

    slope, outside = forward_part(lat, lat_count, grid, up_kernel, bias, act)
    act_patches = patches(positions(act, INNER, 0), False)
    mix_part_sums(grid, act_patches, sums)
    core_start(MIX)
    backward_part(grid, mix_kernel, slope, outside, pre_grad)
    up_part_sums(grid, pre_grad, 0, sums)
    core_start(0)
    x_first(MIX)
    up_part_sums(grid, pre_grad, 1, sums)
    core_start(1)
    x_first(0)
    x_first(1)
    x_second(ORDER[0])
    section_part(act_patches, mix_kernel, staged, out_wide, section)
    x_second(ORDER[1])
    x_second(ORDER[2])
    y_start(ORDER[0])
    input_part(pre_grad, up_kernel, act, input_grad)
    y_start(ORDER[1])
    far_start(ORDER[0])
    y_start(ORDER[2])
    far_start(ORDER[1])
    near_start(ORDER[0])
    far_start(ORDER[2])
    near_start(ORDER[1])
    final_start(ORDER[0])
    near_start(ORDER[2])
    final_start(ORDER[1])
    finish(ORDER[0])
    final_start(ORDER[2])
    finish(ORDER[1])
    for copy in halo:
        copy.wait_send()
    for part in range(PARTS):
        await_bytes(core_in.at[part], core_sem.at[0, part])
        for side in range(2):
            await_bytes(xa_in.at[part, side], x_sem.at[0, part, side])
            await_bytes(xb_in.at[part, side], x_sem.at[2, part, side])
        await_bytes(y_in.at[part], y_sem.at[0, part])
        await_bytes(far.at[part, pl.ds(0, far_count - 1)], far_sem.at[0, part])
        await_bytes(near.at[part, pl.ds(0, 2 * near_count - 1)], near_sem.at[0, part])
        await_bytes(final.at[part, 0], final_sem.at[0, part])
    finish(ORDER[2])


def write_kernel(*refs):
    copies = [pltpu.make_async_copy(refs[i], refs[4 + i], refs[8].at[i]) for i in range(4)]
    for copy in copies:
        copy.start()
    for copy in copies:
        copy.wait()


def shards(elem_codes, block_exps, up_kernel, up_bias, mix_kernel, cotangent):
    lat_count, lon_count = lax.axis_size("lat"), lax.axis_size("lon")
    y_count, z_count = lon_count // 2, lat_count // 4
    far_count, near_count = z_plan(z_count)
    out_cells = 4 * CELLS * lat_count * lon_count
    operands = (
        elem_codes.reshape(CELLS, CIN),
        block_exps.transpose(1, 2, 0).reshape(COLS * CIN // BLOCK, ROWS),
        cotangent.reshape(4 * CELLS, COUT),
        up_kernel.reshape(16, CIN, COUT),
        up_bias.reshape(1, COUT),
        mix_kernel.reshape(9, COUT, COUT),
    )
    dma = pltpu.SemaphoreType.DMA
    results = pl.pallas_call(
        functools.partial(section_kernel, lat_count, lon_count, 1.0 / math.sqrt(out_cells)),
        out_shape=(
            jax.ShapeDtypeStruct((4 * CELLS, COUT), BF16),
            jax.ShapeDtypeStruct((CELLS, CIN), F32),
            jax.ShapeDtypeStruct((4, 4, LON_ALL, COUT), F32),
            jax.ShapeDtypeStruct((9, 8, COUT), F32),
        ),
        in_specs=[pl.BlockSpec(memory_space=pltpu.HBM)] * 6,
        out_specs=[pl.BlockSpec(memory_space=pltpu.VMEM)] * 4,
        scratch_shapes=[pltpu.VMEM(operand.shape, operand.dtype) for operand in operands]
        + [
            dma((6,)),
            pltpu.VMEM((TALL, FLAT, COUT), F32),
            pltpu.VMEM((TALL, CELLS, COUT), F32),
            pltpu.VMEM((4 * CELLS, COUT), F32),
            pltpu.VMEM((2, TALL // 2, 2 * COLS, COUT), BF16),
            pltpu.VMEM((2, TALL, ROWS, COUT), BF16),
            pltpu.VMEM((4, 8, COUT), F32),
            pltpu.VMEM((2, TALL // 2, 2 * COLS, COUT), BF16),
            pltpu.VMEM((2, TALL, ROWS, COUT), BF16),
            pltpu.VMEM((4, 8, COUT), F32),
            dma((8,)),
            dma((8,)),
            pltpu.VMEM((4, FLAT, COUT), F32),
            pltpu.VMEM((4, FLAT, COUT), F32),
            pltpu.VMEM((4 * INNER, COUT), F32),
            pltpu.VMEM((4 * CELLS, COUT), F32),
            pltpu.VMEM((2, PARTS, 2, CIN, SPAN), BF16),
            pltpu.VMEM((PARTS, 2, CIN, SPAN), BF16),
            pltpu.VMEM((PARTS, 4, CIN // 2, SPAN), BF16),
            pltpu.VMEM((PARTS, 2, CIN // 4, SPAN), BF16),
            pltpu.VMEM((PARTS, 2, CIN // 2, SPAN), BF16),
            pltpu.VMEM((PARTS, y_count, 16, SPAN), BF16),
            pltpu.VMEM((PARTS, y_count - 1, 16, SPAN), BF16),
            pltpu.VMEM((PARTS, far_count, 16, SPAN), BF16),
            pltpu.VMEM((PARTS, 2 * near_count, 16, SPAN), BF16),
            pltpu.VMEM((PARTS, 2, 2, 16, SPAN), F32),
            dma((2, PARTS)),
            dma((4, PARTS, 2)),
            dma((2, PARTS)),
            dma((2, PARTS)),
            dma((2, PARTS)),
            dma((2, PARTS)),
        ],
        compiler_params=pltpu.CompilerParams(
            collective_id=0, has_side_effects=True, vmem_limit_bytes=56 * 2**20
        ),
    )(*operands)
    section, input_grad, up_part, mix_part = pl.pallas_call(
        write_kernel,
        out_shape=tuple(jax.ShapeDtypeStruct(result.shape, result.dtype) for result in results),
        in_specs=[pl.BlockSpec(memory_space=pltpu.HBM)] * 4,
        out_specs=[pl.BlockSpec(memory_space=pltpu.HBM)] * 4,
        scratch_shapes=[dma((4,))],
        compiler_params=pltpu.CompilerParams(vmem_limit_bytes=56 * 2**20),
    )(*results)
    return (
        section.reshape(2 * ROWS, 2 * COLS, COUT),
        input_grad.reshape(ROWS, COLS, CIN),
        up_part,
        mix_part.reshape(3, 3, 8, COUT),
    )


def solution(mesh):
    placed = (P("lat", "lon", None), P("lat", "lon", None), P(), P(), P(), P("lat", "lon", None))
    return jax.shard_map(
        shards,
        mesh=mesh,
        in_specs=placed,
        out_specs=(
            P("lat", "lon", None),
            P("lat", "lon", None),
            P(None, None, "lon", None),
            P(None, None, "lon", None),
        ),
        check_vma=False,
    )
```

```python
import functools
import math

import jax
import jax.numpy as jnp
from jax import lax
from jax.experimental import pallas as pl
from jax.experimental.pallas import tpu as pltpu
from jax.sharding import PartitionSpec as P

CIN = 256
COUT = 128
BLOCK = 32
ROWS = 16
COLS = 8
PITCH = 10
CELLS = ROWS * COLS
TALL = CIN // COUT + 4
FLAT = 192
OUTER = 176
INNER = ROWS * PITCH
PARTS = 3
SPAN = 2 * COUT
MIX = 2
ORDER = (2, 0, 1)
LON_ALL = 16
MESH = pl.DeviceIdType.MESH
F32 = jnp.float32
BF16 = jnp.bfloat16


def power_bits(value, bits):
    total = jnp.where(value & 1 != 0, 2.0, 1.0)
    for bit in range(1, bits):
        total = total * jnp.where(value & (1 << bit) != 0, float(1 << (1 << bit)), 1.0)
    return total


def decode(codes, factor):
    sign = jnp.where(codes >= 128, -(2.0**-9), 2.0**-9)
    fraction = (8 + (codes & 7)).astype(F32) * 0.125
    return sign * power_bits((codes >> 3) & 15, 4) * fraction * factor


def block_factors(exps, own):
    factor = power_bits(exps + 2, 2).astype(BF16)
    count = exps.shape[0]
    lane = lax.broadcasted_iota(jnp.int32, (count, COLS * CIN), 1)
    row = lax.broadcasted_iota(jnp.int32, (count, COLS * CIN), 0)
    spread = jnp.where(lane // BLOCK == row, 1.0, 0.0).astype(BF16)
    wide = lax.dot_general(factor, spread, (((0,), (0,)), ((), ())), preferred_element_type=F32)
    for c in range(COLS):
        for i in range(CIN // COUT):
            at = c * CIN + i * COUT
            own[i, pl.ds(c, ROWS, stride=COLS), :] = wide[:, at : at + COUT]


def halo_partners(lat, lon, lat_count, lon_count):
    up, down = lax.rem(lat + lat_count - 1, lat_count), lax.rem(lat + 1, lat_count)
    left, right = lax.rem(lon + lon_count - 1, lon_count), lax.rem(lon + 1, lon_count)
    return up, down, left, right


def halo_fill(codes, exps, cot, grid, own, cot_wide, row_out, col_out, corner_out):
    block_factors(exps[...], own)
    for i in range(CIN // COUT):
        own[i] = decode(codes[:, i * COUT : (i + 1) * COUT], own[i])
    cot_wide[...] = cot[...].astype(F32)
    for r in range(ROWS):
        for s in range(2):
            for t in range(2):
                own[2 + 2 * s + t, r * COLS : (r + 1) * COLS, :] = cot_wide[
                    pl.ds((2 * r + s) * 2 * COLS + t, COLS, stride=2), :
                ]
    for side, r in enumerate((ROWS - 1, 0)):
        for i in range(TALL // 2):
            row_out[side, i] = jnp.concatenate(
                [own[j, r * COLS : (r + 1) * COLS, :] for j in (2 * i, 2 * i + 1)], axis=0
            ).astype(BF16)
    for side, c in enumerate((COLS - 1, 0)):
        for i in range(TALL):
            col_out[side, i] = own[i, pl.ds(c, ROWS, stride=COLS), :].astype(BF16)
    for corner, (r, c) in enumerate(((ROWS - 1, COLS - 1), (ROWS - 1, 0), (0, COLS - 1), (0, 0))):
        cell = r * COLS + c
        corner_out[corner] = jnp.zeros((8, COUT), F32)
        for i in range(TALL):
            corner_out[corner, i : i + 1, :] = own[i, cell : cell + 1, :]
    for r in range(ROWS):
        at = (r + 1) * PITCH + 1
        for i in range(TALL):
            grid[i, at : at + COLS, :] = own[i, r * COLS : (r + 1) * COLS, :]
    tail = (ROWS + 2) * PITCH
    for i in range(TALL):
        grid[i, tail:FLAT, :] = jnp.zeros((FLAT - tail, COUT), F32)


def halo_copies(partners, lat, lon, row_out, col_out, corner_out, row_in, col_in, corner_in, send, recv):
    up, down, left, right = partners
    plan = [
        (row_out.at[0], row_in.at[0], down, lon),
        (row_out.at[1], row_in.at[1], up, lon),
        (col_out.at[0], col_in.at[0], lat, right),
        (col_out.at[1], col_in.at[1], lat, left),
        (corner_out.at[0], corner_in.at[0], down, right),
        (corner_out.at[1], corner_in.at[1], down, left),
        (corner_out.at[2], corner_in.at[2], up, right),
        (corner_out.at[3], corner_in.at[3], up, left),
    ]
    return [
        pltpu.make_async_remote_copy(
            src_ref=src,
            dst_ref=dst,
            send_sem=send.at[i],
            recv_sem=recv.at[i],
            device_id=(to_lat, to_lon),
            device_id_type=MESH,
        )
        for i, (src, dst, to_lat, to_lon) in enumerate(plan)
    ]


def halo_place(lat, lat_count, grid, row_in, col_in, corner_in):
    above = (lat > 0).astype(F32)
    below = (lat < lat_count - 1).astype(F32)
    for side, (r, keep) in enumerate(((0, above), (ROWS + 1, below))):
        at = r * PITCH + 1
        for i in range(TALL // 2):
            part = row_in[side, i].astype(F32) * keep
            grid[2 * i, at : at + COLS, :] = part[:COLS]
            grid[2 * i + 1, at : at + COLS, :] = part[COLS:]
    for side, c in enumerate((0, COLS + 1)):
        for i in range(TALL):
            grid[i, pl.ds(PITCH + c, ROWS, stride=PITCH), :] = col_in[side, i].astype(F32)
    places = ((0, 0, above), (0, COLS + 1, above), (ROWS + 1, 0, below), (ROWS + 1, COLS + 1, below))
    for corner, (r, c, keep) in enumerate(places):
        cell = r * PITCH + c
        for i in range(TALL):
            grid[i, cell : cell + 1, :] = corner_in[corner, i : i + 1, :] * keep


OFFSETS = ((0, 0), (0, 1), (1, 0), (1, 1))


def positions(ref, length, low):
    found = {}
    for dr, dc in OFFSETS:
        for pr in range(2):
            for pc in range(2):
                found[2 * dr + pr, 2 * dc + pc] = ref[
                    low + 2 * pr + pc, pl.ds(dr * PITCH + dc, length), :
                ].astype(BF16)
    return found


def window(ref, start, length, low, high):
    return jnp.concatenate([ref[i, pl.ds(start, length), :] for i in range(low, high)], axis=1)


def keep_wide(ref, value):
    for i in range(4):
        ref[i, :OUTER, :] = value[:, i * COUT : (i + 1) * COUT]
        ref[i, OUTER:, :] = jnp.zeros((FLAT - OUTER, COUT), F32)


def patches(found, flipped):
    stacked = []
    for s in range(2):
        for t in range(2):
            pieces = []
            for ky in range(3):
                for kx in range(3):
                    at = (s - ky + 2, t - kx + 2) if flipped else (s + ky, t + kx)
                    pieces.append(found[at])
            stacked.append(jnp.concatenate(pieces, axis=1))
    return jnp.concatenate(stacked, axis=0)


def beside(array, rows):
    return jnp.concatenate([array[i * rows : (i + 1) * rows] for i in range(4)], axis=1)


def inner_mask(lanes):
    cell = lax.broadcasted_iota(jnp.int32, (INNER, lanes), 0)
    return lax.rem(cell, PITCH) < COLS


def merge_slots(even, odd):
    return jnp.concatenate([even, odd], axis=1).reshape(CIN, COUT).astype(BF16)


def forward_part(lat, lat_count, grid, up_kernel, bias, act):
    windows = [window(grid, dr * PITCH + dc, OUTER, 0, 2).astype(BF16) for dr, dc in OFFSETS]
    forward = jnp.concatenate(
        [
            jnp.concatenate(
                [
                    up_kernel[(2 * (1 - dr) + pr) * 4 + 2 * (1 - dc) + pc]
                    for pr in range(2)
                    for pc in range(2)
                ],
                axis=1,
            )
            for dr, dc in OFFSETS
        ],
        axis=0,
    )
    raw = jnp.dot(jnp.concatenate(windows, axis=1), forward, preferred_element_type=F32)
    plain = (raw + jnp.concatenate([bias[...]] * 4, axis=1)).astype(BF16).astype(F32)
    sigmoid = jax.nn.sigmoid(plain)
    activated = (plain * sigmoid).astype(BF16).astype(F32)
    cell = lax.broadcasted_iota(jnp.int32, (OUTER, 4 * COUT), 0)
    lane = lax.broadcasted_iota(jnp.int32, (OUTER, 4 * COUT), 1)
    outside = ((cell < PITCH) & (lane < 2 * COUT) & (lat == 0)) | (
        (cell >= ROWS * PITCH) & (lane >= 2 * COUT) & (lat == lat_count - 1)
    )
    keep_wide(act, jnp.where(outside, 0.0, activated))
    return sigmoid * (1.0 + plain * (1.0 - sigmoid)), outside


def mix_part_sums(grid, act_patches, sums):
    cot_own = window(grid, PITCH + 1, INNER, 2, TALL)
    cot_own = jnp.where(inner_mask(4 * COUT), cot_own, 0.0).astype(BF16)
    cot_stacked = jnp.concatenate([cot_own[:, i * COUT : (i + 1) * COUT] for i in range(4)], axis=0)
    mix_sum = lax.dot_general(
        act_patches, cot_stacked, (((0,), (0,)), ((), ())), preferred_element_type=F32
    )
    empty = jnp.zeros((LON_ALL, 8, COUT), F32)
    for w in range(4):
        slots = [empty] * 4
        for slot in range(4):
            tap = slot * 4 + w
            if tap < 9:
                slots[slot] = mix_sum[tap * COUT : (tap + 1) * COUT].reshape(LON_ALL, 8, COUT)
        for i in range(2):
            sums[w // 2, MIX, w % 2, :, i * COUT : (i + 1) * COUT] = merge_slots(
                slots[2 * i], slots[2 * i + 1]
            )


def backward_part(grid, mix_kernel, slope, outside, pre_grad):
    backward = jnp.concatenate([mix_kernel[i] for i in range(9)], axis=1)
    act_grad = lax.dot_general(
        patches(positions(grid, OUTER, 2), True),
        backward,
        (((1,), (1,)), ((), ())),
        preferred_element_type=F32,
    )
    graded = (beside(act_grad, OUTER) * slope).astype(BF16).astype(F32)
    keep_wide(pre_grad, jnp.where(outside, 0.0, graded))


def grad_window(pre_grad, dr, dc):
    return window(pre_grad, dr * PITCH + dc, INNER, 0, 4).astype(BF16)


def up_part_sums(grid, pre_grad, dc, sums):
    in_own = window(grid, PITCH + 1, INNER, 0, 2)
    in_own = jnp.where(inner_mask(CIN), in_own, 0.0).astype(BF16)
    for dr in range(2):
        up_sum = lax.dot_general(
            in_own,
            grad_window(pre_grad, dr, dc),
            (((0,), (0,)), ((), ())),
            preferred_element_type=F32,
        ).astype(BF16)
        for pr in range(2):
            sums[dr, dc, pr] = up_sum[:, pr * SPAN : (pr + 1) * SPAN]


def section_part(act_patches, mix_kernel, staged, out_wide, section):
    flat_mix = mix_kernel[...].reshape(9 * COUT, COUT)
    staged[...] = jnp.dot(act_patches, flat_mix, preferred_element_type=F32)
    for s in range(2):
        for t in range(2):
            for r in range(ROWS):
                out_wide[pl.ds((2 * r + s) * 2 * COLS + t, COLS, stride=2), :] = staged[
                    pl.ds((2 * s + t) * INNER + r * PITCH, COLS), :
                ]
    section[...] = out_wide[...].astype(BF16)


def input_part(pre_grad, up_kernel, act, input_grad):
    back_up = jnp.concatenate(
        [
            up_kernel[(2 * dr + pr) * 4 + 2 * dc + pc]
            for dr, dc in OFFSETS
            for pr in range(2)
            for pc in range(2)
        ],
        axis=1,
    )
    grad_windows = jnp.concatenate([grad_window(pre_grad, dr, dc) for dr, dc in OFFSETS], axis=1)
    spread = lax.dot_general(
        grad_windows, back_up, (((1,), (1,)), ((), ())), preferred_element_type=F32
    )
    for i in range(2):
        act[i, :INNER, :] = spread[:, i * COUT : (i + 1) * COUT]
        for r in range(ROWS):
            input_grad[r * COLS : (r + 1) * COLS, i * COUT : (i + 1) * COUT] = act[
                i, pl.ds(r * PITCH, COLS), :
            ]


def reduce_partners(lat, lon, z_count, y_count):
    core, x_hi, z = lax.rem(lat, 2), lax.rem(lat // 2, 2), lat // 4
    y, x_lo = lax.rem(lon, y_count), lon // y_count
    return core, x_hi, z, y, x_lo


def fetch(src, dst, send, recv, to):
    copy = pltpu.make_async_remote_copy(
        src_ref=src, dst_ref=dst, send_sem=send, recv_sem=recv, device_id=to, device_id_type=MESH
    )
    copy.start()


def await_bytes(ref, sem):
    pltpu.make_async_copy(ref, ref, sem).wait()


def z_plan(z_count):
    return 3, z_count // 3


def section_kernel(
    lat_count,
    lon_count,
    scale,
    codes_hbm,
    exps_hbm,
    cot_hbm,
    up_hbm,
    bias_hbm,
    mix_hbm,
    section,
    input_grad,
    up_out,
    mix_out,
    codes,
    exps,
    cot,
    up_kernel,
    bias,
    mix_kernel,
    load_sem,
    grid,
    own,
    cot_wide,
    row_out,
    col_out,
    corner_out,
    row_in,
    col_in,
    corner_in,
    halo_send,
    halo_recv,
    act,
    pre_grad,
    staged,
    out_wide,
    sums,
    core_in,
    x_out,
    xa_in,
    xb_in,
    y_out,
    y_in,
    far,
    near,
    final,
    core_sem,
    x_sem,
    y_sem,
    far_sem,
    near_sem,
    final_sem,
):
    z_count, y_count = lat_count // 4, lon_count // 2
    far_count, near_count = z_plan(z_count)
    lat, lon = lax.axis_index("lat"), lax.axis_index("lon")
    core, x_hi, z, y, x_lo = reduce_partners(lat, lon, z_count, y_count)
    x = 2 * x_hi + x_lo

    def at_x(step):
        other = lax.rem(x + step + 4, 4)
        return 4 * z + 2 * (other // 2) + core, lax.rem(other, 2) * y_count + y

    def at_y(step):
        return lat, x_lo * y_count + lax.rem(y + step, y_count)

    def at_z(step, row):
        return 4 * lax.rem(z + step + z_count, z_count) + 2 * row + core, lon

    partner = (lat + 1 - 2 * core, lon)
    far_steps = [near_count * i for i in range(1, far_count)]
    near_steps = [i if 2 * i <= near_count else i - near_count for i in range(1, near_count)]

    loads = [
        pltpu.make_async_copy(src, dst, load_sem.at[i])
        for i, (src, dst) in enumerate(
            (
                (exps_hbm, exps),
                (codes_hbm, codes),
                (cot_hbm, cot),
                (up_hbm, up_kernel),
                (mix_hbm, mix_kernel),
                (bias_hbm, bias),
            )
        )
    ]
    for load in loads:
        load.start()

    barrier = pltpu.get_barrier_semaphore()
    up, down, left, right = partners = halo_partners(lat, lon, lat_count, lon_count)
    greeted = [(a, b) for a in (up, down) for b in (left, lon, right)] + [(lat, left), (lat, right)]
    greeted += [partner, at_x(1), at_x(-1)]
    greeted += [at_y(step) for step in range(1, y_count)]
    far_all = sorted({step % z_count for base in far_steps for step in (base, -base)})
    near_all = sorted({step % z_count for base in near_steps for step in (base, -base)})
    greeted += [at_z(step, x_hi) for step in far_all + near_all]
    greeted += [at_z(step, 1 - x_hi) for step in [0] + near_all]
    for to in greeted:
        pl.semaphore_signal(barrier, inc=1, device_id=to, device_id_type=MESH)
    for load in loads[:3]:
        load.wait()
    halo_fill(codes, exps, cot, grid, own, cot_wide, row_out, col_out, corner_out)
    pl.semaphore_wait(barrier, len(greeted))
    halo = halo_copies(
        partners, lat, lon, row_out, col_out, corner_out, row_in, col_in, corner_in, halo_send, halo_recv
    )
    for copy in halo:
        copy.start()
    for load in loads[3:]:
        load.wait()
    for copy in halo:
        copy.wait_recv()
    halo_place(lat, lat_count, grid, row_in, col_in, corner_in)

    def core_start(part):
        fetch(sums.at[1 - core, part], core_in.at[part], core_sem.at[0, part], core_sem.at[1, part], partner)

    half = CIN // 4

    def x_first(part):
        await_bytes(core_in.at[part], core_sem.at[1, part])
        merged = sums[core, part].astype(F32) + core_in[part].astype(F32)
        x_out[part] = merged.astype(BF16).reshape(x_out.shape[1:])
        across = lax.rem(x + 2, 4)
        for side, step in ((0, 1), (1, -1)):
            fetch(
                x_out.at[part, across, pl.ds(side * half, half)],
                xa_in.at[part, side],
                x_sem.at[0, part, side],
                x_sem.at[1, part, side],
                at_x(step),
            )

    def x_second(part):
        for side, step in ((0, 1), (1, -1)):
            await_bytes(xa_in.at[part, side], x_sem.at[1, part, side])
            beside_x = lax.rem(x + step + 4, 4)
            rows = pl.ds(side * half, half)
            merged = x_out[part, beside_x, rows].astype(F32) + xa_in[part, side].astype(F32)
            x_out[part, beside_x, rows] = merged.astype(BF16)
            fetch(
                x_out.at[part, beside_x],
                xb_in.at[part, side],
                x_sem.at[2, part, side],
                x_sem.at[3, part, side],
                at_x(step),
            )

    def y_start(part):
        for side in range(2):
            await_bytes(xb_in.at[part, side], x_sem.at[3, part, side])
        merged = x_out[part, x].astype(F32) + xb_in[part, 0].astype(F32) + xb_in[part, 1].astype(F32)
        y_out[part] = merged.astype(BF16).reshape(y_out.shape[1:])
        for step in range(1, y_count):
            fetch(
                y_out.at[part, lax.rem(y + step, y_count)],
                y_in.at[part, step - 1],
                y_sem.at[0, part],
                y_sem.at[1, part],
                at_y(step),
            )

    far_at, near_at = z // near_count, lax.rem(z, near_count)

    def far_start(part):
        await_bytes(y_in.at[part], y_sem.at[1, part])
        total = y_out[part, y].astype(F32)
        for step in range(y_count - 1):
            total = total + y_in[part, step].astype(F32)
        far[part, far_at] = total.astype(BF16)
        for step in far_steps:
            fetch(far.at[part, far_at], far.at[part, far_at], far_sem.at[0, part], far_sem.at[1, part], at_z(step, x_hi))

    def near_start(part):
        await_bytes(far.at[part, pl.ds(0, far_count - 1)], far_sem.at[1, part])
        total = far[part, 0].astype(F32)
        for i in range(1, far_count):
            total = total + far[part, i].astype(F32)
        slot = 2 * near_at + x_hi
        near[part, slot] = total.astype(BF16)
        for to in [at_z(step, 1 - x_hi) for step in [0] + near_steps] + [at_z(step, x_hi) for step in near_steps]:
            fetch(near.at[part, slot], near.at[part, slot], near_sem.at[0, part], near_sem.at[1, part], to)

    def final_start(part):
        await_bytes(near.at[part, pl.ds(0, 2 * near_count - 1)], near_sem.at[1, part])
        for row in range(2):
            total = near[part, row].astype(F32)
            for i in range(1, near_count):
                total = total + near[part, 2 * i + row].astype(F32)
            final[part, core, row] = total * scale
        fetch(
            final.at[part, core], final.at[part, core], final_sem.at[0, part], final_sem.at[1, part], partner
        )

    def finish(part):
        await_bytes(final.at[part, 0], final_sem.at[1, part])
        for w in range(4):
            for i in range(2):
                piece = final[part, w // 2, w % 2, :, i * COUT : (i + 1) * COUT]
                if part != MIX:
                    up_out[w, 2 * part + i] = piece
                    continue
                for slot in range(2):
                    tap = (2 * i + slot) * 4 + w
                    if tap < 9:
                        mix_out[tap] = piece[slot * 8 : slot * 8 + 8]

    slope, outside = forward_part(lat, lat_count, grid, up_kernel, bias, act)
    act_patches = patches(positions(act, INNER, 0), False)
    mix_part_sums(grid, act_patches, sums)
    core_start(MIX)
    backward_part(grid, mix_kernel, slope, outside, pre_grad)
    up_part_sums(grid, pre_grad, 0, sums)
    core_start(0)
    x_first(MIX)
    up_part_sums(grid, pre_grad, 1, sums)
    core_start(1)
    x_first(0)
    x_first(1)
    section_part(act_patches, mix_kernel, staged, out_wide, section)
    for part in ORDER:
        x_second(part)
    input_part(pre_grad, up_kernel, act, input_grad)
    for stage in (y_start, far_start, near_start, final_start):
        for part in ORDER:
            stage(part)
    for copy in halo:
        copy.wait_send()
    for part in range(PARTS):
        await_bytes(core_in.at[part], core_sem.at[0, part])
        for side in range(2):
            await_bytes(xa_in.at[part, side], x_sem.at[0, part, side])
            await_bytes(xb_in.at[part, side], x_sem.at[2, part, side])
        await_bytes(y_in.at[part], y_sem.at[0, part])
        await_bytes(far.at[part, pl.ds(0, far_count - 1)], far_sem.at[0, part])
        await_bytes(near.at[part, pl.ds(0, 2 * near_count - 1)], near_sem.at[0, part])
        await_bytes(final.at[part, 0], final_sem.at[0, part])
    for part in ORDER:
        finish(part)


def write_kernel(*refs):
    for i in range(4):
        refs[4 + i][...] = refs[i][...]


def shards(elem_codes, block_exps, up_kernel, up_bias, mix_kernel, cotangent):
    lat_count, lon_count = lax.axis_size("lat"), lax.axis_size("lon")
    y_count, z_count = lon_count // 2, lat_count // 4
    far_count, near_count = z_plan(z_count)
    out_cells = 4 * CELLS * lat_count * lon_count
    operands = (
        elem_codes.reshape(CELLS, CIN),
        block_exps.transpose(1, 2, 0).reshape(COLS * CIN // BLOCK, ROWS),
        cotangent.reshape(4 * CELLS, COUT),
        up_kernel.reshape(16, CIN, COUT),
        up_bias.reshape(1, COUT),
        mix_kernel.reshape(9, COUT, COUT),
    )
    dma = pltpu.SemaphoreType.DMA
    results = pl.pallas_call(
        functools.partial(section_kernel, lat_count, lon_count, 1.0 / math.sqrt(out_cells)),
        out_shape=(
            jax.ShapeDtypeStruct((4 * CELLS, COUT), BF16),
            jax.ShapeDtypeStruct((CELLS, CIN), F32),
            jax.ShapeDtypeStruct((4, 4, LON_ALL, COUT), F32),
            jax.ShapeDtypeStruct((9, 8, COUT), F32),
        ),
        in_specs=[pl.BlockSpec(memory_space=pltpu.HBM)] * 6,
        out_specs=[pl.BlockSpec(memory_space=pltpu.VMEM)] * 4,
        scratch_shapes=[pltpu.VMEM(operand.shape, operand.dtype) for operand in operands]
        + [
            dma((6,)),
            pltpu.VMEM((TALL, FLAT, COUT), F32),
            pltpu.VMEM((TALL, CELLS, COUT), F32),
            pltpu.VMEM((4 * CELLS, COUT), F32),
            pltpu.VMEM((2, TALL // 2, 2 * COLS, COUT), BF16),
            pltpu.VMEM((2, TALL, ROWS, COUT), BF16),
            pltpu.VMEM((4, 8, COUT), F32),
            pltpu.VMEM((2, TALL // 2, 2 * COLS, COUT), BF16),
            pltpu.VMEM((2, TALL, ROWS, COUT), BF16),
            pltpu.VMEM((4, 8, COUT), F32),
            dma((8,)),
            dma((8,)),
            pltpu.VMEM((4, FLAT, COUT), F32),
            pltpu.VMEM((4, FLAT, COUT), F32),
            pltpu.VMEM((4 * INNER, COUT), F32),
            pltpu.VMEM((4 * CELLS, COUT), F32),
            pltpu.VMEM((2, PARTS, 2, CIN, SPAN), BF16),
            pltpu.VMEM((PARTS, 2, CIN, SPAN), BF16),
            pltpu.VMEM((PARTS, 4, CIN // 2, SPAN), BF16),
            pltpu.VMEM((PARTS, 2, CIN // 4, SPAN), BF16),
            pltpu.VMEM((PARTS, 2, CIN // 2, SPAN), BF16),
            pltpu.VMEM((PARTS, y_count, 16, SPAN), BF16),
            pltpu.VMEM((PARTS, y_count - 1, 16, SPAN), BF16),
            pltpu.VMEM((PARTS, far_count, 16, SPAN), BF16),
            pltpu.VMEM((PARTS, 2 * near_count, 16, SPAN), BF16),
            pltpu.VMEM((PARTS, 2, 2, 16, SPAN), F32),
            dma((2, PARTS)),
            dma((4, PARTS, 2)),
            dma((2, PARTS)),
            dma((2, PARTS)),
            dma((2, PARTS)),
            dma((2, PARTS)),
        ],
        compiler_params=pltpu.CompilerParams(
            collective_id=0, has_side_effects=True, vmem_limit_bytes=56 * 2**20
        ),
    )(*operands)
    section, input_grad, up_part, mix_part = pl.pallas_call(
        write_kernel,
        out_shape=tuple(jax.ShapeDtypeStruct(result.shape, result.dtype) for result in results),
        in_specs=[pl.BlockSpec(memory_space=pltpu.VMEM)] * 4,
        out_specs=[pl.BlockSpec(memory_space=pltpu.VMEM)] * 4,
        compiler_params=pltpu.CompilerParams(vmem_limit_bytes=56 * 2**20),
    )(*results)
    return (
        section.reshape(2 * ROWS, 2 * COLS, COUT),
        input_grad.reshape(ROWS, COLS, CIN),
        up_part,
        mix_part.reshape(3, 3, 8, COUT),
    )


def solution(mesh):
    placed = (P("lat", "lon", None), P("lat", "lon", None), P(), P(), P(), P("lat", "lon", None))
    return jax.shard_map(
        shards,
        mesh=mesh,
        in_specs=placed,
        out_specs=(
            P("lat", "lon", None),
            P("lat", "lon", None),
            P(None, None, "lon", None),
            P(None, None, "lon", None),
        ),
        check_vma=False,
    )
```

```python
import functools
import math

import jax
import jax.numpy as jnp
from jax import lax
from jax.experimental import pallas as pl
from jax.experimental.pallas import tpu as pltpu
from jax.sharding import PartitionSpec as P

CIN = 256
COUT = 128
BLOCK = 32
ROWS = 16
COLS = 8
PITCH = 10
CELLS = ROWS * COLS
TALL = CIN // COUT + 4
FLAT = 192
OUTER = 176
INNER = ROWS * PITCH
PARTS = 3
SPAN = 2 * COUT
MIX = 2
ORDER = (2, 0, 1)
UP = (0, 1)
LON_ALL = 16
MESH = pl.DeviceIdType.MESH
F32 = jnp.float32
BF16 = jnp.bfloat16


def power_bits(value, bits):
    total = jnp.where(value & 1 != 0, 2.0, 1.0)
    for bit in range(1, bits):
        total = total * jnp.where(value & (1 << bit) != 0, float(1 << (1 << bit)), 1.0)
    return total


def decode(codes, factor):
    sign = jnp.where(codes >= 128, -(2.0**-9), 2.0**-9)
    fraction = (8 + (codes & 7)).astype(F32) * 0.125
    return sign * power_bits((codes >> 3) & 15, 4) * fraction * factor


def block_factors(exps, own):
    factor = power_bits(exps + 2, 2).astype(BF16)
    count = exps.shape[0]
    lane = lax.broadcasted_iota(jnp.int32, (count, COLS * CIN), 1)
    row = lax.broadcasted_iota(jnp.int32, (count, COLS * CIN), 0)
    spread = jnp.where(lane // BLOCK == row, 1.0, 0.0).astype(BF16)
    wide = lax.dot_general(factor, spread, (((0,), (0,)), ((), ())), preferred_element_type=F32)
    for c in range(COLS):
        for i in range(CIN // COUT):
            at = c * CIN + i * COUT
            own[i, pl.ds(c, ROWS, stride=COLS), :] = wide[:, at : at + COUT]


def halo_partners(lat, lon, lat_count, lon_count):
    up, down = lax.rem(lat + lat_count - 1, lat_count), lax.rem(lat + 1, lat_count)
    left, right = lax.rem(lon + lon_count - 1, lon_count), lax.rem(lon + 1, lon_count)
    return up, down, left, right


def halo_fill(codes, exps, cot, grid, own, cot_wide, row_out, col_out, corner_out):
    block_factors(exps[...], own)
    for i in range(CIN // COUT):
        own[i] = decode(codes[:, i * COUT : (i + 1) * COUT], own[i])
    cot_wide[...] = cot[...].astype(F32)
    for r in range(ROWS):
        for s in range(2):
            for t in range(2):
                own[2 + 2 * s + t, r * COLS : (r + 1) * COLS, :] = cot_wide[
                    pl.ds((2 * r + s) * 2 * COLS + t, COLS, stride=2), :
                ]
    for side, r in enumerate((ROWS - 1, 0)):
        for i in range(TALL // 2):
            row_out[side, i] = jnp.concatenate(
                [own[j, r * COLS : (r + 1) * COLS, :] for j in (2 * i, 2 * i + 1)], axis=0
            ).astype(BF16)
    for side, c in enumerate((COLS - 1, 0)):
        for i in range(TALL):
            col_out[side, i] = own[i, pl.ds(c, ROWS, stride=COLS), :].astype(BF16)
    for corner, (r, c) in enumerate(((ROWS - 1, COLS - 1), (ROWS - 1, 0), (0, COLS - 1), (0, 0))):
        cell = r * COLS + c
        corner_out[corner] = jnp.zeros((8, COUT), F32)
        for i in range(TALL):
            corner_out[corner, i : i + 1, :] = own[i, cell : cell + 1, :]
    for r in range(ROWS):
        at = (r + 1) * PITCH + 1
        for i in range(TALL):
            grid[i, at : at + COLS, :] = own[i, r * COLS : (r + 1) * COLS, :]
    tail = (ROWS + 2) * PITCH
    for i in range(TALL):
        grid[i, tail:FLAT, :] = jnp.zeros((FLAT - tail, COUT), F32)


def halo_copies(partners, lat, lon, row_out, col_out, corner_out, row_in, col_in, corner_in, send, recv):
    up, down, left, right = partners
    plan = [
        (row_out.at[0], row_in.at[0], down, lon),
        (row_out.at[1], row_in.at[1], up, lon),
        (col_out.at[0], col_in.at[0], lat, right),
        (col_out.at[1], col_in.at[1], lat, left),
        (corner_out.at[0], corner_in.at[0], down, right),
        (corner_out.at[1], corner_in.at[1], down, left),
        (corner_out.at[2], corner_in.at[2], up, right),
        (corner_out.at[3], corner_in.at[3], up, left),
    ]
    return [
        pltpu.make_async_remote_copy(
            src_ref=src,
            dst_ref=dst,
            send_sem=send.at[i],
            recv_sem=recv.at[i],
            device_id=(to_lat, to_lon),
            device_id_type=MESH,
        )
        for i, (src, dst, to_lat, to_lon) in enumerate(plan)
    ]


def halo_place(lat, lat_count, grid, row_in, col_in, corner_in):
    above = (lat > 0).astype(F32)
    below = (lat < lat_count - 1).astype(F32)
    for side, (r, keep) in enumerate(((0, above), (ROWS + 1, below))):
        at = r * PITCH + 1
        for i in range(TALL // 2):
            part = row_in[side, i].astype(F32) * keep
            grid[2 * i, at : at + COLS, :] = part[:COLS]
            grid[2 * i + 1, at : at + COLS, :] = part[COLS:]
    for side, c in enumerate((0, COLS + 1)):
        for i in range(TALL):
            grid[i, pl.ds(PITCH + c, ROWS, stride=PITCH), :] = col_in[side, i].astype(F32)
    places = ((0, 0, above), (0, COLS + 1, above), (ROWS + 1, 0, below), (ROWS + 1, COLS + 1, below))
    for corner, (r, c, keep) in enumerate(places):
        cell = r * PITCH + c
        for i in range(TALL):
            grid[i, cell : cell + 1, :] = corner_in[corner, i : i + 1, :] * keep


OFFSETS = ((0, 0), (0, 1), (1, 0), (1, 1))


def positions(ref, length, low):
    found = {}
    for dr, dc in OFFSETS:
        for pr in range(2):
            for pc in range(2):
                found[2 * dr + pr, 2 * dc + pc] = ref[
                    low + 2 * pr + pc, pl.ds(dr * PITCH + dc, length), :
                ].astype(BF16)
    return found


def window(ref, start, length, low, high):
    return jnp.concatenate([ref[i, pl.ds(start, length), :] for i in range(low, high)], axis=1)


def keep_wide(ref, value):
    for i in range(4):
        ref[i, :OUTER, :] = value[:, i * COUT : (i + 1) * COUT]
        ref[i, OUTER:, :] = jnp.zeros((FLAT - OUTER, COUT), F32)


def patches(found, flipped):
    stacked = []
    for s in range(2):
        for t in range(2):
            pieces = []
            for ky in range(3):
                for kx in range(3):
                    at = (s - ky + 2, t - kx + 2) if flipped else (s + ky, t + kx)
                    pieces.append(found[at])
            stacked.append(jnp.concatenate(pieces, axis=1))
    return jnp.concatenate(stacked, axis=0)


def beside(array, rows):
    return jnp.concatenate([array[i * rows : (i + 1) * rows] for i in range(4)], axis=1)


def inner_mask(lanes):
    cell = lax.broadcasted_iota(jnp.int32, (INNER, lanes), 0)
    return lax.rem(cell, PITCH) < COLS


def merge_slots(even, odd):
    return jnp.concatenate([even, odd], axis=1).reshape(CIN, COUT).astype(BF16)


def forward_part(lat, lat_count, grid, up_kernel, bias, act):
    windows = [window(grid, dr * PITCH + dc, OUTER, 0, 2).astype(BF16) for dr, dc in OFFSETS]
    forward = jnp.concatenate(
        [
            jnp.concatenate(
                [
                    up_kernel[(2 * (1 - dr) + pr) * 4 + 2 * (1 - dc) + pc]
                    for pr in range(2)
                    for pc in range(2)
                ],
                axis=1,
            )
            for dr, dc in OFFSETS
        ],
        axis=0,
    )
    raw = jnp.dot(jnp.concatenate(windows, axis=1), forward, preferred_element_type=F32)
    plain = (raw + jnp.concatenate([bias[...]] * 4, axis=1)).astype(BF16).astype(F32)
    sigmoid = jax.nn.sigmoid(plain)
    activated = (plain * sigmoid).astype(BF16).astype(F32)
    cell = lax.broadcasted_iota(jnp.int32, (OUTER, 4 * COUT), 0)
    lane = lax.broadcasted_iota(jnp.int32, (OUTER, 4 * COUT), 1)
    outside = ((cell < PITCH) & (lane < 2 * COUT) & (lat == 0)) | (
        (cell >= ROWS * PITCH) & (lane >= 2 * COUT) & (lat == lat_count - 1)
    )
    keep_wide(act, jnp.where(outside, 0.0, activated))
    return sigmoid * (1.0 + plain * (1.0 - sigmoid)), outside


def mix_part_sums(grid, act_patches, sums):
    cot_own = window(grid, PITCH + 1, INNER, 2, TALL)
    cot_own = jnp.where(inner_mask(4 * COUT), cot_own, 0.0).astype(BF16)
    cot_stacked = jnp.concatenate([cot_own[:, i * COUT : (i + 1) * COUT] for i in range(4)], axis=0)
    mix_sum = lax.dot_general(
        act_patches, cot_stacked, (((0,), (0,)), ((), ())), preferred_element_type=F32
    )
    empty = jnp.zeros((LON_ALL, 8, COUT), F32)
    for w in range(4):
        slots = [empty] * 4
        for slot in range(4):
            tap = slot * 4 + w
            if tap < 9:
                slots[slot] = mix_sum[tap * COUT : (tap + 1) * COUT].reshape(LON_ALL, 8, COUT)
        for i in range(2):
            sums[w // 2, MIX, w % 2, :, i * COUT : (i + 1) * COUT] = merge_slots(
                slots[2 * i], slots[2 * i + 1]
            )


def backward_part(grid, mix_kernel, slope, outside, pre_grad):
    backward = jnp.concatenate([mix_kernel[i] for i in range(9)], axis=1)
    act_grad = lax.dot_general(
        patches(positions(grid, OUTER, 2), True),
        backward,
        (((1,), (1,)), ((), ())),
        preferred_element_type=F32,
    )
    graded = (beside(act_grad, OUTER) * slope).astype(BF16).astype(F32)
    keep_wide(pre_grad, jnp.where(outside, 0.0, graded))


def grad_window(pre_grad, dr, dc):
    return window(pre_grad, dr * PITCH + dc, INNER, 0, 4).astype(BF16)


def up_part_sums(grid, pre_grad, dc, sums):
    in_own = window(grid, PITCH + 1, INNER, 0, 2)
    in_own = jnp.where(inner_mask(CIN), in_own, 0.0).astype(BF16)
    for dr in range(2):
        up_sum = lax.dot_general(
            in_own,
            grad_window(pre_grad, dr, dc),
            (((0,), (0,)), ((), ())),
            preferred_element_type=F32,
        ).astype(BF16)
        for pr in range(2):
            sums[dr, dc, pr] = up_sum[:, pr * SPAN : (pr + 1) * SPAN]


def section_part(act_patches, mix_kernel, staged, out_wide, section):
    flat_mix = mix_kernel[...].reshape(9 * COUT, COUT)
    staged[...] = jnp.dot(act_patches, flat_mix, preferred_element_type=F32)
    for s in range(2):
        for t in range(2):
            for r in range(ROWS):
                out_wide[pl.ds((2 * r + s) * 2 * COLS + t, COLS, stride=2), :] = staged[
                    pl.ds((2 * s + t) * INNER + r * PITCH, COLS), :
                ]
    section[...] = out_wide[...].astype(BF16)


def input_part(pre_grad, up_kernel, act, input_grad):
    back_up = jnp.concatenate(
        [
            up_kernel[(2 * dr + pr) * 4 + 2 * dc + pc]
            for dr, dc in OFFSETS
            for pr in range(2)
            for pc in range(2)
        ],
        axis=1,
    )
    grad_windows = jnp.concatenate([grad_window(pre_grad, dr, dc) for dr, dc in OFFSETS], axis=1)
    spread = lax.dot_general(
        grad_windows, back_up, (((1,), (1,)), ((), ())), preferred_element_type=F32
    )
    for i in range(2):
        act[i, :INNER, :] = spread[:, i * COUT : (i + 1) * COUT]
        for r in range(ROWS):
            input_grad[r * COLS : (r + 1) * COLS, i * COUT : (i + 1) * COUT] = act[
                i, pl.ds(r * PITCH, COLS), :
            ]


def reduce_partners(lat, lon, z_count, y_count):
    core, x_hi, z = lax.rem(lat, 2), lax.rem(lat // 2, 2), lat // 4
    y, x_lo = lax.rem(lon, y_count), lon // y_count
    return core, x_hi, z, y, x_lo


def fetch(src, dst, send, recv, to):
    copy = pltpu.make_async_remote_copy(
        src_ref=src, dst_ref=dst, send_sem=send, recv_sem=recv, device_id=to, device_id_type=MESH
    )
    copy.start()


def await_bytes(ref, sem):
    pltpu.make_async_copy(ref, ref, sem).wait()


def z_plan(z_count):
    return 3, z_count // 3


def section_kernel(
    lat_count,
    lon_count,
    scale,
    codes_hbm,
    exps_hbm,
    cot_hbm,
    up_hbm,
    bias_hbm,
    mix_hbm,
    section,
    input_grad,
    up_out,
    mix_out,
    codes,
    exps,
    cot,
    up_kernel,
    bias,
    mix_kernel,
    load_sem,
    grid,
    own,
    cot_wide,
    row_out,
    col_out,
    corner_out,
    row_in,
    col_in,
    corner_in,
    halo_send,
    halo_recv,
    act,
    pre_grad,
    staged,
    out_wide,
    sums,
    core_in,
    x_out,
    xa_in,
    xb_in,
    y_out,
    y_in,
    mix_y_in,
    mix_out_x,
    mix_x_in,
    far,
    near,
    final,
    core_sem,
    x_sem,
    y_sem,
    far_sem,
    near_sem,
    final_sem,
    mix_sem,
):
    z_count, y_count = lat_count // 4, lon_count // 2
    far_count, near_count = z_plan(z_count)
    lat, lon = lax.axis_index("lat"), lax.axis_index("lon")
    core, x_hi, z, y, x_lo = reduce_partners(lat, lon, z_count, y_count)
    x = 2 * x_hi + x_lo

    def at_x(step):
        other = lax.rem(x + step + 4, 4)
        return 4 * z + 2 * (other // 2) + core, lax.rem(other, 2) * y_count + y

    def at_y(step):
        return lat, x_lo * y_count + lax.rem(y + step, y_count)

    def at_z(step, row):
        return 4 * lax.rem(z + step + z_count, z_count) + 2 * row + core, lon

    partner = (lat + 1 - 2 * core, lon)
    far_steps = [near_count * i for i in range(1, far_count)]
    near_steps = [i if 2 * i <= near_count else i - near_count for i in range(1, near_count)]

    loads = [
        pltpu.make_async_copy(src, dst, load_sem.at[i])
        for i, (src, dst) in enumerate(
            (
                (exps_hbm, exps),
                (codes_hbm, codes),
                (cot_hbm, cot),
                (up_hbm, up_kernel),
                (mix_hbm, mix_kernel),
                (bias_hbm, bias),
            )
        )
    ]
    for load in loads:
        load.start()

    barrier = pltpu.get_barrier_semaphore()
    up, down, left, right = partners = halo_partners(lat, lon, lat_count, lon_count)
    greeted = [(a, b) for a in (up, down) for b in (left, lon, right)] + [(lat, left), (lat, right)]
    greeted += [partner, at_x(1), at_x(2), at_x(-1)]
    greeted += [at_y(step) for step in range(1, y_count)]
    far_all = sorted({step % z_count for base in far_steps for step in (base, -base)})
    near_all = sorted({step % z_count for base in near_steps for step in (base, -base)})
    greeted += [at_z(step, x_hi) for step in far_all + near_all]
    greeted += [at_z(step, 1 - x_hi) for step in [0] + near_all]
    for to in greeted:
        pl.semaphore_signal(barrier, inc=1, device_id=to, device_id_type=MESH)
    for load in loads[:3]:
        load.wait()
    halo_fill(codes, exps, cot, grid, own, cot_wide, row_out, col_out, corner_out)
    pl.semaphore_wait(barrier, len(greeted))
    halo = halo_copies(
        partners, lat, lon, row_out, col_out, corner_out, row_in, col_in, corner_in, halo_send, halo_recv
    )
    for copy in halo:
        copy.start()
    for load in loads[3:]:
        load.wait()
    for copy in halo:
        copy.wait_recv()
    halo_place(lat, lat_count, grid, row_in, col_in, corner_in)

    def core_start(part):
        fetch(sums.at[1 - core, part], core_in.at[part], core_sem.at[0, part], core_sem.at[1, part], partner)

    half = y_count // 2
    y_steps = sorted(range(1, y_count), key=lambda step: -min(step, y_count - step))

    def core_end(part):
        await_bytes(core_in.at[part], core_sem.at[1, part])
        merged = sums[core, part].astype(F32) + core_in[part].astype(F32)
        x_out[part] = merged.astype(BF16).reshape(x_out.shape[1:])

    def mix_first():
        core_end(MIX)
        for step in y_steps:
            fetch(
                x_out.at[MIX, :, lax.rem(y + step, y_count)],
                mix_y_in.at[step - 1],
                mix_sem.at[0],
                mix_sem.at[1],
                at_y(step),
            )

    def mix_second():
        await_bytes(mix_y_in, mix_sem.at[1])
        total = x_out[MIX, :, y].astype(F32)
        for step in range(y_count - 1):
            total = total + mix_y_in[step].astype(F32)
        mix_out_x[...] = total.astype(BF16)
        for step in (2, 1, 3):
            fetch(
                mix_out_x.at[lax.rem(x + step, 4)],
                mix_x_in.at[step - 1],
                mix_sem.at[2],
                mix_sem.at[3],
                at_x(step),
            )

    def mix_third():
        await_bytes(mix_x_in, mix_sem.at[3])
        total = mix_out_x[x].astype(F32)
        for step in range(3):
            total = total + mix_x_in[step].astype(F32)
        far_send(MIX, total)

    def x_first(part):
        core_end(part)
        across = lax.rem(x + 2, 4)
        for side, step in ((0, 1), (1, -1)):
            fetch(
                x_out.at[part, across, pl.ds(side * half, half)],
                xa_in.at[part, side],
                x_sem.at[0, part, side],
                x_sem.at[1, part, side],
                at_x(step),
            )

    def x_second(part):
        for side, step in ((0, 1), (1, -1)):
            await_bytes(xa_in.at[part, side], x_sem.at[1, part, side])
            beside_x = lax.rem(x + step + 4, 4)
            rows = pl.ds(side * half, half)
            merged = x_out[part, beside_x, rows].astype(F32) + xa_in[part, side].astype(F32)
            x_out[part, beside_x, rows] = merged.astype(BF16)
            fetch(
                x_out.at[part, beside_x],
                xb_in.at[part, side],
                x_sem.at[2, part, side],
                x_sem.at[3, part, side],
                at_x(step),
            )

    def y_start(part):
        for side in range(2):
            await_bytes(xb_in.at[part, side], x_sem.at[3, part, side])
        merged = x_out[part, x].astype(F32) + xb_in[part, 0].astype(F32) + xb_in[part, 1].astype(F32)
        y_out[part] = merged.astype(BF16)
        for step in y_steps:
            fetch(
                y_out.at[part, lax.rem(y + step, y_count)],
                y_in.at[part, step - 1],
                y_sem.at[0, part],
                y_sem.at[1, part],
                at_y(step),
            )

    far_at, near_at = z // near_count, lax.rem(z, near_count)

    def far_start(part):
        await_bytes(y_in.at[part], y_sem.at[1, part])
        total = y_out[part, y].astype(F32)
        for step in range(y_count - 1):
            total = total + y_in[part, step].astype(F32)
        far_send(part, total)

    def far_send(part, total):
        far[part, far_at] = total.astype(BF16)
        for step in far_steps:
            fetch(far.at[part, far_at], far.at[part, far_at], far_sem.at[0, part], far_sem.at[1, part], at_z(step, x_hi))

    def near_start(part):
        await_bytes(far.at[part, pl.ds(0, far_count - 1)], far_sem.at[1, part])
        total = far[part, 0].astype(F32)
        for i in range(1, far_count):
            total = total + far[part, i].astype(F32)
        slot = 2 * near_at + x_hi
        near[part, slot] = total.astype(BF16)
        for to in [at_z(step, 1 - x_hi) for step in [0] + near_steps] + [at_z(step, x_hi) for step in near_steps]:
            fetch(near.at[part, slot], near.at[part, slot], near_sem.at[0, part], near_sem.at[1, part], to)

    def final_start(part):
        await_bytes(near.at[part, pl.ds(0, 2 * near_count - 1)], near_sem.at[1, part])
        for row in range(2):
            total = near[part, row].astype(F32)
            for i in range(1, near_count):
                total = total + near[part, 2 * i + row].astype(F32)
            final[part, core, row] = total * scale
        fetch(
            final.at[part, core], final.at[part, core], final_sem.at[0, part], final_sem.at[1, part], partner
        )

    def finish(part):
        await_bytes(final.at[part, 0], final_sem.at[1, part])
        for w in range(4):
            for i in range(2):
                piece = final[part, w // 2, w % 2, :, i * COUT : (i + 1) * COUT]
                if part != MIX:
                    up_out[w, 2 * part + i] = piece
                    continue
                for slot in range(2):
                    tap = (2 * i + slot) * 4 + w
                    if tap < 9:
                        mix_out[tap] = piece[slot * 8 : slot * 8 + 8]

    slope, outside = forward_part(lat, lat_count, grid, up_kernel, bias, act)
    act_patches = patches(positions(act, INNER, 0), False)
    mix_part_sums(grid, act_patches, sums)
    core_start(MIX)
    backward_part(grid, mix_kernel, slope, outside, pre_grad)
    up_part_sums(grid, pre_grad, 0, sums)
    core_start(0)
    mix_first()
    up_part_sums(grid, pre_grad, 1, sums)
    core_start(1)
    x_first(0)
    x_first(1)
    section_part(act_patches, mix_kernel, staged, out_wide, section)
    for part in UP:
        x_second(part)
    input_part(pre_grad, up_kernel, act, input_grad)
    for part in UP:
        y_start(part)
    mix_second()
    mix_third()
    for part in UP:
        far_start(part)
    for stage in (near_start, final_start):
        for part in ORDER:
            stage(part)
    for copy in halo:
        copy.wait_send()
    await_bytes(mix_y_in, mix_sem.at[0])
    await_bytes(mix_x_in, mix_sem.at[2])
    for part in UP:
        for side in range(2):
            await_bytes(xa_in.at[part, side], x_sem.at[0, part, side])
            await_bytes(xb_in.at[part, side], x_sem.at[2, part, side])
        await_bytes(y_in.at[part], y_sem.at[0, part])
    for part in range(PARTS):
        await_bytes(core_in.at[part], core_sem.at[0, part])
        await_bytes(far.at[part, pl.ds(0, far_count - 1)], far_sem.at[0, part])
        await_bytes(near.at[part, pl.ds(0, 2 * near_count - 1)], near_sem.at[0, part])
        await_bytes(final.at[part, 0], final_sem.at[0, part])
    for part in ORDER:
        finish(part)


def write_kernel(*refs):
    for i in range(4):
        refs[4 + i][...] = refs[i][...]


def shards(elem_codes, block_exps, up_kernel, up_bias, mix_kernel, cotangent):
    lat_count, lon_count = lax.axis_size("lat"), lax.axis_size("lon")
    y_count, z_count = lon_count // 2, lat_count // 4
    far_count, near_count = z_plan(z_count)
    out_cells = 4 * CELLS * lat_count * lon_count
    operands = (
        elem_codes.reshape(CELLS, CIN),
        block_exps.transpose(1, 2, 0).reshape(COLS * CIN // BLOCK, ROWS),
        cotangent.reshape(4 * CELLS, COUT),
        up_kernel.reshape(16, CIN, COUT),
        up_bias.reshape(1, COUT),
        mix_kernel.reshape(9, COUT, COUT),
    )
    dma = pltpu.SemaphoreType.DMA
    results = pl.pallas_call(
        functools.partial(section_kernel, lat_count, lon_count, 1.0 / math.sqrt(out_cells)),
        out_shape=(
            jax.ShapeDtypeStruct((4 * CELLS, COUT), BF16),
            jax.ShapeDtypeStruct((CELLS, CIN), F32),
            jax.ShapeDtypeStruct((4, 4, LON_ALL, COUT), F32),
            jax.ShapeDtypeStruct((9, 8, COUT), F32),
        ),
        in_specs=[pl.BlockSpec(memory_space=pltpu.HBM)] * 6,
        out_specs=[pl.BlockSpec(memory_space=pltpu.VMEM)] * 4,
        scratch_shapes=[pltpu.VMEM(operand.shape, operand.dtype) for operand in operands]
        + [
            dma((6,)),
            pltpu.VMEM((TALL, FLAT, COUT), F32),
            pltpu.VMEM((TALL, CELLS, COUT), F32),
            pltpu.VMEM((4 * CELLS, COUT), F32),
            pltpu.VMEM((2, TALL // 2, 2 * COLS, COUT), BF16),
            pltpu.VMEM((2, TALL, ROWS, COUT), BF16),
            pltpu.VMEM((4, 8, COUT), F32),
            pltpu.VMEM((2, TALL // 2, 2 * COLS, COUT), BF16),
            pltpu.VMEM((2, TALL, ROWS, COUT), BF16),
            pltpu.VMEM((4, 8, COUT), F32),
            dma((8,)),
            dma((8,)),
            pltpu.VMEM((4, FLAT, COUT), F32),
            pltpu.VMEM((4, FLAT, COUT), F32),
            pltpu.VMEM((4 * INNER, COUT), F32),
            pltpu.VMEM((4 * CELLS, COUT), F32),
            pltpu.VMEM((2, PARTS, 2, CIN, SPAN), BF16),
            pltpu.VMEM((PARTS, 2, CIN, SPAN), BF16),
            pltpu.VMEM((PARTS, 4, y_count, 16, SPAN), BF16),
            pltpu.VMEM((2, 2, y_count // 2, 16, SPAN), BF16),
            pltpu.VMEM((2, 2, y_count, 16, SPAN), BF16),
            pltpu.VMEM((2, y_count, 16, SPAN), BF16),
            pltpu.VMEM((2, y_count - 1, 16, SPAN), BF16),
            pltpu.VMEM((y_count - 1, 4, 16, SPAN), BF16),
            pltpu.VMEM((4, 16, SPAN), BF16),
            pltpu.VMEM((3, 16, SPAN), BF16),
            pltpu.VMEM((PARTS, far_count, 16, SPAN), BF16),
            pltpu.VMEM((PARTS, 2 * near_count, 16, SPAN), BF16),
            pltpu.VMEM((PARTS, 2, 2, 16, SPAN), F32),
            dma((2, PARTS)),
            dma((4, 2, 2)),
            dma((2, 2)),
            dma((2, PARTS)),
            dma((2, PARTS)),
            dma((2, PARTS)),
            dma((4,)),
        ],
        compiler_params=pltpu.CompilerParams(
            collective_id=0, has_side_effects=True, vmem_limit_bytes=56 * 2**20
        ),
    )(*operands)
    section, input_grad, up_part, mix_part = pl.pallas_call(
        write_kernel,
        out_shape=tuple(jax.ShapeDtypeStruct(result.shape, result.dtype) for result in results),
        in_specs=[pl.BlockSpec(memory_space=pltpu.VMEM)] * 4,
        out_specs=[pl.BlockSpec(memory_space=pltpu.VMEM)] * 4,
        compiler_params=pltpu.CompilerParams(vmem_limit_bytes=56 * 2**20),
    )(*results)
    return (
        section.reshape(2 * ROWS, 2 * COLS, COUT),
        input_grad.reshape(ROWS, COLS, CIN),
        up_part,
        mix_part.reshape(3, 3, 8, COUT),
    )


def solution(mesh):
    placed = (P("lat", "lon", None), P("lat", "lon", None), P(), P(), P(), P("lat", "lon", None))
    return jax.shard_map(
        shards,
        mesh=mesh,
        in_specs=placed,
        out_specs=(
            P("lat", "lon", None),
            P("lat", "lon", None),
            P(None, None, "lon", None),
            P(None, None, "lon", None),
        ),
        check_vma=False,
    )
```

```python
import functools
import math

import jax
import jax.numpy as jnp
from jax import lax
from jax.experimental import pallas as pl
from jax.experimental.pallas import tpu as pltpu
from jax.sharding import PartitionSpec as P

CIN = 256
COUT = 128
BLOCK = 32
ROWS = 16
COLS = 8
PITCH = 10
CELLS = ROWS * COLS
TALL = CIN // COUT + 4
FLAT = 192
OUTER = 176
INNER = ROWS * PITCH
PARTS = 3
SPAN = 2 * COUT
MIX = 2
ORDER = (2, 0, 1)
UP = (0, 1)
LON_ALL = 16
MESH = pl.DeviceIdType.MESH
F32 = jnp.float32
BF16 = jnp.bfloat16


def power_bits(value, bits):
    total = jnp.where(value & 1 != 0, 2.0, 1.0)
    for bit in range(1, bits):
        total = total * jnp.where(value & (1 << bit) != 0, float(1 << (1 << bit)), 1.0)
    return total


def decode(codes, factor):
    sign = jnp.where(codes >= 128, -(2.0**-9), 2.0**-9)
    fraction = (8 + (codes & 7)).astype(F32) * 0.125
    return sign * power_bits((codes >> 3) & 15, 4) * fraction * factor


def block_factors(exps, own):
    factor = power_bits(exps + 2, 2).astype(BF16)
    count = exps.shape[0]
    lane = lax.broadcasted_iota(jnp.int32, (count, COLS * CIN), 1)
    row = lax.broadcasted_iota(jnp.int32, (count, COLS * CIN), 0)
    spread = jnp.where(lane // BLOCK == row, 1.0, 0.0).astype(BF16)
    wide = lax.dot_general(factor, spread, (((0,), (0,)), ((), ())), preferred_element_type=F32)
    for c in range(COLS):
        for i in range(CIN // COUT):
            at = c * CIN + i * COUT
            own[i, pl.ds(c, ROWS, stride=COLS), :] = wide[:, at : at + COUT]


def halo_partners(lat, lon, lat_count, lon_count):
    up, down = lax.rem(lat + lat_count - 1, lat_count), lax.rem(lat + 1, lat_count)
    left, right = lax.rem(lon + lon_count - 1, lon_count), lax.rem(lon + 1, lon_count)
    return up, down, left, right


def halo_fill(codes, exps, cot, grid, own, cot_wide, row_out, col_out, corner_out):
    block_factors(exps[...], own)
    for i in range(CIN // COUT):
        own[i] = decode(codes[:, i * COUT : (i + 1) * COUT], own[i])
    cot_wide[...] = cot[...].astype(F32)
    for r in range(ROWS):
        for s in range(2):
            for t in range(2):
                own[2 + 2 * s + t, r * COLS : (r + 1) * COLS, :] = cot_wide[
                    pl.ds((2 * r + s) * 2 * COLS + t, COLS, stride=2), :
                ]
    for side, r in enumerate((ROWS - 1, 0)):
        for i in range(TALL // 2):
            row_out[side, i] = jnp.concatenate(
                [own[j, r * COLS : (r + 1) * COLS, :] for j in (2 * i, 2 * i + 1)], axis=0
            ).astype(BF16)
    for side, c in enumerate((COLS - 1, 0)):
        for i in range(TALL):
            col_out[side, i] = own[i, pl.ds(c, ROWS, stride=COLS), :].astype(BF16)
    for corner, (r, c) in enumerate(((ROWS - 1, COLS - 1), (ROWS - 1, 0), (0, COLS - 1), (0, 0))):
        cell = r * COLS + c
        corner_out[corner] = jnp.zeros((8, COUT), F32)
        for i in range(TALL):
            corner_out[corner, i : i + 1, :] = own[i, cell : cell + 1, :]
    for r in range(ROWS):
        at = (r + 1) * PITCH + 1
        for i in range(TALL):
            grid[i, at : at + COLS, :] = own[i, r * COLS : (r + 1) * COLS, :]
    tail = (ROWS + 2) * PITCH
    for i in range(TALL):
        grid[i, tail:FLAT, :] = jnp.zeros((FLAT - tail, COUT), F32)


def halo_copies(partners, lat, lon, row_out, col_out, corner_out, row_in, col_in, corner_in, send, recv):
    up, down, left, right = partners
    plan = [
        (row_out.at[0], row_in.at[0], down, lon),
        (row_out.at[1], row_in.at[1], up, lon),
        (col_out.at[0], col_in.at[0], lat, right),
        (col_out.at[1], col_in.at[1], lat, left),
        (corner_out.at[0], corner_in.at[0], down, right),
        (corner_out.at[1], corner_in.at[1], down, left),
        (corner_out.at[2], corner_in.at[2], up, right),
        (corner_out.at[3], corner_in.at[3], up, left),
    ]
    return [
        pltpu.make_async_remote_copy(
            src_ref=src,
            dst_ref=dst,
            send_sem=send.at[i],
            recv_sem=recv.at[i],
            device_id=(to_lat, to_lon),
            device_id_type=MESH,
        )
        for i, (src, dst, to_lat, to_lon) in enumerate(plan)
    ]


def halo_place(lat, lat_count, grid, row_in, col_in, corner_in):
    above = (lat > 0).astype(F32)
    below = (lat < lat_count - 1).astype(F32)
    for side, (r, keep) in enumerate(((0, above), (ROWS + 1, below))):
        at = r * PITCH + 1
        for i in range(TALL // 2):
            part = row_in[side, i].astype(F32) * keep
            grid[2 * i, at : at + COLS, :] = part[:COLS]
            grid[2 * i + 1, at : at + COLS, :] = part[COLS:]
    for side, c in enumerate((0, COLS + 1)):
        for i in range(TALL):
            grid[i, pl.ds(PITCH + c, ROWS, stride=PITCH), :] = col_in[side, i].astype(F32)
    places = ((0, 0, above), (0, COLS + 1, above), (ROWS + 1, 0, below), (ROWS + 1, COLS + 1, below))
    for corner, (r, c, keep) in enumerate(places):
        cell = r * PITCH + c
        for i in range(TALL):
            grid[i, cell : cell + 1, :] = corner_in[corner, i : i + 1, :] * keep


OFFSETS = ((0, 0), (0, 1), (1, 0), (1, 1))


def positions(ref, length, low):
    found = {}
    for dr, dc in OFFSETS:
        for pr in range(2):
            for pc in range(2):
                found[2 * dr + pr, 2 * dc + pc] = ref[
                    low + 2 * pr + pc, pl.ds(dr * PITCH + dc, length), :
                ].astype(BF16)
    return found


def window(ref, start, length, low, high):
    return jnp.concatenate([ref[i, pl.ds(start, length), :] for i in range(low, high)], axis=1)


def keep_wide(ref, value):
    for i in range(4):
        ref[i, :OUTER, :] = value[:, i * COUT : (i + 1) * COUT]
        ref[i, OUTER:, :] = jnp.zeros((FLAT - OUTER, COUT), F32)


def patches(found, flipped):
    stacked = []
    for s in range(2):
        for t in range(2):
            pieces = []
            for ky in range(3):
                for kx in range(3):
                    at = (s - ky + 2, t - kx + 2) if flipped else (s + ky, t + kx)
                    pieces.append(found[at])
            stacked.append(jnp.concatenate(pieces, axis=1))
    return jnp.concatenate(stacked, axis=0)


def beside(array, rows):
    return jnp.concatenate([array[i * rows : (i + 1) * rows] for i in range(4)], axis=1)


def inner_mask(lanes):
    cell = lax.broadcasted_iota(jnp.int32, (INNER, lanes), 0)
    return lax.rem(cell, PITCH) < COLS


def merge_slots(even, odd):
    return jnp.concatenate([even, odd], axis=1).reshape(CIN, COUT).astype(BF16)


def forward_part(lat, lat_count, grid, up_kernel, bias, act):
    windows = [window(grid, dr * PITCH + dc, OUTER, 0, 2).astype(BF16) for dr, dc in OFFSETS]
    forward = jnp.concatenate(
        [
            jnp.concatenate(
                [
                    up_kernel[(2 * (1 - dr) + pr) * 4 + 2 * (1 - dc) + pc]
                    for pr in range(2)
                    for pc in range(2)
                ],
                axis=1,
            )
            for dr, dc in OFFSETS
        ],
        axis=0,
    )
    raw = jnp.dot(jnp.concatenate(windows, axis=1), forward, preferred_element_type=F32)
    plain = (raw + jnp.concatenate([bias[...]] * 4, axis=1)).astype(BF16).astype(F32)
    sigmoid = jax.nn.sigmoid(plain)
    activated = (plain * sigmoid).astype(BF16).astype(F32)
    cell = lax.broadcasted_iota(jnp.int32, (OUTER, 4 * COUT), 0)
    lane = lax.broadcasted_iota(jnp.int32, (OUTER, 4 * COUT), 1)
    outside = ((cell < PITCH) & (lane < 2 * COUT) & (lat == 0)) | (
        (cell >= ROWS * PITCH) & (lane >= 2 * COUT) & (lat == lat_count - 1)
    )
    keep_wide(act, jnp.where(outside, 0.0, activated))
    return sigmoid * (1.0 + plain * (1.0 - sigmoid)), outside


def mix_part_sums(grid, act_patches, sums):
    cot_own = window(grid, PITCH + 1, INNER, 2, TALL)
    cot_own = jnp.where(inner_mask(4 * COUT), cot_own, 0.0).astype(BF16)
    cot_stacked = jnp.concatenate([cot_own[:, i * COUT : (i + 1) * COUT] for i in range(4)], axis=0)
    mix_sum = lax.dot_general(
        act_patches, cot_stacked, (((0,), (0,)), ((), ())), preferred_element_type=F32
    )
    empty = jnp.zeros((LON_ALL, 8, COUT), F32)
    for w in range(4):
        slots = [empty] * 4
        for slot in range(4):
            tap = slot * 4 + w
            if tap < 9:
                slots[slot] = mix_sum[tap * COUT : (tap + 1) * COUT].reshape(LON_ALL, 8, COUT)
        for i in range(2):
            sums[w // 2, MIX, w % 2, :, i * COUT : (i + 1) * COUT] = merge_slots(
                slots[2 * i], slots[2 * i + 1]
            )


def backward_part(grid, mix_kernel, slope, outside, pre_grad):
    backward = jnp.concatenate([mix_kernel[i] for i in range(9)], axis=1)
    act_grad = lax.dot_general(
        patches(positions(grid, OUTER, 2), True),
        backward,
        (((1,), (1,)), ((), ())),
        preferred_element_type=F32,
    )
    graded = (beside(act_grad, OUTER) * slope).astype(BF16).astype(F32)
    keep_wide(pre_grad, jnp.where(outside, 0.0, graded))


def grad_window(pre_grad, dr, dc):
    return window(pre_grad, dr * PITCH + dc, INNER, 0, 4).astype(BF16)


def up_part_sums(grid, pre_grad, dc, sums):
    in_own = window(grid, PITCH + 1, INNER, 0, 2)
    in_own = jnp.where(inner_mask(CIN), in_own, 0.0).astype(BF16)
    for dr in range(2):
        up_sum = lax.dot_general(
            in_own,
            grad_window(pre_grad, dr, dc),
            (((0,), (0,)), ((), ())),
            preferred_element_type=F32,
        ).astype(BF16)
        for pr in range(2):
            sums[dr, dc, pr] = up_sum[:, pr * SPAN : (pr + 1) * SPAN]


def section_part(act_patches, mix_kernel, staged, out_wide, section):
    flat_mix = mix_kernel[...].reshape(9 * COUT, COUT)
    staged[...] = jnp.dot(act_patches, flat_mix, preferred_element_type=F32)
    for s in range(2):
        for t in range(2):
            for r in range(ROWS):
                out_wide[pl.ds((2 * r + s) * 2 * COLS + t, COLS, stride=2), :] = staged[
                    pl.ds((2 * s + t) * INNER + r * PITCH, COLS), :
                ]
    section[...] = out_wide[...].astype(BF16)


def input_part(pre_grad, up_kernel, act, input_grad):
    back_up = jnp.concatenate(
        [
            up_kernel[(2 * dr + pr) * 4 + 2 * dc + pc]
            for dr, dc in OFFSETS
            for pr in range(2)
            for pc in range(2)
        ],
        axis=1,
    )
    grad_windows = jnp.concatenate([grad_window(pre_grad, dr, dc) for dr, dc in OFFSETS], axis=1)
    spread = lax.dot_general(
        grad_windows, back_up, (((1,), (1,)), ((), ())), preferred_element_type=F32
    )
    for i in range(2):
        act[i, :INNER, :] = spread[:, i * COUT : (i + 1) * COUT]
        for r in range(ROWS):
            input_grad[r * COLS : (r + 1) * COLS, i * COUT : (i + 1) * COUT] = act[
                i, pl.ds(r * PITCH, COLS), :
            ]


def reduce_partners(lat, lon, z_count, y_count):
    core, x_hi, z = lax.rem(lat, 2), lax.rem(lat // 2, 2), lat // 4
    y, x_lo = lax.rem(lon, y_count), lon // y_count
    return core, x_hi, z, y, x_lo


def fetch(src, dst, send, recv, to):
    copy = pltpu.make_async_remote_copy(
        src_ref=src, dst_ref=dst, send_sem=send, recv_sem=recv, device_id=to, device_id_type=MESH
    )
    copy.start()


def await_bytes(ref, sem):
    pltpu.make_async_copy(ref, ref, sem).wait()


def z_plan(z_count):
    return 3, z_count // 3


def section_kernel(
    lat_count,
    lon_count,
    scale,
    codes_hbm,
    exps_hbm,
    cot_hbm,
    up_hbm,
    bias_hbm,
    mix_hbm,
    section,
    input_grad,
    up_out,
    mix_out,
    codes,
    exps,
    cot,
    up_kernel,
    bias,
    mix_kernel,
    load_sem,
    grid,
    own,
    cot_wide,
    row_out,
    col_out,
    corner_out,
    row_in,
    col_in,
    corner_in,
    halo_send,
    halo_recv,
    act,
    pre_grad,
    staged,
    out_wide,
    sums,
    core_in,
    x_out,
    xa_in,
    xb_in,
    y_out,
    y_in,
    mix_y_in,
    mix_out_x,
    mix_x_in,
    far,
    near,
    final,
    core_sem,
    x_sem,
    y_sem,
    far_sem,
    near_sem,
    final_sem,
    mix_sem,
):
    z_count, y_count = lat_count // 4, lon_count // 2
    far_count, near_count = z_plan(z_count)
    lat, lon = lax.axis_index("lat"), lax.axis_index("lon")
    core, x_hi, z, y, x_lo = reduce_partners(lat, lon, z_count, y_count)
    x = 2 * x_hi + x_lo

    def at_x(step):
        other = lax.rem(x + step + 4, 4)
        return 4 * z + 2 * (other // 2) + core, lax.rem(other, 2) * y_count + y

    def at_y(step):
        return lat, x_lo * y_count + lax.rem(y + step, y_count)

    def at_z(step, row):
        return 4 * lax.rem(z + step + z_count, z_count) + 2 * row + core, lon

    partner = (lat + 1 - 2 * core, lon)
    far_steps = [near_count * i for i in range(1, far_count)]
    near_steps = [i if 2 * i <= near_count else i - near_count for i in range(1, near_count)]

    loads = [
        pltpu.make_async_copy(src, dst, load_sem.at[i])
        for i, (src, dst) in enumerate(
            (
                (exps_hbm, exps),
                (codes_hbm, codes),
                (cot_hbm, cot),
                (up_hbm, up_kernel),
                (mix_hbm, mix_kernel),
                (bias_hbm, bias),
            )
        )
    ]
    for load in loads:
        load.start()

    barrier = pltpu.get_barrier_semaphore()
    up, down, left, right = partners = halo_partners(lat, lon, lat_count, lon_count)
    greeted = [(a, b) for a in (up, down) for b in (left, lon, right)] + [(lat, left), (lat, right)]
    greeted += [partner, at_x(1), at_x(2), at_x(-1)]
    greeted += [at_y(step) for step in range(1, y_count)]
    far_all = sorted({step % z_count for base in far_steps for step in (base, -base)})
    near_all = sorted({step % z_count for base in near_steps for step in (base, -base)})
    greeted += [at_z(step, x_hi) for step in far_all + near_all]
    greeted += [at_z(step, 1 - x_hi) for step in [0] + near_all]
    for to in greeted:
        pl.semaphore_signal(barrier, inc=1, device_id=to, device_id_type=MESH)
    for load in loads[:3]:
        load.wait()
    halo_fill(codes, exps, cot, grid, own, cot_wide, row_out, col_out, corner_out)
    pl.semaphore_wait(barrier, len(greeted))
    halo = halo_copies(
        partners, lat, lon, row_out, col_out, corner_out, row_in, col_in, corner_in, halo_send, halo_recv
    )
    for copy in reversed(halo):
        copy.start()
    for load in loads[3:]:
        load.wait()
    for copy in halo:
        copy.wait_recv()
    halo_place(lat, lat_count, grid, row_in, col_in, corner_in)

    def core_start(part):
        fetch(sums.at[1 - core, part], core_in.at[part], core_sem.at[0, part], core_sem.at[1, part], partner)

    half = y_count // 2
    y_steps = sorted(range(1, y_count), key=lambda step: -min(step, y_count - step))

    def core_end(part):
        await_bytes(core_in.at[part], core_sem.at[1, part])
        merged = sums[core, part].astype(F32) + core_in[part].astype(F32)
        x_out[part] = merged.astype(BF16).reshape(x_out.shape[1:])

    def mix_first():
        core_end(MIX)
        for step in y_steps:
            fetch(
                x_out.at[MIX, :, lax.rem(y + step, y_count)],
                mix_y_in.at[step - 1],
                mix_sem.at[0],
                mix_sem.at[1],
                at_y(step),
            )

    def mix_second():
        await_bytes(mix_y_in, mix_sem.at[1])
        total = x_out[MIX, :, y].astype(F32)
        for step in range(y_count - 1):
            total = total + mix_y_in[step].astype(F32)
        mix_out_x[...] = total.astype(BF16)
        for step in (2, 1, 3):
            fetch(
                mix_out_x.at[lax.rem(x + step, 4)],
                mix_x_in.at[step - 1],
                mix_sem.at[2],
                mix_sem.at[3],
                at_x(step),
            )

    def mix_third():
        await_bytes(mix_x_in, mix_sem.at[3])
        total = mix_out_x[x].astype(F32)
        for step in range(3):
            total = total + mix_x_in[step].astype(F32)
        far_send(MIX, total)

    def x_first(part):
        core_end(part)
        across = lax.rem(x + 2, 4)
        for side, step in ((0, 1), (1, -1)):
            fetch(
                x_out.at[part, across, pl.ds(side * half, half)],
                xa_in.at[part, side],
                x_sem.at[0, part, side],
                x_sem.at[1, part, side],
                at_x(step),
            )

    def x_second(part):
        for side, step in ((0, 1), (1, -1)):
            await_bytes(xa_in.at[part, side], x_sem.at[1, part, side])
            beside_x = lax.rem(x + step + 4, 4)
            rows = pl.ds(side * half, half)
            merged = x_out[part, beside_x, rows].astype(F32) + xa_in[part, side].astype(F32)
            x_out[part, beside_x, rows] = merged.astype(BF16)
            fetch(
                x_out.at[part, beside_x],
                xb_in.at[part, side],
                x_sem.at[2, part, side],
                x_sem.at[3, part, side],
                at_x(step),
            )

    def y_start(part):
        for side in range(2):
            await_bytes(xb_in.at[part, side], x_sem.at[3, part, side])
        merged = x_out[part, x].astype(F32) + xb_in[part, 0].astype(F32) + xb_in[part, 1].astype(F32)
        y_out[part] = merged.astype(BF16)
        for step in y_steps:
            fetch(
                y_out.at[part, lax.rem(y + step, y_count)],
                y_in.at[part, step - 1],
                y_sem.at[0, part],
                y_sem.at[1, part],
                at_y(step),
            )

    far_at, near_at = z // near_count, lax.rem(z, near_count)

    def far_start(part):
        await_bytes(y_in.at[part], y_sem.at[1, part])
        total = y_out[part, y].astype(F32)
        for step in range(y_count - 1):
            total = total + y_in[part, step].astype(F32)
        far_send(part, total)

    def far_send(part, total):
        far[part, far_at] = total.astype(BF16)
        for step in far_steps:
            fetch(far.at[part, far_at], far.at[part, far_at], far_sem.at[0, part], far_sem.at[1, part], at_z(step, x_hi))

    def near_start(part):
        await_bytes(far.at[part, pl.ds(0, far_count - 1)], far_sem.at[1, part])
        total = far[part, 0].astype(F32)
        for i in range(1, far_count):
            total = total + far[part, i].astype(F32)
        slot = 2 * near_at + x_hi
        near[part, slot] = total.astype(BF16)
        for to in [at_z(step, 1 - x_hi) for step in [0] + near_steps] + [at_z(step, x_hi) for step in near_steps]:
            fetch(near.at[part, slot], near.at[part, slot], near_sem.at[0, part], near_sem.at[1, part], to)

    def final_start(part):
        await_bytes(near.at[part, pl.ds(0, 2 * near_count - 1)], near_sem.at[1, part])
        for row in range(2):
            total = near[part, row].astype(F32)
            for i in range(1, near_count):
                total = total + near[part, 2 * i + row].astype(F32)
            final[part, core, row] = total * scale
        fetch(
            final.at[part, core], final.at[part, core], final_sem.at[0, part], final_sem.at[1, part], partner
        )

    def finish(part):
        await_bytes(final.at[part, 0], final_sem.at[1, part])
        for w in range(4):
            for i in range(2):
                piece = final[part, w // 2, w % 2, :, i * COUT : (i + 1) * COUT]
                if part != MIX:
                    up_out[w, 2 * part + i] = piece
                    continue
                for slot in range(2):
                    tap = (2 * i + slot) * 4 + w
                    if tap < 9:
                        mix_out[tap] = piece[slot * 8 : slot * 8 + 8]

    slope, outside = forward_part(lat, lat_count, grid, up_kernel, bias, act)
    act_patches = patches(positions(act, INNER, 0), False)
    mix_part_sums(grid, act_patches, sums)
    core_start(MIX)
    backward_part(grid, mix_kernel, slope, outside, pre_grad)
    up_part_sums(grid, pre_grad, 0, sums)
    core_start(0)
    mix_first()
    up_part_sums(grid, pre_grad, 1, sums)
    core_start(1)
    x_first(0)
    x_first(1)
    for part in UP:
        x_second(part)
    for part in UP:
        y_start(part)
    mix_second()
    section_part(act_patches, mix_kernel, staged, out_wide, section)
    mix_third()
    for part in UP:
        far_start(part)
    input_part(pre_grad, up_kernel, act, input_grad)
    for stage in (near_start, final_start):
        for part in ORDER:
            stage(part)
    for copy in halo:
        copy.wait_send()
    await_bytes(mix_y_in, mix_sem.at[0])
    await_bytes(mix_x_in, mix_sem.at[2])
    for part in UP:
        for side in range(2):
            await_bytes(xa_in.at[part, side], x_sem.at[0, part, side])
            await_bytes(xb_in.at[part, side], x_sem.at[2, part, side])
        await_bytes(y_in.at[part], y_sem.at[0, part])
    for part in range(PARTS):
        await_bytes(core_in.at[part], core_sem.at[0, part])
        await_bytes(far.at[part, pl.ds(0, far_count - 1)], far_sem.at[0, part])
        await_bytes(near.at[part, pl.ds(0, 2 * near_count - 1)], near_sem.at[0, part])
        await_bytes(final.at[part, 0], final_sem.at[0, part])
    for part in ORDER:
        finish(part)


def write_kernel(*refs):
    for i in range(4):
        refs[4 + i][...] = refs[i][...]


def shards(elem_codes, block_exps, up_kernel, up_bias, mix_kernel, cotangent):
    lat_count, lon_count = lax.axis_size("lat"), lax.axis_size("lon")
    y_count, z_count = lon_count // 2, lat_count // 4
    far_count, near_count = z_plan(z_count)
    out_cells = 4 * CELLS * lat_count * lon_count
    operands = (
        elem_codes.reshape(CELLS, CIN),
        block_exps.transpose(1, 2, 0).reshape(COLS * CIN // BLOCK, ROWS),
        cotangent.reshape(4 * CELLS, COUT),
        up_kernel.reshape(16, CIN, COUT),
        up_bias.reshape(1, COUT),
        mix_kernel.reshape(9, COUT, COUT),
    )
    dma = pltpu.SemaphoreType.DMA
    results = pl.pallas_call(
        functools.partial(section_kernel, lat_count, lon_count, 1.0 / math.sqrt(out_cells)),
        out_shape=(
            jax.ShapeDtypeStruct((4 * CELLS, COUT), BF16),
            jax.ShapeDtypeStruct((CELLS, CIN), F32),
            jax.ShapeDtypeStruct((4, 4, LON_ALL, COUT), F32),
            jax.ShapeDtypeStruct((9, 8, COUT), F32),
        ),
        in_specs=[pl.BlockSpec(memory_space=pltpu.HBM)] * 6,
        out_specs=[pl.BlockSpec(memory_space=pltpu.VMEM)] * 4,
        scratch_shapes=[pltpu.VMEM(operand.shape, operand.dtype) for operand in operands]
        + [
            dma((6,)),
            pltpu.VMEM((TALL, FLAT, COUT), F32),
            pltpu.VMEM((TALL, CELLS, COUT), F32),
            pltpu.VMEM((4 * CELLS, COUT), F32),
            pltpu.VMEM((2, TALL // 2, 2 * COLS, COUT), BF16),
            pltpu.VMEM((2, TALL, ROWS, COUT), BF16),
            pltpu.VMEM((4, 8, COUT), F32),
            pltpu.VMEM((2, TALL // 2, 2 * COLS, COUT), BF16),
            pltpu.VMEM((2, TALL, ROWS, COUT), BF16),
            pltpu.VMEM((4, 8, COUT), F32),
            dma((8,)),
            dma((8,)),
            pltpu.VMEM((4, FLAT, COUT), F32),
            pltpu.VMEM((4, FLAT, COUT), F32),
            pltpu.VMEM((4 * INNER, COUT), F32),
            pltpu.VMEM((4 * CELLS, COUT), F32),
            pltpu.VMEM((2, PARTS, 2, CIN, SPAN), BF16),
            pltpu.VMEM((PARTS, 2, CIN, SPAN), BF16),
            pltpu.VMEM((PARTS, 4, y_count, 16, SPAN), BF16),
            pltpu.VMEM((2, 2, y_count // 2, 16, SPAN), BF16),
            pltpu.VMEM((2, 2, y_count, 16, SPAN), BF16),
            pltpu.VMEM((2, y_count, 16, SPAN), BF16),
            pltpu.VMEM((2, y_count - 1, 16, SPAN), BF16),
            pltpu.VMEM((y_count - 1, 4, 16, SPAN), BF16),
            pltpu.VMEM((4, 16, SPAN), BF16),
            pltpu.VMEM((3, 16, SPAN), BF16),
            pltpu.VMEM((PARTS, far_count, 16, SPAN), BF16),
            pltpu.VMEM((PARTS, 2 * near_count, 16, SPAN), BF16),
            pltpu.VMEM((PARTS, 2, 2, 16, SPAN), F32),
            dma((2, PARTS)),
            dma((4, 2, 2)),
            dma((2, 2)),
            dma((2, PARTS)),
            dma((2, PARTS)),
            dma((2, PARTS)),
            dma((4,)),
        ],
        compiler_params=pltpu.CompilerParams(
            collective_id=0, has_side_effects=True, vmem_limit_bytes=56 * 2**20
        ),
    )(*operands)
    section, input_grad, up_part, mix_part = pl.pallas_call(
        write_kernel,
        out_shape=tuple(jax.ShapeDtypeStruct(result.shape, result.dtype) for result in results),
        in_specs=[pl.BlockSpec(memory_space=pltpu.VMEM)] * 4,
        out_specs=[pl.BlockSpec(memory_space=pltpu.VMEM)] * 4,
        compiler_params=pltpu.CompilerParams(vmem_limit_bytes=56 * 2**20),
    )(*results)
    return (
        section.reshape(2 * ROWS, 2 * COLS, COUT),
        input_grad.reshape(ROWS, COLS, CIN),
        up_part,
        mix_part.reshape(3, 3, 8, COUT),
    )


def solution(mesh):
    placed = (P("lat", "lon", None), P("lat", "lon", None), P(), P(), P(), P("lat", "lon", None))
    return jax.shard_map(
        shards,
        mesh=mesh,
        in_specs=placed,
        out_specs=(
            P("lat", "lon", None),
            P("lat", "lon", None),
            P(None, None, "lon", None),
            P(None, None, "lon", None),
        ),
        check_vma=False,
    )
```

```python
import functools
import math

import jax
import jax.numpy as jnp
from jax import lax
from jax.experimental import pallas as pl
from jax.experimental.pallas import tpu as pltpu
from jax.sharding import PartitionSpec as P

CIN = 256
COUT = 128
BLOCK = 32
ROWS = 16
COLS = 8
PITCH = 10
CELLS = ROWS * COLS
TALL = CIN // COUT + 4
FLAT = 192
OUTER = 176
INNER = ROWS * PITCH
PARTS = 3
SPAN = 2 * COUT
MIX = 2
ORDER = (2, 0, 1)
UP = (0, 1)
LON_ALL = 16
MESH = pl.DeviceIdType.MESH
F32 = jnp.float32
BF16 = jnp.bfloat16


def power_bits(value, bits):
    total = jnp.where(value & 1 != 0, 2.0, 1.0)
    for bit in range(1, bits):
        total = total * jnp.where(value & (1 << bit) != 0, float(1 << (1 << bit)), 1.0)
    return total


def decode(codes, factor):
    sign = jnp.where(codes >= 128, -(2.0**-9), 2.0**-9)
    fraction = (8 + (codes & 7)).astype(F32) * 0.125
    return sign * power_bits((codes >> 3) & 15, 4) * fraction * factor


def block_factors(exps, own):
    factor = power_bits(exps + 2, 2).astype(BF16)
    count = exps.shape[0]
    lane = lax.broadcasted_iota(jnp.int32, (count, COLS * CIN), 1)
    row = lax.broadcasted_iota(jnp.int32, (count, COLS * CIN), 0)
    spread = jnp.where(lane // BLOCK == row, 1.0, 0.0).astype(BF16)
    wide = lax.dot_general(factor, spread, (((0,), (0,)), ((), ())), preferred_element_type=F32)
    for c in range(COLS):
        for i in range(CIN // COUT):
            at = c * CIN + i * COUT
            own[i, pl.ds(c, ROWS, stride=COLS), :] = wide[:, at : at + COUT]


def halo_partners(lat, lon, lat_count, lon_count):
    up, down = lax.rem(lat + lat_count - 1, lat_count), lax.rem(lat + 1, lat_count)
    left, right = lax.rem(lon + lon_count - 1, lon_count), lax.rem(lon + 1, lon_count)
    return up, down, left, right


def halo_fill(codes, exps, cot, grid, own, cot_wide, row_out, col_out, corner_out):
    block_factors(exps[...], own)
    for i in range(CIN // COUT):
        own[i] = decode(codes[:, i * COUT : (i + 1) * COUT], own[i])
    cot_wide[...] = cot[...].astype(F32)
    for r in range(ROWS):
        for s in range(2):
            for t in range(2):
                own[2 + 2 * s + t, r * COLS : (r + 1) * COLS, :] = cot_wide[
                    pl.ds((2 * r + s) * 2 * COLS + t, COLS, stride=2), :
                ]
    for side, r in enumerate((ROWS - 1, 0)):
        for i in range(TALL // 2):
            row_out[side, i] = jnp.concatenate(
                [own[j, r * COLS : (r + 1) * COLS, :] for j in (2 * i, 2 * i + 1)], axis=0
            ).astype(BF16)
    for side, c in enumerate((COLS - 1, 0)):
        for i in range(TALL):
            col_out[side, i] = own[i, pl.ds(c, ROWS, stride=COLS), :].astype(BF16)
    for corner, (r, c) in enumerate(((ROWS - 1, COLS - 1), (ROWS - 1, 0), (0, COLS - 1), (0, 0))):
        cell = r * COLS + c
        corner_out[corner] = jnp.zeros((8, COUT), F32)
        for i in range(TALL):
            corner_out[corner, i : i + 1, :] = own[i, cell : cell + 1, :]
    for r in range(ROWS):
        at = (r + 1) * PITCH + 1
        for i in range(TALL):
            grid[i, at : at + COLS, :] = own[i, r * COLS : (r + 1) * COLS, :]
    tail = (ROWS + 2) * PITCH
    for i in range(TALL):
        grid[i, tail:FLAT, :] = jnp.zeros((FLAT - tail, COUT), F32)


def halo_copies(partners, lat, lon, row_out, col_out, corner_out, row_in, col_in, corner_in, send, recv):
    up, down, left, right = partners
    plan = [
        (row_out.at[0], row_in.at[0], down, lon),
        (row_out.at[1], row_in.at[1], up, lon),
        (col_out.at[0], col_in.at[0], lat, right),
        (col_out.at[1], col_in.at[1], lat, left),
        (corner_out.at[0], corner_in.at[0], down, right),
        (corner_out.at[1], corner_in.at[1], down, left),
        (corner_out.at[2], corner_in.at[2], up, right),
        (corner_out.at[3], corner_in.at[3], up, left),
    ]
    return [
        pltpu.make_async_remote_copy(
            src_ref=src,
            dst_ref=dst,
            send_sem=send.at[i],
            recv_sem=recv.at[i],
            device_id=(to_lat, to_lon),
            device_id_type=MESH,
        )
        for i, (src, dst, to_lat, to_lon) in enumerate(plan)
    ]


def halo_place(lat, lat_count, grid, row_in, col_in, corner_in):
    above = (lat > 0).astype(F32)
    below = (lat < lat_count - 1).astype(F32)
    for side, (r, keep) in enumerate(((0, above), (ROWS + 1, below))):
        at = r * PITCH + 1
        for i in range(TALL // 2):
            part = row_in[side, i].astype(F32) * keep
            grid[2 * i, at : at + COLS, :] = part[:COLS]
            grid[2 * i + 1, at : at + COLS, :] = part[COLS:]
    for side, c in enumerate((0, COLS + 1)):
        for i in range(TALL):
            grid[i, pl.ds(PITCH + c, ROWS, stride=PITCH), :] = col_in[side, i].astype(F32)
    places = ((0, 0, above), (0, COLS + 1, above), (ROWS + 1, 0, below), (ROWS + 1, COLS + 1, below))
    for corner, (r, c, keep) in enumerate(places):
        cell = r * PITCH + c
        for i in range(TALL):
            grid[i, cell : cell + 1, :] = corner_in[corner, i : i + 1, :] * keep


OFFSETS = ((0, 0), (0, 1), (1, 0), (1, 1))


def positions(ref, length, low):
    found = {}
    for dr, dc in OFFSETS:
        for pr in range(2):
            for pc in range(2):
                found[2 * dr + pr, 2 * dc + pc] = ref[
                    low + 2 * pr + pc, pl.ds(dr * PITCH + dc, length), :
                ].astype(BF16)
    return found


def window(ref, start, length, low, high):
    return jnp.concatenate([ref[i, pl.ds(start, length), :] for i in range(low, high)], axis=1)


def keep_wide(ref, value):
    for i in range(4):
        ref[i, :OUTER, :] = value[:, i * COUT : (i + 1) * COUT]
        ref[i, OUTER:, :] = jnp.zeros((FLAT - OUTER, COUT), F32)


def patches(found, flipped):
    stacked = []
    for s in range(2):
        for t in range(2):
            pieces = []
            for ky in range(3):
                for kx in range(3):
                    at = (s - ky + 2, t - kx + 2) if flipped else (s + ky, t + kx)
                    pieces.append(found[at])
            stacked.append(jnp.concatenate(pieces, axis=1))
    return jnp.concatenate(stacked, axis=0)


def beside(array, rows):
    return jnp.concatenate([array[i * rows : (i + 1) * rows] for i in range(4)], axis=1)


def inner_mask(lanes):
    cell = lax.broadcasted_iota(jnp.int32, (INNER, lanes), 0)
    return lax.rem(cell, PITCH) < COLS


def merge_slots(even, odd):
    return jnp.concatenate([even, odd], axis=1).reshape(CIN, COUT).astype(BF16)


def forward_part(lat, lat_count, grid, up_kernel, bias, act):
    windows = [window(grid, dr * PITCH + dc, OUTER, 0, 2).astype(BF16) for dr, dc in OFFSETS]
    forward = jnp.concatenate(
        [
            jnp.concatenate(
                [
                    up_kernel[(2 * (1 - dr) + pr) * 4 + 2 * (1 - dc) + pc]
                    for pr in range(2)
                    for pc in range(2)
                ],
                axis=1,
            )
            for dr, dc in OFFSETS
        ],
        axis=0,
    )
    raw = jnp.dot(jnp.concatenate(windows, axis=1), forward, preferred_element_type=F32)
    plain = (raw + jnp.concatenate([bias[...]] * 4, axis=1)).astype(BF16).astype(F32)
    sigmoid = jax.nn.sigmoid(plain)
    activated = (plain * sigmoid).astype(BF16).astype(F32)
    cell = lax.broadcasted_iota(jnp.int32, (OUTER, 4 * COUT), 0)
    lane = lax.broadcasted_iota(jnp.int32, (OUTER, 4 * COUT), 1)
    outside = ((cell < PITCH) & (lane < 2 * COUT) & (lat == 0)) | (
        (cell >= ROWS * PITCH) & (lane >= 2 * COUT) & (lat == lat_count - 1)
    )
    keep_wide(act, jnp.where(outside, 0.0, activated))
    return sigmoid * (1.0 + plain * (1.0 - sigmoid)), outside


def mix_part_sums(grid, act_patches, sums):
    cot_own = window(grid, PITCH + 1, INNER, 2, TALL)
    cot_own = jnp.where(inner_mask(4 * COUT), cot_own, 0.0).astype(BF16)
    cot_stacked = jnp.concatenate([cot_own[:, i * COUT : (i + 1) * COUT] for i in range(4)], axis=0)
    mix_sum = lax.dot_general(
        act_patches, cot_stacked, (((0,), (0,)), ((), ())), preferred_element_type=F32
    )
    empty = jnp.zeros((LON_ALL, 8, COUT), F32)
    for w in range(4):
        slots = [empty] * 4
        for slot in range(4):
            tap = slot * 4 + w
            if tap < 9:
                slots[slot] = mix_sum[tap * COUT : (tap + 1) * COUT].reshape(LON_ALL, 8, COUT)
        for i in range(2):
            sums[w // 2, MIX, w % 2, :, i * COUT : (i + 1) * COUT] = merge_slots(
                slots[2 * i], slots[2 * i + 1]
            )


def backward_part(grid, mix_kernel, slope, outside, pre_grad):
    backward = jnp.concatenate([mix_kernel[i] for i in range(9)], axis=1)
    act_grad = lax.dot_general(
        patches(positions(grid, OUTER, 2), True),
        backward,
        (((1,), (1,)), ((), ())),
        preferred_element_type=F32,
    )
    graded = (beside(act_grad, OUTER) * slope).astype(BF16).astype(F32)
    keep_wide(pre_grad, jnp.where(outside, 0.0, graded))


def grad_window(pre_grad, dr, dc):
    return window(pre_grad, dr * PITCH + dc, INNER, 0, 4).astype(BF16)


def up_part_sums(grid, pre_grad, dc, sums):
    in_own = window(grid, PITCH + 1, INNER, 0, 2)
    in_own = jnp.where(inner_mask(CIN), in_own, 0.0).astype(BF16)
    for dr in range(2):
        up_sum = lax.dot_general(
            in_own,
            grad_window(pre_grad, dr, dc),
            (((0,), (0,)), ((), ())),
            preferred_element_type=F32,
        ).astype(BF16)
        for pr in range(2):
            sums[dr, dc, pr] = up_sum[:, pr * SPAN : (pr + 1) * SPAN]


def section_part(act_patches, mix_kernel, staged, out_wide, section):
    flat_mix = mix_kernel[...].reshape(9 * COUT, COUT)
    staged[...] = jnp.dot(act_patches, flat_mix, preferred_element_type=F32)
    for s in range(2):
        for t in range(2):
            for r in range(ROWS):
                out_wide[pl.ds((2 * r + s) * 2 * COLS + t, COLS, stride=2), :] = staged[
                    pl.ds((2 * s + t) * INNER + r * PITCH, COLS), :
                ]
    section[...] = out_wide[...].astype(BF16)


def input_part(pre_grad, up_kernel, act, input_grad):
    back_up = jnp.concatenate(
        [
            up_kernel[(2 * dr + pr) * 4 + 2 * dc + pc]
            for dr, dc in OFFSETS
            for pr in range(2)
            for pc in range(2)
        ],
        axis=1,
    )
    grad_windows = jnp.concatenate([grad_window(pre_grad, dr, dc) for dr, dc in OFFSETS], axis=1)
    spread = lax.dot_general(
        grad_windows, back_up, (((1,), (1,)), ((), ())), preferred_element_type=F32
    )
    for i in range(2):
        act[i, :INNER, :] = spread[:, i * COUT : (i + 1) * COUT]
        for r in range(ROWS):
            input_grad[r * COLS : (r + 1) * COLS, i * COUT : (i + 1) * COUT] = act[
                i, pl.ds(r * PITCH, COLS), :
            ]


def reduce_partners(lat, lon, z_count, y_count):
    core, x_hi, z = lax.rem(lat, 2), lax.rem(lat // 2, 2), lat // 4
    y, x_lo = lax.rem(lon, y_count), lon // y_count
    return core, x_hi, z, y, x_lo


def fetch(src, dst, send, recv, to):
    copy = pltpu.make_async_remote_copy(
        src_ref=src, dst_ref=dst, send_sem=send, recv_sem=recv, device_id=to, device_id_type=MESH
    )
    copy.start()


def await_bytes(ref, sem):
    pltpu.make_async_copy(ref, ref, sem).wait()


def z_plan(z_count):
    return 3, z_count // 3


def section_kernel(
    lat_count,
    lon_count,
    scale,
    codes_hbm,
    exps_hbm,
    cot_hbm,
    up_hbm,
    bias_hbm,
    mix_hbm,
    section,
    input_grad,
    up_out,
    mix_out,
    codes,
    exps,
    cot,
    up_kernel,
    bias,
    mix_kernel,
    load_sem,
    grid,
    own,
    cot_wide,
    row_out,
    col_out,
    corner_out,
    row_in,
    col_in,
    corner_in,
    halo_send,
    halo_recv,
    act,
    pre_grad,
    staged,
    out_wide,
    sums,
    core_in,
    x_out,
    xa_in,
    xb_in,
    y_out,
    y_in,
    mix_y_in,
    mix_out_x,
    mix_x_in,
    far,
    near,
    final,
    core_sem,
    x_sem,
    y_sem,
    far_sem,
    near_sem,
    final_sem,
    mix_sem,
):
    z_count, y_count = lat_count // 4, lon_count // 2
    far_count, near_count = z_plan(z_count)
    lat, lon = lax.axis_index("lat"), lax.axis_index("lon")
    core, x_hi, z, y, x_lo = reduce_partners(lat, lon, z_count, y_count)
    x = 2 * x_hi + x_lo

    def at_x(step):
        other = lax.rem(x + step + 4, 4)
        return 4 * z + 2 * (other // 2) + core, lax.rem(other, 2) * y_count + y

    def at_y(step):
        return lat, x_lo * y_count + lax.rem(y + step, y_count)

    def at_z(step, row):
        return 4 * lax.rem(z + step + z_count, z_count) + 2 * row + core, lon

    partner = (lat + 1 - 2 * core, lon)
    far_steps = [near_count * i for i in range(1, far_count)]
    near_steps = [i if 2 * i <= near_count else i - near_count for i in range(1, near_count)]

    loads = [
        pltpu.make_async_copy(src, dst, load_sem.at[i])
        for i, (src, dst) in enumerate(
            (
                (exps_hbm, exps),
                (codes_hbm, codes),
                (cot_hbm, cot),
                (up_hbm, up_kernel),
                (mix_hbm, mix_kernel),
                (bias_hbm, bias),
            )
        )
    ]
    barrier = pltpu.get_barrier_semaphore()
    up, down, left, right = partners = halo_partners(lat, lon, lat_count, lon_count)
    greeted = [(a, b) for a in (up, down) for b in (left, lon, right)] + [(lat, left), (lat, right)]
    greeted += [partner, at_x(1), at_x(2), at_x(-1)]
    greeted += [at_y(step) for step in range(1, y_count)]
    far_all = sorted({step % z_count for base in far_steps for step in (base, -base)})
    near_all = sorted({step % z_count for base in near_steps for step in (base, -base)})
    greeted += [at_z(step, x_hi) for step in far_all + near_all]
    greeted += [at_z(step, 1 - x_hi) for step in [0] + near_all]
    for to in greeted:
        pl.semaphore_signal(barrier, inc=1, device_id=to, device_id_type=MESH)
    for load in loads:
        load.start()
    for load in loads[:3]:
        load.wait()
    halo_fill(codes, exps, cot, grid, own, cot_wide, row_out, col_out, corner_out)
    pl.semaphore_wait(barrier, len(greeted))
    halo = halo_copies(
        partners, lat, lon, row_out, col_out, corner_out, row_in, col_in, corner_in, halo_send, halo_recv
    )
    for copy in reversed(halo):
        copy.start()
    for load in loads[3:]:
        load.wait()
    for copy in halo:
        copy.wait_recv()
    halo_place(lat, lat_count, grid, row_in, col_in, corner_in)

    def core_start(part):
        fetch(sums.at[1 - core, part], core_in.at[part], core_sem.at[0, part], core_sem.at[1, part], partner)

    half = y_count // 2
    y_steps = sorted(range(1, y_count), key=lambda step: -min(step, y_count - step))

    def core_end(part):
        await_bytes(core_in.at[part], core_sem.at[1, part])
        merged = sums[core, part].astype(F32) + core_in[part].astype(F32)
        x_out[part] = merged.astype(BF16).reshape(x_out.shape[1:])

    def mix_first():
        core_end(MIX)
        for step in y_steps:
            fetch(
                x_out.at[MIX, :, lax.rem(y + step, y_count)],
                mix_y_in.at[step - 1],
                mix_sem.at[0],
                mix_sem.at[1],
                at_y(step),
            )

    def mix_second():
        await_bytes(mix_y_in, mix_sem.at[1])
        total = x_out[MIX, :, y].astype(F32)
        for step in range(y_count - 1):
            total = total + mix_y_in[step].astype(F32)
        mix_out_x[...] = total.astype(BF16)
        for step in (2, 1, 3):
            fetch(
                mix_out_x.at[lax.rem(x + step, 4)],
                mix_x_in.at[step - 1],
                mix_sem.at[2],
                mix_sem.at[3],
                at_x(step),
            )

    def mix_third():
        await_bytes(mix_x_in, mix_sem.at[3])
        total = mix_out_x[x].astype(F32)
        for step in range(3):
            total = total + mix_x_in[step].astype(F32)
        far_send(MIX, total)

    def x_first(part):
        core_end(part)
        across = lax.rem(x + 2, 4)
        for side, step in ((0, 1), (1, -1)):
            fetch(
                x_out.at[part, across, pl.ds(side * half, half)],
                xa_in.at[part, side],
                x_sem.at[0, part, side],
                x_sem.at[1, part, side],
                at_x(step),
            )

    def x_second(part):
        for side, step in ((0, 1), (1, -1)):
            await_bytes(xa_in.at[part, side], x_sem.at[1, part, side])
            beside_x = lax.rem(x + step + 4, 4)
            rows = pl.ds(side * half, half)
            merged = x_out[part, beside_x, rows].astype(F32) + xa_in[part, side].astype(F32)
            x_out[part, beside_x, rows] = merged.astype(BF16)
            fetch(
                x_out.at[part, beside_x],
                xb_in.at[part, side],
                x_sem.at[2, part, side],
                x_sem.at[3, part, side],
                at_x(step),
            )

    def y_start(part):
        for side in range(2):
            await_bytes(xb_in.at[part, side], x_sem.at[3, part, side])
        merged = x_out[part, x].astype(F32) + xb_in[part, 0].astype(F32) + xb_in[part, 1].astype(F32)
        y_out[part] = merged.astype(BF16)
        for step in y_steps:
            fetch(
                y_out.at[part, lax.rem(y + step, y_count)],
                y_in.at[part, step - 1],
                y_sem.at[0, part],
                y_sem.at[1, part],
                at_y(step),
            )

    far_at, near_at = z // near_count, lax.rem(z, near_count)

    def far_start(part):
        await_bytes(y_in.at[part], y_sem.at[1, part])
        total = y_out[part, y].astype(F32)
        for step in range(y_count - 1):
            total = total + y_in[part, step].astype(F32)
        far_send(part, total)

    def far_send(part, total):
        far[part, far_at] = total.astype(BF16)
        for step in far_steps:
            fetch(far.at[part, far_at], far.at[part, far_at], far_sem.at[0, part], far_sem.at[1, part], at_z(step, x_hi))

    def near_start(part):
        await_bytes(far.at[part, pl.ds(0, far_count - 1)], far_sem.at[1, part])
        total = far[part, 0].astype(F32)
        for i in range(1, far_count):
            total = total + far[part, i].astype(F32)
        slot = 2 * near_at + x_hi
        near[part, slot] = total.astype(BF16)
        for to in [at_z(step, 1 - x_hi) for step in [0] + near_steps] + [at_z(step, x_hi) for step in near_steps]:
            fetch(near.at[part, slot], near.at[part, slot], near_sem.at[0, part], near_sem.at[1, part], to)

    def final_start(part):
        await_bytes(near.at[part, pl.ds(0, 2 * near_count - 1)], near_sem.at[1, part])
        for row in range(2):
            total = near[part, row].astype(F32)
            for i in range(1, near_count):
                total = total + near[part, 2 * i + row].astype(F32)
            final[part, core, row] = total * scale
        fetch(
            final.at[part, core], final.at[part, core], final_sem.at[0, part], final_sem.at[1, part], partner
        )

    def finish(part):
        await_bytes(final.at[part, 0], final_sem.at[1, part])
        for w in range(4):
            for i in range(2):
                piece = final[part, w // 2, w % 2, :, i * COUT : (i + 1) * COUT]
                if part != MIX:
                    up_out[w, 2 * part + i] = piece
                    continue
                for slot in range(2):
                    tap = (2 * i + slot) * 4 + w
                    if tap < 9:
                        mix_out[tap] = piece[slot * 8 : slot * 8 + 8]

    slope, outside = forward_part(lat, lat_count, grid, up_kernel, bias, act)
    act_patches = patches(positions(act, INNER, 0), False)
    mix_part_sums(grid, act_patches, sums)
    core_start(MIX)
    backward_part(grid, mix_kernel, slope, outside, pre_grad)
    up_part_sums(grid, pre_grad, 0, sums)
    core_start(0)
    mix_first()
    up_part_sums(grid, pre_grad, 1, sums)
    core_start(1)
    x_first(0)
    x_first(1)
    for part in UP:
        x_second(part)
    for part in UP:
        y_start(part)
    mix_second()
    section_part(act_patches, mix_kernel, staged, out_wide, section)
    mix_third()
    for part in UP:
        far_start(part)
    input_part(pre_grad, up_kernel, act, input_grad)
    for stage in (near_start, final_start):
        for part in ORDER:
            stage(part)
    for copy in halo:
        copy.wait_send()
    await_bytes(mix_y_in, mix_sem.at[0])
    await_bytes(mix_x_in, mix_sem.at[2])
    for part in UP:
        for side in range(2):
            await_bytes(xa_in.at[part, side], x_sem.at[0, part, side])
            await_bytes(xb_in.at[part, side], x_sem.at[2, part, side])
        await_bytes(y_in.at[part], y_sem.at[0, part])
    for part in range(PARTS):
        await_bytes(core_in.at[part], core_sem.at[0, part])
        await_bytes(far.at[part, pl.ds(0, far_count - 1)], far_sem.at[0, part])
        await_bytes(near.at[part, pl.ds(0, 2 * near_count - 1)], near_sem.at[0, part])
        await_bytes(final.at[part, 0], final_sem.at[0, part])
    for part in ORDER:
        finish(part)


def write_kernel(*refs):
    copies = [pltpu.make_async_copy(refs[i], refs[4 + i], refs[8].at[i]) for i in range(4)]
    for copy in copies:
        copy.start()
    for copy in copies:
        copy.wait()


def shards(elem_codes, block_exps, up_kernel, up_bias, mix_kernel, cotangent):
    lat_count, lon_count = lax.axis_size("lat"), lax.axis_size("lon")
    y_count, z_count = lon_count // 2, lat_count // 4
    far_count, near_count = z_plan(z_count)
    out_cells = 4 * CELLS * lat_count * lon_count
    operands = (
        elem_codes.reshape(CELLS, CIN),
        block_exps.transpose(1, 2, 0).reshape(COLS * CIN // BLOCK, ROWS),
        cotangent.reshape(4 * CELLS, COUT),
        up_kernel.reshape(16, CIN, COUT),
        up_bias.reshape(1, COUT),
        mix_kernel.reshape(9, COUT, COUT),
    )
    dma = pltpu.SemaphoreType.DMA
    results = pl.pallas_call(
        functools.partial(section_kernel, lat_count, lon_count, 1.0 / math.sqrt(out_cells)),
        out_shape=(
            pltpu.VMEM((4 * CELLS, COUT), BF16),
            pltpu.VMEM((CELLS, CIN), F32),
            pltpu.VMEM((4, 4, LON_ALL, COUT), F32),
            pltpu.VMEM((9, 8, COUT), F32),
        ),
        in_specs=[pl.BlockSpec(memory_space=pltpu.HBM)] * 6,
        out_specs=[pl.BlockSpec(memory_space=pltpu.VMEM)] * 4,
        scratch_shapes=[pltpu.VMEM(operand.shape, operand.dtype) for operand in operands]
        + [
            dma((6,)),
            pltpu.VMEM((TALL, FLAT, COUT), F32),
            pltpu.VMEM((TALL, CELLS, COUT), F32),
            pltpu.VMEM((4 * CELLS, COUT), F32),
            pltpu.VMEM((2, TALL // 2, 2 * COLS, COUT), BF16),
            pltpu.VMEM((2, TALL, ROWS, COUT), BF16),
            pltpu.VMEM((4, 8, COUT), F32),
            pltpu.VMEM((2, TALL // 2, 2 * COLS, COUT), BF16),
            pltpu.VMEM((2, TALL, ROWS, COUT), BF16),
            pltpu.VMEM((4, 8, COUT), F32),
            dma((8,)),
            dma((8,)),
            pltpu.VMEM((4, FLAT, COUT), F32),
            pltpu.VMEM((4, FLAT, COUT), F32),
            pltpu.VMEM((4 * INNER, COUT), F32),
            pltpu.VMEM((4 * CELLS, COUT), F32),
            pltpu.VMEM((2, PARTS, 2, CIN, SPAN), BF16),
            pltpu.VMEM((PARTS, 2, CIN, SPAN), BF16),
            pltpu.VMEM((PARTS, 4, y_count, 16, SPAN), BF16),
            pltpu.VMEM((2, 2, y_count // 2, 16, SPAN), BF16),
            pltpu.VMEM((2, 2, y_count, 16, SPAN), BF16),
            pltpu.VMEM((2, y_count, 16, SPAN), BF16),
            pltpu.VMEM((2, y_count - 1, 16, SPAN), BF16),
            pltpu.VMEM((y_count - 1, 4, 16, SPAN), BF16),
            pltpu.VMEM((4, 16, SPAN), BF16),
            pltpu.VMEM((3, 16, SPAN), BF16),
            pltpu.VMEM((PARTS, far_count, 16, SPAN), BF16),
            pltpu.VMEM((PARTS, 2 * near_count, 16, SPAN), BF16),
            pltpu.VMEM((PARTS, 2, 2, 16, SPAN), F32),
            dma((2, PARTS)),
            dma((4, 2, 2)),
            dma((2, 2)),
            dma((2, PARTS)),
            dma((2, PARTS)),
            dma((2, PARTS)),
            dma((4,)),
        ],
        compiler_params=pltpu.CompilerParams(
            collective_id=0, has_side_effects=True, vmem_limit_bytes=40 * 2**20
        ),
    )(*[pltpu.with_memory_space_constraint(operand, pltpu.HBM) for operand in operands])
    section, input_grad, up_part, mix_part = pl.pallas_call(
        write_kernel,
        out_shape=tuple(jax.ShapeDtypeStruct(result.shape, result.dtype) for result in results),
        in_specs=[pl.BlockSpec(memory_space=pltpu.VMEM)] * 4,
        out_specs=[pl.BlockSpec(memory_space=pltpu.HBM)] * 4,
        scratch_shapes=[dma((4,))],
        compiler_params=pltpu.CompilerParams(vmem_limit_bytes=8 * 2**20),
    )(*results)
    return (
        section.reshape(2 * ROWS, 2 * COLS, COUT),
        input_grad.reshape(ROWS, COLS, CIN),
        up_part,
        mix_part.reshape(3, 3, 8, COUT),
    )


def solution(mesh):
    placed = (P("lat", "lon", None), P("lat", "lon", None), P(), P(), P(), P("lat", "lon", None))
    return jax.shard_map(
        shards,
        mesh=mesh,
        in_specs=placed,
        out_specs=(
            P("lat", "lon", None),
            P("lat", "lon", None),
            P(None, None, "lon", None),
            P(None, None, "lon", None),
        ),
        check_vma=False,
    )
```

```python
import functools
import math

import jax
import jax.numpy as jnp
from jax import lax
from jax.experimental import pallas as pl
from jax.experimental.pallas import tpu as pltpu
from jax.sharding import PartitionSpec as P

CIN = 256
COUT = 128
BLOCK = 32
ROWS = 16
COLS = 8
PITCH = 10
CELLS = ROWS * COLS
TALL = CIN // COUT + 4
FLAT = 192
OUTER = 176
INNER = ROWS * PITCH
PARTS = 3
SPAN = 2 * COUT
MIX = 2
MIX_TAPS = (5, 4)
MIX_ROWS = 48
UP = (0, 1)
LON_ALL = 16
MESH = pl.DeviceIdType.MESH
F32 = jnp.float32
BF16 = jnp.bfloat16


def power_bits(value, bits):
    total = jnp.where(value & 1 != 0, 2.0, 1.0)
    for bit in range(1, bits):
        total = total * jnp.where(value & (1 << bit) != 0, float(1 << (1 << bit)), 1.0)
    return total


def decode(codes, factor):
    sign = jnp.where(codes >= 128, -(2.0**-9), 2.0**-9)
    fraction = (8 + (codes & 7)).astype(F32) * 0.125
    return sign * power_bits((codes >> 3) & 15, 4) * fraction * factor


def block_factors(exps, own):
    factor = power_bits(exps + 2, 2).astype(BF16)
    count = exps.shape[0]
    lane = lax.broadcasted_iota(jnp.int32, (count, COLS * CIN), 1)
    row = lax.broadcasted_iota(jnp.int32, (count, COLS * CIN), 0)
    spread = jnp.where(lane // BLOCK == row, 1.0, 0.0).astype(BF16)
    wide = lax.dot_general(factor, spread, (((0,), (0,)), ((), ())), preferred_element_type=F32)
    for c in range(COLS):
        for i in range(CIN // COUT):
            at = c * CIN + i * COUT
            own[i, pl.ds(c, ROWS, stride=COLS), :] = wide[:, at : at + COUT]


def halo_partners(lat, lon, lat_count, lon_count):
    up, down = lax.rem(lat + lat_count - 1, lat_count), lax.rem(lat + 1, lat_count)
    left, right = lax.rem(lon + lon_count - 1, lon_count), lax.rem(lon + 1, lon_count)
    return up, down, left, right


def halo_fill(codes, exps, cot, grid, own, cot_wide, row_out, col_out, corner_out):
    block_factors(exps[...], own)
    for i in range(CIN // COUT):
        own[i] = decode(codes[:, i * COUT : (i + 1) * COUT], own[i])
    cot_wide[...] = cot[...].astype(F32)
    for r in range(ROWS):
        for s in range(2):
            for t in range(2):
                own[2 + 2 * s + t, r * COLS : (r + 1) * COLS, :] = cot_wide[
                    pl.ds((2 * r + s) * 2 * COLS + t, COLS, stride=2), :
                ]
    for side, r in enumerate((ROWS - 1, 0)):
        for i in range(TALL // 2):
            row_out[side, i] = jnp.concatenate(
                [own[j, r * COLS : (r + 1) * COLS, :] for j in (2 * i, 2 * i + 1)], axis=0
            ).astype(BF16)
    for side, c in enumerate((COLS - 1, 0)):
        for i in range(TALL):
            col_out[side, i] = own[i, pl.ds(c, ROWS, stride=COLS), :].astype(BF16)
    for corner, (r, c) in enumerate(((ROWS - 1, COLS - 1), (ROWS - 1, 0), (0, COLS - 1), (0, 0))):
        cell = r * COLS + c
        corner_out[corner] = jnp.zeros((8, COUT), F32)
        for i in range(TALL):
            corner_out[corner, i : i + 1, :] = own[i, cell : cell + 1, :]
    for r in range(ROWS):
        at = (r + 1) * PITCH + 1
        for i in range(TALL):
            grid[i, at : at + COLS, :] = own[i, r * COLS : (r + 1) * COLS, :]
    tail = (ROWS + 2) * PITCH
    for i in range(TALL):
        grid[i, tail:FLAT, :] = jnp.zeros((FLAT - tail, COUT), F32)


def halo_copies(partners, lat, lon, row_out, col_out, corner_out, row_in, col_in, corner_in, send, recv):
    up, down, left, right = partners
    plan = [
        (row_out.at[0], row_in.at[0], down, lon),
        (row_out.at[1], row_in.at[1], up, lon),
        (col_out.at[0], col_in.at[0], lat, right),
        (col_out.at[1], col_in.at[1], lat, left),
        (corner_out.at[0], corner_in.at[0], down, right),
        (corner_out.at[1], corner_in.at[1], down, left),
        (corner_out.at[2], corner_in.at[2], up, right),
        (corner_out.at[3], corner_in.at[3], up, left),
    ]
    return [
        pltpu.make_async_remote_copy(
            src_ref=src,
            dst_ref=dst,
            send_sem=send.at[i],
            recv_sem=recv.at[i],
            device_id=(to_lat, to_lon),
            device_id_type=MESH,
        )
        for i, (src, dst, to_lat, to_lon) in enumerate(plan)
    ]


def halo_place(lat, lat_count, grid, row_in, col_in, corner_in):
    above = (lat > 0).astype(F32)
    below = (lat < lat_count - 1).astype(F32)
    for side, (r, keep) in enumerate(((0, above), (ROWS + 1, below))):
        at = r * PITCH + 1
        for i in range(TALL // 2):
            part = row_in[side, i].astype(F32) * keep
            grid[2 * i, at : at + COLS, :] = part[:COLS]
            grid[2 * i + 1, at : at + COLS, :] = part[COLS:]
    for side, c in enumerate((0, COLS + 1)):
        for i in range(TALL):
            grid[i, pl.ds(PITCH + c, ROWS, stride=PITCH), :] = col_in[side, i].astype(F32)
    places = ((0, 0, above), (0, COLS + 1, above), (ROWS + 1, 0, below), (ROWS + 1, COLS + 1, below))
    for corner, (r, c, keep) in enumerate(places):
        cell = r * PITCH + c
        for i in range(TALL):
            grid[i, cell : cell + 1, :] = corner_in[corner, i : i + 1, :] * keep


OFFSETS = ((0, 0), (0, 1), (1, 0), (1, 1))


def positions(ref, length, low):
    found = {}
    for dr, dc in OFFSETS:
        for pr in range(2):
            for pc in range(2):
                found[2 * dr + pr, 2 * dc + pc] = ref[
                    low + 2 * pr + pc, pl.ds(dr * PITCH + dc, length), :
                ].astype(BF16)
    return found


def window(ref, start, length, low, high):
    return jnp.concatenate([ref[i, pl.ds(start, length), :] for i in range(low, high)], axis=1)


def keep_wide(ref, value):
    for i in range(4):
        ref[i, :OUTER, :] = value[:, i * COUT : (i + 1) * COUT]
        ref[i, OUTER:, :] = jnp.zeros((FLAT - OUTER, COUT), F32)


def patches(found, flipped):
    stacked = []
    for s in range(2):
        for t in range(2):
            pieces = []
            for ky in range(3):
                for kx in range(3):
                    at = (s - ky + 2, t - kx + 2) if flipped else (s + ky, t + kx)
                    pieces.append(found[at])
            stacked.append(jnp.concatenate(pieces, axis=1))
    return jnp.concatenate(stacked, axis=0)


def beside(array, rows):
    return jnp.concatenate([array[i * rows : (i + 1) * rows] for i in range(4)], axis=1)


def inner_mask(lanes):
    cell = lax.broadcasted_iota(jnp.int32, (INNER, lanes), 0)
    return lax.rem(cell, PITCH) < COLS


def forward_part(lat, lat_count, grid, up_kernel, bias, act):
    windows = [window(grid, dr * PITCH + dc, OUTER, 0, 2).astype(BF16) for dr, dc in OFFSETS]
    forward = jnp.concatenate(
        [
            jnp.concatenate(
                [
                    up_kernel[(2 * (1 - dr) + pr) * 4 + 2 * (1 - dc) + pc]
                    for pr in range(2)
                    for pc in range(2)
                ],
                axis=1,
            )
            for dr, dc in OFFSETS
        ],
        axis=0,
    )
    raw = jnp.dot(jnp.concatenate(windows, axis=1), forward, preferred_element_type=F32)
    plain = (raw + jnp.concatenate([bias[...]] * 4, axis=1)).astype(BF16).astype(F32)
    sigmoid = jax.nn.sigmoid(plain)
    activated = (plain * sigmoid).astype(BF16).astype(F32)
    cell = lax.broadcasted_iota(jnp.int32, (OUTER, 4 * COUT), 0)
    lane = lax.broadcasted_iota(jnp.int32, (OUTER, 4 * COUT), 1)
    outside = ((cell < PITCH) & (lane < 2 * COUT) & (lat == 0)) | (
        (cell >= ROWS * PITCH) & (lane >= 2 * COUT) & (lat == lat_count - 1)
    )
    keep_wide(act, jnp.where(outside, 0.0, activated))
    return sigmoid * (1.0 + plain * (1.0 - sigmoid)), outside


def mix_part_sums(grid, act_patches, mix_sums):
    cot_own = window(grid, PITCH + 1, INNER, 2, TALL)
    cot_own = jnp.where(inner_mask(4 * COUT), cot_own, 0.0).astype(BF16)
    cot_stacked = jnp.concatenate([cot_own[:, i * COUT : (i + 1) * COUT] for i in range(4)], axis=0)
    mix_sum = lax.dot_general(
        act_patches, cot_stacked, (((0,), (0,)), ((), ())), preferred_element_type=F32
    )
    empty = jnp.zeros((LON_ALL, 8, COUT), F32)
    tap = 0
    for core, count in enumerate(MIX_TAPS):
        rows = [empty] * (MIX_ROWS // 8)
        for i in range(count):
            rows[i] = mix_sum[tap * COUT : (tap + 1) * COUT].reshape(LON_ALL, 8, COUT)
            tap += 1
        mix_sums[core] = jnp.concatenate(rows, axis=1).astype(BF16).reshape(mix_sums.shape[1:])


def backward_part(grid, mix_kernel, slope, outside, pre_grad):
    backward = jnp.concatenate([mix_kernel[i] for i in range(9)], axis=1)
    act_grad = lax.dot_general(
        patches(positions(grid, OUTER, 2), True),
        backward,
        (((1,), (1,)), ((), ())),
        preferred_element_type=F32,
    )
    graded = (beside(act_grad, OUTER) * slope).astype(BF16).astype(F32)
    keep_wide(pre_grad, jnp.where(outside, 0.0, graded))


def grad_window(pre_grad, dr, dc):
    return window(pre_grad, dr * PITCH + dc, INNER, 0, 4).astype(BF16)


def up_part_sums(grid, pre_grad, dc, sums):
    in_own = window(grid, PITCH + 1, INNER, 0, 2)
    in_own = jnp.where(inner_mask(CIN), in_own, 0.0).astype(BF16)
    for dr in range(2):
        up_sum = lax.dot_general(
            in_own,
            grad_window(pre_grad, dr, dc),
            (((0,), (0,)), ((), ())),
            preferred_element_type=F32,
        ).astype(BF16)
        for pr in range(2):
            sums[dr, dc, pr] = up_sum[:, pr * SPAN : (pr + 1) * SPAN]


def section_part(act_patches, mix_kernel, staged, out_wide, section):
    flat_mix = mix_kernel[...].reshape(9 * COUT, COUT)
    staged[...] = jnp.dot(act_patches, flat_mix, preferred_element_type=F32)
    for s in range(2):
        for t in range(2):
            for r in range(ROWS):
                out_wide[pl.ds((2 * r + s) * 2 * COLS + t, COLS, stride=2), :] = staged[
                    pl.ds((2 * s + t) * INNER + r * PITCH, COLS), :
                ]
    section[...] = out_wide[...].astype(BF16)


def input_part(pre_grad, up_kernel, act, input_grad):
    back_up = jnp.concatenate(
        [
            up_kernel[(2 * dr + pr) * 4 + 2 * dc + pc]
            for dr, dc in OFFSETS
            for pr in range(2)
            for pc in range(2)
        ],
        axis=1,
    )
    grad_windows = jnp.concatenate([grad_window(pre_grad, dr, dc) for dr, dc in OFFSETS], axis=1)
    spread = lax.dot_general(
        grad_windows, back_up, (((1,), (1,)), ((), ())), preferred_element_type=F32
    )
    for i in range(2):
        act[i, :INNER, :] = spread[:, i * COUT : (i + 1) * COUT]
        for r in range(ROWS):
            input_grad[r * COLS : (r + 1) * COLS, i * COUT : (i + 1) * COUT] = act[
                i, pl.ds(r * PITCH, COLS), :
            ]


def reduce_partners(lat, lon, z_count, y_count):
    core, x_hi, z = lax.rem(lat, 2), lax.rem(lat // 2, 2), lat // 4
    y, x_lo = lax.rem(lon, y_count), lon // y_count
    return core, x_hi, z, y, x_lo


def fetch(src, dst, send, recv, to):
    copy = pltpu.make_async_remote_copy(
        src_ref=src, dst_ref=dst, send_sem=send, recv_sem=recv, device_id=to, device_id_type=MESH
    )
    copy.start()


def await_bytes(ref, sem):
    pltpu.make_async_copy(ref, ref, sem).wait()


def z_plan(z_count):
    return 3, z_count // 3


def section_kernel(
    lat_count,
    lon_count,
    scale,
    codes_hbm,
    exps_hbm,
    cot_hbm,
    up_hbm,
    bias_hbm,
    mix_hbm,
    section,
    input_grad,
    up_out,
    mix_out,
    codes,
    exps,
    cot,
    up_kernel,
    bias,
    mix_kernel,
    load_sem,
    grid,
    own,
    cot_wide,
    row_out,
    col_out,
    corner_out,
    row_in,
    col_in,
    corner_in,
    halo_send,
    halo_recv,
    act,
    pre_grad,
    staged,
    out_wide,
    sums,
    core_in,
    x_out,
    xa_in,
    xb_in,
    y_out,
    y_in,
    mix_sums,
    mix_core_in,
    mix_y_out,
    mix_y_in,
    mix_x_out,
    mix_x_in,
    mix_far,
    mix_near,
    mix_final,
    far,
    near,
    final,
    core_sem,
    x_sem,
    y_sem,
    far_sem,
    near_sem,
    final_sem,
    mix_sem,
):
    z_count, y_count = lat_count // 4, lon_count // 2
    far_count, near_count = z_plan(z_count)
    lat, lon = lax.axis_index("lat"), lax.axis_index("lon")
    core, x_hi, z, y, x_lo = reduce_partners(lat, lon, z_count, y_count)
    x = 2 * x_hi + x_lo

    def at_x(step):
        other = lax.rem(x + step + 4, 4)
        return 4 * z + 2 * (other // 2) + core, lax.rem(other, 2) * y_count + y

    def at_y(step):
        return lat, x_lo * y_count + lax.rem(y + step, y_count)

    def at_z(step, row):
        return 4 * lax.rem(z + step + z_count, z_count) + 2 * row + core, lon

    partner = (lat + 1 - 2 * core, lon)
    far_steps = [near_count * i for i in range(1, far_count)]
    near_steps = [i if 2 * i <= near_count else i - near_count for i in range(1, near_count)]

    loads = [
        pltpu.make_async_copy(src, dst, load_sem.at[i])
        for i, (src, dst) in enumerate(
            (
                (exps_hbm, exps),
                (codes_hbm, codes),
                (cot_hbm, cot),
                (up_hbm, up_kernel),
                (mix_hbm, mix_kernel),
                (bias_hbm, bias),
            )
        )
    ]
    barrier = pltpu.get_barrier_semaphore()
    up, down, left, right = partners = halo_partners(lat, lon, lat_count, lon_count)
    greeted = [(a, b) for a in (up, down) for b in (left, lon, right)] + [(lat, left), (lat, right)]
    greeted += [partner, at_x(1), at_x(2), at_x(-1)]
    greeted += [at_y(step) for step in range(1, y_count)]
    far_all = sorted({step % z_count for base in far_steps for step in (base, -base)})
    near_all = sorted({step % z_count for base in near_steps for step in (base, -base)})
    greeted += [at_z(step, x_hi) for step in far_all + near_all]
    greeted += [at_z(step, 1 - x_hi) for step in [0] + near_all]
    for to in greeted:
        pl.semaphore_signal(barrier, inc=1, device_id=to, device_id_type=MESH)
    for load in loads:
        load.start()
    for load in loads[:3]:
        load.wait()
    halo_fill(codes, exps, cot, grid, own, cot_wide, row_out, col_out, corner_out)
    pl.semaphore_wait(barrier, len(greeted))
    halo = halo_copies(
        partners, lat, lon, row_out, col_out, corner_out, row_in, col_in, corner_in, halo_send, halo_recv
    )
    for copy in reversed(halo):
        copy.start()
    for load in loads[3:]:
        load.wait()
    for copy in halo:
        copy.wait_recv()
    halo_place(lat, lat_count, grid, row_in, col_in, corner_in)

    def core_start(part):
        fetch(sums.at[1 - core, part], core_in.at[part], core_sem.at[0, part], core_sem.at[1, part], partner)

    half = y_count // 2
    y_steps = sorted(range(1, y_count), key=lambda step: -min(step, y_count - step))

    def core_end(part):
        await_bytes(core_in.at[part], core_sem.at[1, part])
        merged = sums[core, part].astype(F32) + core_in[part].astype(F32)
        x_out[part] = merged.astype(BF16).reshape(x_out.shape[1:])

    def mix_first():
        await_bytes(mix_core_in, core_sem.at[1, MIX])
        mix_y_out[...] = (mix_sums[core].astype(F32) + mix_core_in[...].astype(F32)).astype(BF16)
        for step in y_steps:
            fetch(
                mix_y_out.at[:, lax.rem(y + step, y_count)],
                mix_y_in.at[step - 1],
                mix_sem.at[0],
                mix_sem.at[1],
                at_y(step),
            )

    def mix_second():
        await_bytes(mix_y_in, mix_sem.at[1])
        total = mix_y_out[:, y].astype(F32)
        for step in range(y_count - 1):
            total = total + mix_y_in[step].astype(F32)
        mix_x_out[...] = total.astype(BF16)
        for step in (2, 1, 3):
            fetch(
                mix_x_out.at[lax.rem(x + step, 2)], mix_x_in.at[x], mix_sem.at[2], mix_sem.at[3], at_x(step)
            )
        mix_x_in[x] = mix_x_out[x_lo]

    def summed(ref, count):
        total = ref[0].astype(F32)
        for i in range(1, count):
            total = total + ref[i].astype(F32)
        return total

    def mix_third():
        await_bytes(mix_x_in.at[pl.ds(0, 3)], mix_sem.at[3])
        mix_far[far_at] = summed(mix_x_in, 4).astype(BF16)
        for step in far_steps:
            fetch(mix_far.at[far_at], mix_far.at[far_at], far_sem.at[0, MIX], far_sem.at[1, MIX], at_z(step, x_hi))

    def mix_fourth():
        await_bytes(mix_far.at[pl.ds(0, far_count - 1)], far_sem.at[1, MIX])
        mix_near[near_at] = summed(mix_far, far_count).astype(BF16)
        for step in near_steps:
            fetch(
                mix_near.at[near_at], mix_near.at[near_at], near_sem.at[0, MIX], near_sem.at[1, MIX], at_z(step, x_hi)
            )

    def mix_fifth():
        await_bytes(mix_near.at[pl.ds(0, near_count - 1)], near_sem.at[1, MIX])
        mix_final[core] = summed(mix_near, near_count) * scale
        fetch(mix_final.at[core], mix_final.at[core], final_sem.at[0, MIX], final_sem.at[1, MIX], partner)

    def mix_finish():
        await_bytes(mix_final.at[0], final_sem.at[1, MIX])
        tap = 0
        for owner, count in enumerate(MIX_TAPS):
            for i in range(count):
                mix_out[tap] = mix_final[owner, i * 8 : i * 8 + 8, :]
                tap += 1

    def x_first(part):
        core_end(part)
        across = lax.rem(x + 2, 4)
        for side, step in ((0, 1), (1, -1)):
            fetch(
                x_out.at[part, across, pl.ds(side * half, half)],
                xa_in.at[part, side],
                x_sem.at[0, part, side],
                x_sem.at[1, part, side],
                at_x(step),
            )

    def x_second(part):
        for side, step in ((0, 1), (1, -1)):
            await_bytes(xa_in.at[part, side], x_sem.at[1, part, side])
            beside_x = lax.rem(x + step + 4, 4)
            rows = pl.ds(side * half, half)
            merged = x_out[part, beside_x, rows].astype(F32) + xa_in[part, side].astype(F32)
            x_out[part, beside_x, rows] = merged.astype(BF16)
            fetch(
                x_out.at[part, beside_x],
                xb_in.at[part, side],
                x_sem.at[2, part, side],
                x_sem.at[3, part, side],
                at_x(step),
            )

    def y_start(part):
        for side in range(2):
            await_bytes(xb_in.at[part, side], x_sem.at[3, part, side])
        merged = x_out[part, x].astype(F32) + xb_in[part, 0].astype(F32) + xb_in[part, 1].astype(F32)
        y_out[part] = merged.astype(BF16)
        for step in y_steps:
            fetch(
                y_out.at[part, lax.rem(y + step, y_count)],
                y_in.at[part, step - 1],
                y_sem.at[0, part],
                y_sem.at[1, part],
                at_y(step),
            )

    far_at, near_at = z // near_count, lax.rem(z, near_count)

    def far_start(part):
        await_bytes(y_in.at[part], y_sem.at[1, part])
        total = y_out[part, y].astype(F32)
        for step in range(y_count - 1):
            total = total + y_in[part, step].astype(F32)
        far_send(part, total)

    def far_send(part, total):
        far[part, far_at] = total.astype(BF16)
        for step in far_steps:
            fetch(far.at[part, far_at], far.at[part, far_at], far_sem.at[0, part], far_sem.at[1, part], at_z(step, x_hi))

    def near_start(part):
        await_bytes(far.at[part, pl.ds(0, far_count - 1)], far_sem.at[1, part])
        total = far[part, 0].astype(F32)
        for i in range(1, far_count):
            total = total + far[part, i].astype(F32)
        slot = 2 * near_at + x_hi
        near[part, slot] = total.astype(BF16)
        for to in [at_z(step, 1 - x_hi) for step in [0] + near_steps] + [at_z(step, x_hi) for step in near_steps]:
            fetch(near.at[part, slot], near.at[part, slot], near_sem.at[0, part], near_sem.at[1, part], to)

    def final_start(part):
        await_bytes(near.at[part, pl.ds(0, 2 * near_count - 1)], near_sem.at[1, part])
        for row in range(2):
            total = near[part, row].astype(F32)
            for i in range(1, near_count):
                total = total + near[part, 2 * i + row].astype(F32)
            final[part, core, row] = total * scale
        fetch(
            final.at[part, core], final.at[part, core], final_sem.at[0, part], final_sem.at[1, part], partner
        )

    def finish(part):
        await_bytes(final.at[part, 0], final_sem.at[1, part])
        for w in range(4):
            for i in range(2):
                up_out[w, 2 * part + i] = final[part, w // 2, w % 2, :, i * COUT : (i + 1) * COUT]

    slope, outside = forward_part(lat, lat_count, grid, up_kernel, bias, act)
    act_patches = patches(positions(act, INNER, 0), False)
    mix_part_sums(grid, act_patches, mix_sums)
    fetch(mix_sums.at[1 - core], mix_core_in, core_sem.at[0, MIX], core_sem.at[1, MIX], partner)
    backward_part(grid, mix_kernel, slope, outside, pre_grad)
    up_part_sums(grid, pre_grad, 0, sums)
    core_start(0)
    up_part_sums(grid, pre_grad, 1, sums)
    core_start(1)
    mix_first()
    x_first(0)
    x_first(1)
    for part in UP:
        x_second(part)
    for part in UP:
        y_start(part)
    mix_second()
    section_part(act_patches, mix_kernel, staged, out_wide, section)
    mix_third()
    for part in UP:
        far_start(part)
    input_part(pre_grad, up_kernel, act, input_grad)
    mix_fourth()
    for part in UP:
        near_start(part)
    mix_fifth()
    for part in UP:
        final_start(part)
    mix_finish()
    for copy in halo:
        copy.wait_send()
    await_bytes(mix_y_in, mix_sem.at[0])
    await_bytes(mix_x_in.at[pl.ds(0, 3)], mix_sem.at[2])
    await_bytes(mix_core_in, core_sem.at[0, MIX])
    await_bytes(mix_far.at[pl.ds(0, far_count - 1)], far_sem.at[0, MIX])
    await_bytes(mix_near.at[pl.ds(0, near_count - 1)], near_sem.at[0, MIX])
    await_bytes(mix_final.at[0], final_sem.at[0, MIX])
    for part in UP:
        for side in range(2):
            await_bytes(xa_in.at[part, side], x_sem.at[0, part, side])
            await_bytes(xb_in.at[part, side], x_sem.at[2, part, side])
        await_bytes(y_in.at[part], y_sem.at[0, part])
        await_bytes(core_in.at[part], core_sem.at[0, part])
        await_bytes(far.at[part, pl.ds(0, far_count - 1)], far_sem.at[0, part])
        await_bytes(near.at[part, pl.ds(0, 2 * near_count - 1)], near_sem.at[0, part])
        await_bytes(final.at[part, 0], final_sem.at[0, part])
    for part in UP:
        finish(part)


def write_kernel(*refs):
    copies = [pltpu.make_async_copy(refs[i], refs[4 + i], refs[8].at[i]) for i in range(4)]
    for copy in copies:
        copy.start()
    for copy in copies:
        copy.wait()


def shards(elem_codes, block_exps, up_kernel, up_bias, mix_kernel, cotangent):
    lat_count, lon_count = lax.axis_size("lat"), lax.axis_size("lon")
    y_count, z_count = lon_count // 2, lat_count // 4
    far_count, near_count = z_plan(z_count)
    out_cells = 4 * CELLS * lat_count * lon_count
    operands = (
        elem_codes.reshape(CELLS, CIN),
        block_exps.transpose(1, 2, 0).reshape(COLS * CIN // BLOCK, ROWS),
        cotangent.reshape(4 * CELLS, COUT),
        up_kernel.reshape(16, CIN, COUT),
        up_bias.reshape(1, COUT),
        mix_kernel.reshape(9, COUT, COUT),
    )
    dma = pltpu.SemaphoreType.DMA
    results = pl.pallas_call(
        functools.partial(section_kernel, lat_count, lon_count, 1.0 / math.sqrt(out_cells)),
        out_shape=(
            pltpu.VMEM((4 * CELLS, COUT), BF16),
            pltpu.VMEM((CELLS, CIN), F32),
            pltpu.VMEM((4, 4, LON_ALL, COUT), F32),
            pltpu.VMEM((9, 8, COUT), F32),
        ),
        in_specs=[pl.BlockSpec(memory_space=pltpu.HBM)] * 6,
        out_specs=[pl.BlockSpec(memory_space=pltpu.VMEM)] * 4,
        scratch_shapes=[pltpu.VMEM(operand.shape, operand.dtype) for operand in operands]
        + [
            dma((6,)),
            pltpu.VMEM((TALL, FLAT, COUT), F32),
            pltpu.VMEM((TALL, CELLS, COUT), F32),
            pltpu.VMEM((4 * CELLS, COUT), F32),
            pltpu.VMEM((2, TALL // 2, 2 * COLS, COUT), BF16),
            pltpu.VMEM((2, TALL, ROWS, COUT), BF16),
            pltpu.VMEM((4, 8, COUT), F32),
            pltpu.VMEM((2, TALL // 2, 2 * COLS, COUT), BF16),
            pltpu.VMEM((2, TALL, ROWS, COUT), BF16),
            pltpu.VMEM((4, 8, COUT), F32),
            dma((8,)),
            dma((8,)),
            pltpu.VMEM((4, FLAT, COUT), F32),
            pltpu.VMEM((4, FLAT, COUT), F32),
            pltpu.VMEM((4 * INNER, COUT), F32),
            pltpu.VMEM((4 * CELLS, COUT), F32),
            pltpu.VMEM((2, 2, 2, CIN, SPAN), BF16),
            pltpu.VMEM((2, 2, CIN, SPAN), BF16),
            pltpu.VMEM((2, 4, y_count, 16, SPAN), BF16),
            pltpu.VMEM((2, 2, y_count // 2, 16, SPAN), BF16),
            pltpu.VMEM((2, 2, y_count, 16, SPAN), BF16),
            pltpu.VMEM((2, y_count, 16, SPAN), BF16),
            pltpu.VMEM((2, y_count - 1, 16, SPAN), BF16),
            pltpu.VMEM((2, 2, y_count, MIX_ROWS, COUT), BF16),
            pltpu.VMEM((2, y_count, MIX_ROWS, COUT), BF16),
            pltpu.VMEM((2, y_count, MIX_ROWS, COUT), BF16),
            pltpu.VMEM((y_count - 1, 2, MIX_ROWS, COUT), BF16),
            pltpu.VMEM((2, MIX_ROWS, COUT), BF16),
            pltpu.VMEM((4, MIX_ROWS, COUT), BF16),
            pltpu.VMEM((far_count, MIX_ROWS, COUT), BF16),
            pltpu.VMEM((near_count, MIX_ROWS, COUT), BF16),
            pltpu.VMEM((2, MIX_ROWS, COUT), F32),
            pltpu.VMEM((2, far_count, 16, SPAN), BF16),
            pltpu.VMEM((2, 2 * near_count, 16, SPAN), BF16),
            pltpu.VMEM((2, 2, 2, 16, SPAN), F32),
            dma((2, PARTS)),
            dma((4, 2, 2)),
            dma((2, 2)),
            dma((2, PARTS)),
            dma((2, PARTS)),
            dma((2, PARTS)),
            dma((4,)),
        ],
        compiler_params=pltpu.CompilerParams(
            collective_id=0, has_side_effects=True, vmem_limit_bytes=40 * 2**20
        ),
    )(*[pltpu.with_memory_space_constraint(operand, pltpu.HBM) for operand in operands])
    section, input_grad, up_part, mix_part = pl.pallas_call(
        write_kernel,
        out_shape=tuple(jax.ShapeDtypeStruct(result.shape, result.dtype) for result in results),
        in_specs=[pl.BlockSpec(memory_space=pltpu.VMEM)] * 4,
        out_specs=[pl.BlockSpec(memory_space=pltpu.HBM)] * 4,
        scratch_shapes=[dma((4,))],
        compiler_params=pltpu.CompilerParams(vmem_limit_bytes=8 * 2**20),
    )(*results)
    return (
        section.reshape(2 * ROWS, 2 * COLS, COUT),
        input_grad.reshape(ROWS, COLS, CIN),
        up_part,
        mix_part.reshape(3, 3, 8, COUT),
    )


def solution(mesh):
    placed = (P("lat", "lon", None), P("lat", "lon", None), P(), P(), P(), P("lat", "lon", None))
    return jax.shard_map(
        shards,
        mesh=mesh,
        in_specs=placed,
        out_specs=(
            P("lat", "lon", None),
            P("lat", "lon", None),
            P(None, None, "lon", None),
            P(None, None, "lon", None),
        ),
        check_vma=False,
    )
```

```python
import functools
import math

import jax
import jax.numpy as jnp
from jax import lax
from jax.experimental import pallas as pl
from jax.experimental.pallas import tpu as pltpu
from jax.sharding import PartitionSpec as P

CIN = 256
COUT = 128
BLOCK = 32
ROWS = 16
COLS = 8
PITCH = 10
CELLS = ROWS * COLS
TALL = CIN // COUT + 4
FLAT = 192
OUTER = 176
INNER = ROWS * PITCH
PARTS = 5
SPAN = COUT
MIX = 4
MIX_TAPS = (5, 4)
MIX_ROWS = 48
UP = (0, 1, 2, 3)
LON_ALL = 16
MESH = pl.DeviceIdType.MESH
F32 = jnp.float32
BF16 = jnp.bfloat16


def power_bits(value, bits):
    total = jnp.where(value & 1 != 0, 2.0, 1.0)
    for bit in range(1, bits):
        total = total * jnp.where(value & (1 << bit) != 0, float(1 << (1 << bit)), 1.0)
    return total


def decode(codes, factor):
    sign = jnp.where(codes >= 128, -(2.0**-9), 2.0**-9)
    fraction = (8 + (codes & 7)).astype(F32) * 0.125
    return sign * power_bits((codes >> 3) & 15, 4) * fraction * factor


def block_factors(exps, own):
    factor = power_bits(exps + 2, 2).astype(BF16)
    count = exps.shape[0]
    lane = lax.broadcasted_iota(jnp.int32, (count, COLS * CIN), 1)
    row = lax.broadcasted_iota(jnp.int32, (count, COLS * CIN), 0)
    spread = jnp.where(lane // BLOCK == row, 1.0, 0.0).astype(BF16)
    wide = lax.dot_general(factor, spread, (((0,), (0,)), ((), ())), preferred_element_type=F32)
    for c in range(COLS):
        for i in range(CIN // COUT):
            at = c * CIN + i * COUT
            own[i, pl.ds(c, ROWS, stride=COLS), :] = wide[:, at : at + COUT]


def halo_partners(lat, lon, lat_count, lon_count):
    up, down = lax.rem(lat + lat_count - 1, lat_count), lax.rem(lat + 1, lat_count)
    left, right = lax.rem(lon + lon_count - 1, lon_count), lax.rem(lon + 1, lon_count)
    return up, down, left, right


def halo_fill(codes, exps, cot, grid, own, cot_wide, row_out, col_out, corner_out):
    block_factors(exps[...], own)
    for i in range(CIN // COUT):
        own[i] = decode(codes[:, i * COUT : (i + 1) * COUT], own[i])
    cot_wide[...] = cot[...].astype(F32)
    for r in range(ROWS):
        for s in range(2):
            for t in range(2):
                own[2 + 2 * s + t, r * COLS : (r + 1) * COLS, :] = cot_wide[
                    pl.ds((2 * r + s) * 2 * COLS + t, COLS, stride=2), :
                ]
    for side, r in enumerate((ROWS - 1, 0)):
        for i in range(TALL // 2):
            row_out[side, i] = jnp.concatenate(
                [own[j, r * COLS : (r + 1) * COLS, :] for j in (2 * i, 2 * i + 1)], axis=0
            ).astype(BF16)
    for side, c in enumerate((COLS - 1, 0)):
        for i in range(TALL):
            col_out[side, i] = own[i, pl.ds(c, ROWS, stride=COLS), :].astype(BF16)
    for corner, (r, c) in enumerate(((ROWS - 1, COLS - 1), (ROWS - 1, 0), (0, COLS - 1), (0, 0))):
        cell = r * COLS + c
        corner_out[corner] = jnp.zeros((8, COUT), F32)
        for i in range(TALL):
            corner_out[corner, i : i + 1, :] = own[i, cell : cell + 1, :]
    for r in range(ROWS):
        at = (r + 1) * PITCH + 1
        for i in range(TALL):
            grid[i, at : at + COLS, :] = own[i, r * COLS : (r + 1) * COLS, :]
    tail = (ROWS + 2) * PITCH
    for i in range(TALL):
        grid[i, tail:FLAT, :] = jnp.zeros((FLAT - tail, COUT), F32)


def halo_copies(partners, lat, lon, row_out, col_out, corner_out, row_in, col_in, corner_in, send, recv):
    up, down, left, right = partners
    plan = [
        (row_out.at[0], row_in.at[0], down, lon),
        (row_out.at[1], row_in.at[1], up, lon),
        (col_out.at[0], col_in.at[0], lat, right),
        (col_out.at[1], col_in.at[1], lat, left),
        (corner_out.at[0], corner_in.at[0], down, right),
        (corner_out.at[1], corner_in.at[1], down, left),
        (corner_out.at[2], corner_in.at[2], up, right),
        (corner_out.at[3], corner_in.at[3], up, left),
    ]
    return [
        pltpu.make_async_remote_copy(
            src_ref=src,
            dst_ref=dst,
            send_sem=send.at[i],
            recv_sem=recv.at[i],
            device_id=(to_lat, to_lon),
            device_id_type=MESH,
        )
        for i, (src, dst, to_lat, to_lon) in enumerate(plan)
    ]


def halo_place(copies, lat, lat_count, grid, row_in, col_in, corner_in):
    above = (lat > 0).astype(F32)
    below = (lat < lat_count - 1).astype(F32)
    for side, (r, keep) in enumerate(((0, above), (ROWS + 1, below))):
        copies[side].wait_recv()
        at = r * PITCH + 1
        for i in range(TALL // 2):
            part = row_in[side, i].astype(F32) * keep
            grid[2 * i, at : at + COLS, :] = part[:COLS]
            grid[2 * i + 1, at : at + COLS, :] = part[COLS:]
    for side, c in enumerate((0, COLS + 1)):
        copies[2 + side].wait_recv()
        for i in range(TALL):
            grid[i, pl.ds(PITCH + c, ROWS, stride=PITCH), :] = col_in[side, i].astype(F32)
    places = ((0, 0, above), (0, COLS + 1, above), (ROWS + 1, 0, below), (ROWS + 1, COLS + 1, below))
    for corner, (r, c, keep) in enumerate(places):
        copies[4 + corner].wait_recv()
        cell = r * PITCH + c
        for i in range(TALL):
            grid[i, cell : cell + 1, :] = corner_in[corner, i : i + 1, :] * keep


OFFSETS = ((0, 0), (0, 1), (1, 0), (1, 1))


def positions(ref, length, low):
    found = {}
    for dr, dc in OFFSETS:
        for pr in range(2):
            for pc in range(2):
                found[2 * dr + pr, 2 * dc + pc] = ref[
                    low + 2 * pr + pc, pl.ds(dr * PITCH + dc, length), :
                ].astype(BF16)
    return found


def window(ref, start, length, low, high):
    return jnp.concatenate([ref[i, pl.ds(start, length), :] for i in range(low, high)], axis=1)


def keep_wide(ref, value):
    for i in range(4):
        ref[i, :OUTER, :] = value[:, i * COUT : (i + 1) * COUT]
        ref[i, OUTER:, :] = jnp.zeros((FLAT - OUTER, COUT), F32)


def patches(found, flipped):
    stacked = []
    for s in range(2):
        for t in range(2):
            pieces = []
            for ky in range(3):
                for kx in range(3):
                    at = (s - ky + 2, t - kx + 2) if flipped else (s + ky, t + kx)
                    pieces.append(found[at])
            stacked.append(jnp.concatenate(pieces, axis=1))
    return jnp.concatenate(stacked, axis=0)


def beside(array, rows):
    return jnp.concatenate([array[i * rows : (i + 1) * rows] for i in range(4)], axis=1)


def inner_mask(lanes):
    cell = lax.broadcasted_iota(jnp.int32, (INNER, lanes), 0)
    return lax.rem(cell, PITCH) < COLS


def forward_part(lat, lat_count, grid, up_kernel, bias, act):
    windows = [window(grid, dr * PITCH + dc, OUTER, 0, 2).astype(BF16) for dr, dc in OFFSETS]
    forward = jnp.concatenate(
        [
            jnp.concatenate(
                [
                    up_kernel[(2 * (1 - dr) + pr) * 4 + 2 * (1 - dc) + pc]
                    for pr in range(2)
                    for pc in range(2)
                ],
                axis=1,
            )
            for dr, dc in OFFSETS
        ],
        axis=0,
    )
    raw = jnp.dot(jnp.concatenate(windows, axis=1), forward, preferred_element_type=F32)
    plain = (raw + jnp.concatenate([bias[...]] * 4, axis=1)).astype(BF16).astype(F32)
    sigmoid = jax.nn.sigmoid(plain)
    activated = (plain * sigmoid).astype(BF16).astype(F32)
    cell = lax.broadcasted_iota(jnp.int32, (OUTER, 4 * COUT), 0)
    lane = lax.broadcasted_iota(jnp.int32, (OUTER, 4 * COUT), 1)
    outside = ((cell < PITCH) & (lane < 2 * COUT) & (lat == 0)) | (
        (cell >= ROWS * PITCH) & (lane >= 2 * COUT) & (lat == lat_count - 1)
    )
    keep_wide(act, jnp.where(outside, 0.0, activated))
    return sigmoid * (1.0 + plain * (1.0 - sigmoid)), outside


def mix_part_sums(grid, act_patches, mix_sums):
    cot_own = window(grid, PITCH + 1, INNER, 2, TALL)
    cot_own = jnp.where(inner_mask(4 * COUT), cot_own, 0.0).astype(BF16)
    cot_stacked = jnp.concatenate([cot_own[:, i * COUT : (i + 1) * COUT] for i in range(4)], axis=0)
    mix_sum = lax.dot_general(
        act_patches, cot_stacked, (((0,), (0,)), ((), ())), preferred_element_type=F32
    )
    empty = jnp.zeros((LON_ALL, 8, COUT), F32)
    tap = 0
    for core, count in enumerate(MIX_TAPS):
        rows = [empty] * (MIX_ROWS // 8)
        for i in range(count):
            rows[i] = mix_sum[tap * COUT : (tap + 1) * COUT].reshape(LON_ALL, 8, COUT)
            tap += 1
        mix_sums[core] = jnp.concatenate(rows, axis=1).astype(BF16).reshape(mix_sums.shape[1:])


def backward_part(grid, mix_kernel, slope, outside, pre_grad):
    backward = jnp.concatenate([mix_kernel[i] for i in range(9)], axis=1)
    act_grad = lax.dot_general(
        patches(positions(grid, OUTER, 2), True),
        backward,
        (((1,), (1,)), ((), ())),
        preferred_element_type=F32,
    )
    graded = (beside(act_grad, OUTER) * slope).astype(BF16).astype(F32)
    keep_wide(pre_grad, jnp.where(outside, 0.0, graded))


def grad_window(pre_grad, dr, dc):
    return window(pre_grad, dr * PITCH + dc, INNER, 0, 4).astype(BF16)


def up_part_sums(grid, pre_grad, dc, sums):
    in_own = window(grid, PITCH + 1, INNER, 0, 2)
    in_own = jnp.where(inner_mask(CIN), in_own, 0.0).astype(BF16)
    for dr in range(2):
        up_sum = lax.dot_general(
            in_own,
            grad_window(pre_grad, dr, dc),
            (((0,), (0,)), ((), ())),
            preferred_element_type=F32,
        ).astype(BF16)
        for pr in range(2):
            for pc in range(2):
                at = (2 * pr + pc) * COUT
                sums[dr, 2 * dc + pc, pr] = up_sum[:, at : at + COUT]


def section_part(act_patches, mix_kernel, staged, out_wide, section):
    flat_mix = mix_kernel[...].reshape(9 * COUT, COUT)
    staged[...] = jnp.dot(act_patches, flat_mix, preferred_element_type=F32)
    for s in range(2):
        for t in range(2):
            for r in range(ROWS):
                out_wide[pl.ds((2 * r + s) * 2 * COLS + t, COLS, stride=2), :] = staged[
                    pl.ds((2 * s + t) * INNER + r * PITCH, COLS), :
                ]
    section[...] = out_wide[...].astype(BF16)


def input_part(pre_grad, up_kernel, act, input_grad):
    back_up = jnp.concatenate(
        [
            up_kernel[(2 * dr + pr) * 4 + 2 * dc + pc]
            for dr, dc in OFFSETS
            for pr in range(2)
            for pc in range(2)
        ],
        axis=1,
    )
    grad_windows = jnp.concatenate([grad_window(pre_grad, dr, dc) for dr, dc in OFFSETS], axis=1)
    spread = lax.dot_general(
        grad_windows, back_up, (((1,), (1,)), ((), ())), preferred_element_type=F32
    )
    for i in range(2):
        act[i, :INNER, :] = spread[:, i * COUT : (i + 1) * COUT]
        for r in range(ROWS):
            input_grad[r * COLS : (r + 1) * COLS, i * COUT : (i + 1) * COUT] = act[
                i, pl.ds(r * PITCH, COLS), :
            ]


def reduce_partners(lat, lon, z_count, y_count):
    core, x_hi, z = lax.rem(lat, 2), lax.rem(lat // 2, 2), lat // 4
    y, x_lo = lax.rem(lon, y_count), lon // y_count
    return core, x_hi, z, y, x_lo


def fetch(src, dst, send, recv, to):
    copy = pltpu.make_async_remote_copy(
        src_ref=src, dst_ref=dst, send_sem=send, recv_sem=recv, device_id=to, device_id_type=MESH
    )
    copy.start()


def await_bytes(ref, sem):
    pltpu.make_async_copy(ref, ref, sem).wait()


def z_plan(z_count):
    return 3, z_count // 3


def section_kernel(
    lat_count,
    lon_count,
    scale,
    codes_hbm,
    exps_hbm,
    cot_hbm,
    up_hbm,
    bias_hbm,
    mix_hbm,
    section,
    input_grad,
    up_out,
    mix_out,
    codes,
    exps,
    cot,
    up_kernel,
    bias,
    mix_kernel,
    load_sem,
    grid,
    own,
    cot_wide,
    row_out,
    col_out,
    corner_out,
    row_in,
    col_in,
    corner_in,
    halo_send,
    halo_recv,
    act,
    pre_grad,
    staged,
    out_wide,
    sums,
    core_in,
    x_out,
    xa_in,
    xb_in,
    y_out,
    y_in,
    mix_sums,
    mix_core_in,
    mix_y_out,
    mix_y_in,
    mix_x_out,
    mix_x_in,
    mix_far,
    mix_near,
    mix_final,
    far,
    near,
    final,
    core_sem,
    x_sem,
    y_sem,
    far_sem,
    near_sem,
    final_sem,
    mix_sem,
):
    z_count, y_count = lat_count // 4, lon_count // 2
    far_count, near_count = z_plan(z_count)
    lat, lon = lax.axis_index("lat"), lax.axis_index("lon")
    core, x_hi, z, y, x_lo = reduce_partners(lat, lon, z_count, y_count)
    x = 2 * x_hi + x_lo

    def at_x(step):
        other = lax.rem(x + step + 4, 4)
        return 4 * z + 2 * (other // 2) + core, lax.rem(other, 2) * y_count + y

    def at_y(step):
        return lat, x_lo * y_count + lax.rem(y + step, y_count)

    def at_z(step, row):
        return 4 * lax.rem(z + step + z_count, z_count) + 2 * row + core, lon

    partner = (lat + 1 - 2 * core, lon)
    far_steps = [near_count * i for i in range(1, far_count)]
    near_steps = [i if 2 * i <= near_count else i - near_count for i in range(1, near_count)]

    loads = [
        pltpu.make_async_copy(src, dst, load_sem.at[i])
        for i, (src, dst) in enumerate(
            (
                (exps_hbm, exps),
                (codes_hbm, codes),
                (cot_hbm, cot),
                (up_hbm, up_kernel),
                (mix_hbm, mix_kernel),
                (bias_hbm, bias),
            )
        )
    ]
    barrier = pltpu.get_barrier_semaphore()
    up, down, left, right = partners = halo_partners(lat, lon, lat_count, lon_count)
    greeted = [(a, b) for a in (up, down) for b in (left, lon, right)] + [(lat, left), (lat, right)]
    greeted += [partner, at_x(1), at_x(2), at_x(-1)]
    greeted += [at_y(step) for step in range(1, y_count)]
    far_all = sorted({step % z_count for base in far_steps for step in (base, -base)})
    near_all = sorted({step % z_count for base in near_steps for step in (base, -base)})
    greeted += [at_z(step, x_hi) for step in far_all + near_all]
    greeted += [at_z(step, 1 - x_hi) for step in [0] + near_all]
    for to in greeted:
        pl.semaphore_signal(barrier, inc=1, device_id=to, device_id_type=MESH)
    for load in loads:
        load.start()
    for load in loads[:3]:
        load.wait()
    halo_fill(codes, exps, cot, grid, own, cot_wide, row_out, col_out, corner_out)
    pl.semaphore_wait(barrier, len(greeted))
    halo = halo_copies(
        partners, lat, lon, row_out, col_out, corner_out, row_in, col_in, corner_in, halo_send, halo_recv
    )
    for copy in reversed(halo):
        copy.start()
    for load in loads[3:]:
        load.wait()
    halo_place(halo, lat, lat_count, grid, row_in, col_in, corner_in)

    def core_start(part):
        fetch(sums.at[1 - core, part], core_in.at[part], core_sem.at[0, part], core_sem.at[1, part], partner)

    half = y_count // 2
    y_steps = sorted(range(1, y_count), key=lambda step: -min(step, y_count - step))

    def core_end(part):
        await_bytes(core_in.at[part], core_sem.at[1, part])
        merged = sums[core, part].astype(F32) + core_in[part].astype(F32)
        x_out[part] = merged.astype(BF16).reshape(x_out.shape[1:])

    def mix_first():
        await_bytes(mix_core_in, core_sem.at[1, MIX])
        mix_y_out[...] = (mix_sums[core].astype(F32) + mix_core_in[...].astype(F32)).astype(BF16)
        for step in y_steps:
            fetch(
                mix_y_out.at[:, lax.rem(y + step, y_count)],
                mix_y_in.at[step - 1],
                mix_sem.at[0],
                mix_sem.at[1],
                at_y(step),
            )

    def mix_second():
        await_bytes(mix_y_in, mix_sem.at[1])
        total = mix_y_out[:, y].astype(F32)
        for step in range(y_count - 1):
            total = total + mix_y_in[step].astype(F32)
        mix_x_out[...] = total.astype(BF16)
        for step in (2, 1, 3):
            fetch(
                mix_x_out.at[lax.rem(x + step, 2)], mix_x_in.at[x], mix_sem.at[2], mix_sem.at[3], at_x(step)
            )
        mix_x_in[x] = mix_x_out[x_lo]

    def summed(ref, count):
        total = ref[0].astype(F32)
        for i in range(1, count):
            total = total + ref[i].astype(F32)
        return total

    def mix_third():
        await_bytes(mix_x_in.at[pl.ds(0, 3)], mix_sem.at[3])
        mix_far[far_at] = summed(mix_x_in, 4).astype(BF16)
        for step in far_steps:
            fetch(mix_far.at[far_at], mix_far.at[far_at], far_sem.at[0, MIX], far_sem.at[1, MIX], at_z(step, x_hi))

    def mix_fourth():
        await_bytes(mix_far.at[pl.ds(0, far_count - 1)], far_sem.at[1, MIX])
        mix_near[near_at] = summed(mix_far, far_count).astype(BF16)
        for step in near_steps:
            fetch(
                mix_near.at[near_at], mix_near.at[near_at], near_sem.at[0, MIX], near_sem.at[1, MIX], at_z(step, x_hi)
            )

    def mix_fifth():
        await_bytes(mix_near.at[pl.ds(0, near_count - 1)], near_sem.at[1, MIX])
        mix_final[core] = summed(mix_near, near_count) * scale
        fetch(mix_final.at[core], mix_final.at[core], final_sem.at[0, MIX], final_sem.at[1, MIX], partner)

    def mix_finish():
        await_bytes(mix_final.at[0], final_sem.at[1, MIX])
        tap = 0
        for owner, count in enumerate(MIX_TAPS):
            for i in range(count):
                mix_out[tap] = mix_final[owner, i * 8 : i * 8 + 8, :]
                tap += 1

    def x_first(part):
        core_end(part)
        across = lax.rem(x + 2, 4)
        for side, step in ((0, 1), (1, -1)):
            fetch(
                x_out.at[part, across, pl.ds(side * half, half)],
                xa_in.at[part, side],
                x_sem.at[0, part, side],
                x_sem.at[1, part, side],
                at_x(step),
            )

    def x_second(part):
        for side, step in ((0, 1), (1, -1)):
            await_bytes(xa_in.at[part, side], x_sem.at[1, part, side])
            beside_x = lax.rem(x + step + 4, 4)
            rows = pl.ds(side * half, half)
            merged = x_out[part, beside_x, rows].astype(F32) + xa_in[part, side].astype(F32)
            x_out[part, beside_x, rows] = merged.astype(BF16)
            fetch(
                x_out.at[part, beside_x],
                xb_in.at[part, side],
                x_sem.at[2, part, side],
                x_sem.at[3, part, side],
                at_x(step),
            )

    def y_start(part):
        for side in range(2):
            await_bytes(xb_in.at[part, side], x_sem.at[3, part, side])
        merged = x_out[part, x].astype(F32) + xb_in[part, 0].astype(F32) + xb_in[part, 1].astype(F32)
        y_out[part] = merged.astype(BF16)
        for step in y_steps:
            fetch(
                y_out.at[part, lax.rem(y + step, y_count)],
                y_in.at[part, step - 1],
                y_sem.at[0, part],
                y_sem.at[1, part],
                at_y(step),
            )

    far_at, near_at = z // near_count, lax.rem(z, near_count)

    def far_start(part):
        await_bytes(y_in.at[part], y_sem.at[1, part])
        total = y_out[part, y].astype(F32)
        for step in range(y_count - 1):
            total = total + y_in[part, step].astype(F32)
        far_send(part, total)

    def far_send(part, total):
        far[part, far_at] = total.astype(BF16)
        for step in far_steps:
            fetch(far.at[part, far_at], far.at[part, far_at], far_sem.at[0, part], far_sem.at[1, part], at_z(step, x_hi))

    def near_start(part):
        await_bytes(far.at[part, pl.ds(0, far_count - 1)], far_sem.at[1, part])
        total = far[part, 0].astype(F32)
        for i in range(1, far_count):
            total = total + far[part, i].astype(F32)
        slot = 2 * near_at + x_hi
        near[part, slot] = total.astype(BF16)
        for to in [at_z(step, 1 - x_hi) for step in [0] + near_steps] + [at_z(step, x_hi) for step in near_steps]:
            fetch(near.at[part, slot], near.at[part, slot], near_sem.at[0, part], near_sem.at[1, part], to)

    def final_start(part):
        await_bytes(near.at[part, pl.ds(0, 2 * near_count - 1)], near_sem.at[1, part])
        for row in range(2):
            total = near[part, row].astype(F32)
            for i in range(1, near_count):
                total = total + near[part, 2 * i + row].astype(F32)
            final[part, core, row] = total * scale
        fetch(
            final.at[part, core], final.at[part, core], final_sem.at[0, part], final_sem.at[1, part], partner
        )

    def finish(part):
        await_bytes(final.at[part, 0], final_sem.at[1, part])
        for w in range(4):
            up_out[w, part] = final[part, w // 2, w % 2]

    slope, outside = forward_part(lat, lat_count, grid, up_kernel, bias, act)
    act_patches = patches(positions(act, INNER, 0), False)
    mix_part_sums(grid, act_patches, mix_sums)
    fetch(mix_sums.at[1 - core], mix_core_in, core_sem.at[0, MIX], core_sem.at[1, MIX], partner)
    backward_part(grid, mix_kernel, slope, outside, pre_grad)
    for dc in range(2):
        up_part_sums(grid, pre_grad, dc, sums)
        for pc in range(2):
            core_start(2 * dc + pc)
    mix_first()
    for part in UP:
        x_first(part)
    for part in UP:
        x_second(part)
    for part in UP:
        y_start(part)
    mix_second()
    section_part(act_patches, mix_kernel, staged, out_wide, section)
    mix_third()
    for part in UP:
        far_start(part)
    input_part(pre_grad, up_kernel, act, input_grad)
    mix_fourth()
    for part in UP:
        near_start(part)
    mix_fifth()
    for part in UP:
        final_start(part)
    mix_finish()
    for copy in halo:
        copy.wait_send()
    await_bytes(mix_y_in, mix_sem.at[0])
    await_bytes(mix_x_in.at[pl.ds(0, 3)], mix_sem.at[2])
    await_bytes(mix_core_in, core_sem.at[0, MIX])
    await_bytes(mix_far.at[pl.ds(0, far_count - 1)], far_sem.at[0, MIX])
    await_bytes(mix_near.at[pl.ds(0, near_count - 1)], near_sem.at[0, MIX])
    await_bytes(mix_final.at[0], final_sem.at[0, MIX])
    for part in UP:
        for side in range(2):
            await_bytes(xa_in.at[part, side], x_sem.at[0, part, side])
            await_bytes(xb_in.at[part, side], x_sem.at[2, part, side])
        await_bytes(y_in.at[part], y_sem.at[0, part])
        await_bytes(core_in.at[part], core_sem.at[0, part])
        await_bytes(far.at[part, pl.ds(0, far_count - 1)], far_sem.at[0, part])
        await_bytes(near.at[part, pl.ds(0, 2 * near_count - 1)], near_sem.at[0, part])
        await_bytes(final.at[part, 0], final_sem.at[0, part])
    for part in UP:
        finish(part)


def write_kernel(*refs):
    copies = [pltpu.make_async_copy(refs[i], refs[4 + i], refs[8].at[i]) for i in range(4)]
    for copy in copies:
        copy.start()
    for copy in copies:
        copy.wait()


def shards(elem_codes, block_exps, up_kernel, up_bias, mix_kernel, cotangent):
    lat_count, lon_count = lax.axis_size("lat"), lax.axis_size("lon")
    y_count, z_count = lon_count // 2, lat_count // 4
    far_count, near_count = z_plan(z_count)
    out_cells = 4 * CELLS * lat_count * lon_count
    operands = (
        elem_codes.reshape(CELLS, CIN),
        block_exps.transpose(1, 2, 0).reshape(COLS * CIN // BLOCK, ROWS),
        cotangent.reshape(4 * CELLS, COUT),
        up_kernel.reshape(16, CIN, COUT),
        up_bias.reshape(1, COUT),
        mix_kernel.reshape(9, COUT, COUT),
    )
    dma = pltpu.SemaphoreType.DMA
    results = pl.pallas_call(
        functools.partial(section_kernel, lat_count, lon_count, 1.0 / math.sqrt(out_cells)),
        out_shape=(
            pltpu.VMEM((4 * CELLS, COUT), BF16),
            pltpu.VMEM((CELLS, CIN), F32),
            pltpu.VMEM((4, 4, LON_ALL, COUT), F32),
            pltpu.VMEM((9, 8, COUT), F32),
        ),
        in_specs=[pl.BlockSpec(memory_space=pltpu.HBM)] * 6,
        out_specs=[pl.BlockSpec(memory_space=pltpu.VMEM)] * 4,
        scratch_shapes=[pltpu.VMEM(operand.shape, operand.dtype) for operand in operands]
        + [
            dma((6,)),
            pltpu.VMEM((TALL, FLAT, COUT), F32),
            pltpu.VMEM((TALL, CELLS, COUT), F32),
            pltpu.VMEM((4 * CELLS, COUT), F32),
            pltpu.VMEM((2, TALL // 2, 2 * COLS, COUT), BF16),
            pltpu.VMEM((2, TALL, ROWS, COUT), BF16),
            pltpu.VMEM((4, 8, COUT), F32),
            pltpu.VMEM((2, TALL // 2, 2 * COLS, COUT), BF16),
            pltpu.VMEM((2, TALL, ROWS, COUT), BF16),
            pltpu.VMEM((4, 8, COUT), F32),
            dma((8,)),
            dma((8,)),
            pltpu.VMEM((4, FLAT, COUT), F32),
            pltpu.VMEM((4, FLAT, COUT), F32),
            pltpu.VMEM((4 * INNER, COUT), F32),
            pltpu.VMEM((4 * CELLS, COUT), F32),
            pltpu.VMEM((2, len(UP), 2, CIN, SPAN), BF16),
            pltpu.VMEM((len(UP), 2, CIN, SPAN), BF16),
            pltpu.VMEM((len(UP), 4, y_count, 16, SPAN), BF16),
            pltpu.VMEM((len(UP), 2, y_count // 2, 16, SPAN), BF16),
            pltpu.VMEM((len(UP), 2, y_count, 16, SPAN), BF16),
            pltpu.VMEM((len(UP), y_count, 16, SPAN), BF16),
            pltpu.VMEM((len(UP), y_count - 1, 16, SPAN), BF16),
            pltpu.VMEM((2, 2, y_count, MIX_ROWS, COUT), BF16),
            pltpu.VMEM((2, y_count, MIX_ROWS, COUT), BF16),
            pltpu.VMEM((2, y_count, MIX_ROWS, COUT), BF16),
            pltpu.VMEM((y_count - 1, 2, MIX_ROWS, COUT), BF16),
            pltpu.VMEM((2, MIX_ROWS, COUT), BF16),
            pltpu.VMEM((4, MIX_ROWS, COUT), BF16),
            pltpu.VMEM((far_count, MIX_ROWS, COUT), BF16),
            pltpu.VMEM((near_count, MIX_ROWS, COUT), BF16),
            pltpu.VMEM((2, MIX_ROWS, COUT), F32),
            pltpu.VMEM((len(UP), far_count, 16, SPAN), BF16),
            pltpu.VMEM((len(UP), 2 * near_count, 16, SPAN), BF16),
            pltpu.VMEM((len(UP), 2, 2, 16, SPAN), F32),
            dma((2, PARTS)),
            dma((4, len(UP), 2)),
            dma((2, len(UP))),
            dma((2, PARTS)),
            dma((2, PARTS)),
            dma((2, PARTS)),
            dma((4,)),
        ],
        compiler_params=pltpu.CompilerParams(
            collective_id=0, has_side_effects=True, vmem_limit_bytes=40 * 2**20
        ),
    )(*[pltpu.with_memory_space_constraint(operand, pltpu.HBM) for operand in operands])
    section, input_grad, up_part, mix_part = pl.pallas_call(
        write_kernel,
        out_shape=tuple(jax.ShapeDtypeStruct(result.shape, result.dtype) for result in results),
        in_specs=[pl.BlockSpec(memory_space=pltpu.VMEM)] * 4,
        out_specs=[pl.BlockSpec(memory_space=pltpu.HBM)] * 4,
        scratch_shapes=[dma((4,))],
        compiler_params=pltpu.CompilerParams(vmem_limit_bytes=8 * 2**20),
    )(*results)
    return (
        section.reshape(2 * ROWS, 2 * COLS, COUT),
        input_grad.reshape(ROWS, COLS, CIN),
        up_part,
        mix_part.reshape(3, 3, 8, COUT),
    )


def solution(mesh):
    placed = (P("lat", "lon", None), P("lat", "lon", None), P(), P(), P(), P("lat", "lon", None))
    return jax.shard_map(
        shards,
        mesh=mesh,
        in_specs=placed,
        out_specs=(
            P("lat", "lon", None),
            P("lat", "lon", None),
            P(None, None, "lon", None),
            P(None, None, "lon", None),
        ),
        check_vma=False,
    )
```

```python
import functools
import math

import jax
import jax.numpy as jnp
from jax import lax
from jax.experimental import pallas as pl
from jax.experimental.pallas import tpu as pltpu
from jax.sharding import PartitionSpec as P

CIN = 256
COUT = 128
BLOCK = 32
ROWS = 16
COLS = 8
PITCH = 10
CELLS = ROWS * COLS
TALL = CIN // COUT + 4
FLAT = 192
OUTER = 176
INNER = ROWS * PITCH
PARTS = 3
SPAN = 2 * COUT
MIX = 2
MIX_TAPS = (5, 4)
MIX_ROWS = 48
UP = (0, 1)
LON_ALL = 16
MESH = pl.DeviceIdType.MESH
F32 = jnp.float32
BF16 = jnp.bfloat16


def power_bits(value, bits):
    total = jnp.where(value & 1 != 0, 2.0, 1.0)
    for bit in range(1, bits):
        total = total * jnp.where(value & (1 << bit) != 0, float(1 << (1 << bit)), 1.0)
    return total


def decode(codes, factor):
    sign = jnp.where(codes >= 128, -(2.0**-9), 2.0**-9)
    fraction = (8 + (codes & 7)).astype(F32) * 0.125
    return sign * power_bits((codes >> 3) & 15, 4) * fraction * factor


def block_factors(exps, own):
    factor = power_bits(exps + 2, 2).astype(BF16)
    count = exps.shape[0]
    lane = lax.broadcasted_iota(jnp.int32, (count, COLS * CIN), 1)
    row = lax.broadcasted_iota(jnp.int32, (count, COLS * CIN), 0)
    spread = jnp.where(lane // BLOCK == row, 1.0, 0.0).astype(BF16)
    wide = lax.dot_general(factor, spread, (((0,), (0,)), ((), ())), preferred_element_type=F32)
    for c in range(COLS):
        for i in range(CIN // COUT):
            at = c * CIN + i * COUT
            own[i, pl.ds(c, ROWS, stride=COLS), :] = wide[:, at : at + COUT]


def halo_partners(lat, lon, lat_count, lon_count):
    up, down = lax.rem(lat + lat_count - 1, lat_count), lax.rem(lat + 1, lat_count)
    left, right = lax.rem(lon + lon_count - 1, lon_count), lax.rem(lon + 1, lon_count)
    return up, down, left, right


def halo_fill(codes, exps, cot, grid, own, cot_wide, row_out, col_out, corner_out):
    block_factors(exps[...], own)
    for i in range(CIN // COUT):
        own[i] = decode(codes[:, i * COUT : (i + 1) * COUT], own[i])
    cot_wide[...] = cot[...].astype(F32)
    for r in range(ROWS):
        for s in range(2):
            for t in range(2):
                own[2 + 2 * s + t, r * COLS : (r + 1) * COLS, :] = cot_wide[
                    pl.ds((2 * r + s) * 2 * COLS + t, COLS, stride=2), :
                ]
    for side, r in enumerate((ROWS - 1, 0)):
        for i in range(TALL // 2):
            row_out[side, i] = jnp.concatenate(
                [own[j, r * COLS : (r + 1) * COLS, :] for j in (2 * i, 2 * i + 1)], axis=0
            ).astype(BF16)
    for side, c in enumerate((COLS - 1, 0)):
        for i in range(TALL):
            col_out[side, i] = own[i, pl.ds(c, ROWS, stride=COLS), :].astype(BF16)
    for corner, (r, c) in enumerate(((ROWS - 1, COLS - 1), (ROWS - 1, 0), (0, COLS - 1), (0, 0))):
        cell = r * COLS + c
        corner_out[corner] = jnp.zeros((8, COUT), F32)
        for i in range(TALL):
            corner_out[corner, i : i + 1, :] = own[i, cell : cell + 1, :]
    for r in range(ROWS):
        at = (r + 1) * PITCH + 1
        for i in range(TALL):
            grid[i, at : at + COLS, :] = own[i, r * COLS : (r + 1) * COLS, :]
    tail = (ROWS + 2) * PITCH
    for i in range(TALL):
        grid[i, tail:FLAT, :] = jnp.zeros((FLAT - tail, COUT), F32)


def halo_copies(partners, lat, lon, row_out, col_out, corner_out, row_in, col_in, corner_in, send, recv):
    up, down, left, right = partners
    plan = [
        (row_out.at[0], row_in.at[0], down, lon),
        (row_out.at[1], row_in.at[1], up, lon),
        (col_out.at[0], col_in.at[0], lat, right),
        (col_out.at[1], col_in.at[1], lat, left),
        (corner_out.at[0], corner_in.at[0], down, right),
        (corner_out.at[1], corner_in.at[1], down, left),
        (corner_out.at[2], corner_in.at[2], up, right),
        (corner_out.at[3], corner_in.at[3], up, left),
    ]
    return [
        pltpu.make_async_remote_copy(
            src_ref=src,
            dst_ref=dst,
            send_sem=send.at[i],
            recv_sem=recv.at[i],
            device_id=(to_lat, to_lon),
            device_id_type=MESH,
        )
        for i, (src, dst, to_lat, to_lon) in enumerate(plan)
    ]


def halo_place(copies, lat, lat_count, grid, row_in, col_in, corner_in):
    above = (lat > 0).astype(F32)
    below = (lat < lat_count - 1).astype(F32)
    for side, (r, keep) in enumerate(((0, above), (ROWS + 1, below))):
        copies[side].wait_recv()
        at = r * PITCH + 1
        for i in range(TALL // 2):
            part = row_in[side, i].astype(F32) * keep
            grid[2 * i, at : at + COLS, :] = part[:COLS]
            grid[2 * i + 1, at : at + COLS, :] = part[COLS:]
    for side, c in enumerate((0, COLS + 1)):
        copies[2 + side].wait_recv()
        for i in range(TALL):
            grid[i, pl.ds(PITCH + c, ROWS, stride=PITCH), :] = col_in[side, i].astype(F32)
    places = ((0, 0, above), (0, COLS + 1, above), (ROWS + 1, 0, below), (ROWS + 1, COLS + 1, below))
    for corner, (r, c, keep) in enumerate(places):
        copies[4 + corner].wait_recv()
        cell = r * PITCH + c
        for i in range(TALL):
            grid[i, cell : cell + 1, :] = corner_in[corner, i : i + 1, :] * keep


OFFSETS = ((0, 0), (0, 1), (1, 0), (1, 1))


def positions(ref, length, low):
    found = {}
    for dr, dc in OFFSETS:
        for pr in range(2):
            for pc in range(2):
                found[2 * dr + pr, 2 * dc + pc] = ref[
                    low + 2 * pr + pc, pl.ds(dr * PITCH + dc, length), :
                ].astype(BF16)
    return found


def window(ref, start, length, low, high):
    return jnp.concatenate([ref[i, pl.ds(start, length), :] for i in range(low, high)], axis=1)


def keep_wide(ref, value):
    for i in range(4):
        ref[i, :OUTER, :] = value[:, i * COUT : (i + 1) * COUT]
        ref[i, OUTER:, :] = jnp.zeros((FLAT - OUTER, COUT), F32)


def patches(found, flipped):
    stacked = []
    for s in range(2):
        for t in range(2):
            pieces = []
            for ky in range(3):
                for kx in range(3):
                    at = (s - ky + 2, t - kx + 2) if flipped else (s + ky, t + kx)
                    pieces.append(found[at])
            stacked.append(jnp.concatenate(pieces, axis=1))
    return jnp.concatenate(stacked, axis=0)


def beside(array, rows):
    return jnp.concatenate([array[i * rows : (i + 1) * rows] for i in range(4)], axis=1)


def inner_mask(lanes):
    cell = lax.broadcasted_iota(jnp.int32, (INNER, lanes), 0)
    return lax.rem(cell, PITCH) < COLS


def forward_part(lat, lat_count, grid, up_kernel, bias, act):
    windows = [window(grid, dr * PITCH + dc, OUTER, 0, 2).astype(BF16) for dr, dc in OFFSETS]
    forward = jnp.concatenate(
        [
            jnp.concatenate(
                [
                    up_kernel[(2 * (1 - dr) + pr) * 4 + 2 * (1 - dc) + pc]
                    for pr in range(2)
                    for pc in range(2)
                ],
                axis=1,
            )
            for dr, dc in OFFSETS
        ],
        axis=0,
    )
    raw = jnp.dot(jnp.concatenate(windows, axis=1), forward, preferred_element_type=F32)
    plain = (raw + jnp.concatenate([bias[...]] * 4, axis=1)).astype(BF16).astype(F32)
    sigmoid = jax.nn.sigmoid(plain)
    activated = (plain * sigmoid).astype(BF16).astype(F32)
    cell = lax.broadcasted_iota(jnp.int32, (OUTER, 4 * COUT), 0)
    lane = lax.broadcasted_iota(jnp.int32, (OUTER, 4 * COUT), 1)
    outside = ((cell < PITCH) & (lane < 2 * COUT) & (lat == 0)) | (
        (cell >= ROWS * PITCH) & (lane >= 2 * COUT) & (lat == lat_count - 1)
    )
    keep_wide(act, jnp.where(outside, 0.0, activated))
    return sigmoid * (1.0 + plain * (1.0 - sigmoid)), outside


def mix_part_sums(grid, act_patches, mix_sums):
    cot_own = window(grid, PITCH + 1, INNER, 2, TALL)
    cot_own = jnp.where(inner_mask(4 * COUT), cot_own, 0.0).astype(BF16)
    cot_stacked = jnp.concatenate([cot_own[:, i * COUT : (i + 1) * COUT] for i in range(4)], axis=0)
    mix_sum = lax.dot_general(
        act_patches, cot_stacked, (((0,), (0,)), ((), ())), preferred_element_type=F32
    )
    empty = jnp.zeros((LON_ALL, 8, COUT), F32)
    tap = 0
    for core, count in enumerate(MIX_TAPS):
        rows = [empty] * (MIX_ROWS // 8)
        for i in range(count):
            rows[i] = mix_sum[tap * COUT : (tap + 1) * COUT].reshape(LON_ALL, 8, COUT)
            tap += 1
        mix_sums[core] = jnp.concatenate(rows, axis=1).astype(BF16).reshape(mix_sums.shape[1:])


def backward_part(grid, mix_kernel, slope, outside, pre_grad):
    backward = jnp.concatenate([mix_kernel[i] for i in range(9)], axis=1)
    act_grad = lax.dot_general(
        patches(positions(grid, OUTER, 2), True),
        backward,
        (((1,), (1,)), ((), ())),
        preferred_element_type=F32,
    )
    graded = (beside(act_grad, OUTER) * slope).astype(BF16).astype(F32)
    keep_wide(pre_grad, jnp.where(outside, 0.0, graded))


def grad_window(pre_grad, dr, dc):
    return window(pre_grad, dr * PITCH + dc, INNER, 0, 4).astype(BF16)


def up_part_sums(grid, pre_grad, dc, sums):
    in_own = window(grid, PITCH + 1, INNER, 0, 2)
    in_own = jnp.where(inner_mask(CIN), in_own, 0.0).astype(BF16)
    for dr in range(2):
        up_sum = lax.dot_general(
            in_own,
            grad_window(pre_grad, dr, dc),
            (((0,), (0,)), ((), ())),
            preferred_element_type=F32,
        ).astype(BF16)
        for pr in range(2):
            sums[dr, dc, pr] = up_sum[:, pr * SPAN : (pr + 1) * SPAN]


def section_part(act_patches, mix_kernel, staged, out_wide, section):
    flat_mix = mix_kernel[...].reshape(9 * COUT, COUT)
    staged[...] = jnp.dot(act_patches, flat_mix, preferred_element_type=F32)
    for s in range(2):
        for t in range(2):
            for r in range(ROWS):
                out_wide[pl.ds((2 * r + s) * 2 * COLS + t, COLS, stride=2), :] = staged[
                    pl.ds((2 * s + t) * INNER + r * PITCH, COLS), :
                ]
    section[...] = out_wide[...].astype(BF16)


def input_part(pre_grad, up_kernel, act, input_grad):
    back_up = jnp.concatenate(
        [
            up_kernel[(2 * dr + pr) * 4 + 2 * dc + pc]
            for dr, dc in OFFSETS
            for pr in range(2)
            for pc in range(2)
        ],
        axis=1,
    )
    grad_windows = jnp.concatenate([grad_window(pre_grad, dr, dc) for dr, dc in OFFSETS], axis=1)
    spread = lax.dot_general(
        grad_windows, back_up, (((1,), (1,)), ((), ())), preferred_element_type=F32
    )
    for i in range(2):
        act[i, :INNER, :] = spread[:, i * COUT : (i + 1) * COUT]
        for r in range(ROWS):
            input_grad[r * COLS : (r + 1) * COLS, i * COUT : (i + 1) * COUT] = act[
                i, pl.ds(r * PITCH, COLS), :
            ]


def reduce_partners(lat, lon, z_count, y_count):
    core, x_hi, z = lax.rem(lat, 2), lax.rem(lat // 2, 2), lat // 4
    y, x_lo = lax.rem(lon, y_count), lon // y_count
    return core, x_hi, z, y, x_lo


def fetch(src, dst, send, recv, to):
    copy = pltpu.make_async_remote_copy(
        src_ref=src, dst_ref=dst, send_sem=send, recv_sem=recv, device_id=to, device_id_type=MESH
    )
    copy.start()


def await_bytes(ref, sem):
    pltpu.make_async_copy(ref, ref, sem).wait()


def z_plan(z_count):
    return 3, z_count // 3


def section_kernel(
    lat_count,
    lon_count,
    scale,
    codes_hbm,
    exps_hbm,
    cot_hbm,
    up_hbm,
    bias_hbm,
    mix_hbm,
    section,
    input_grad,
    up_out,
    mix_out,
    codes,
    exps,
    cot,
    up_kernel,
    bias,
    mix_kernel,
    load_sem,
    grid,
    own,
    cot_wide,
    row_out,
    col_out,
    corner_out,
    row_in,
    col_in,
    corner_in,
    halo_send,
    halo_recv,
    act,
    pre_grad,
    staged,
    out_wide,
    sums,
    core_in,
    x_out,
    x_in,
    y_out,
    y_in,
    mix_sums,
    mix_core_in,
    mix_y_out,
    mix_y_in,
    mix_x_out,
    mix_x_in,
    mix_far,
    mix_near,
    mix_final,
    far,
    near,
    final,
    core_sem,
    x_sem,
    y_sem,
    far_sem,
    near_sem,
    final_sem,
    mix_sem,
):
    z_count, y_count = lat_count // 4, lon_count // 2
    far_count, near_count = z_plan(z_count)
    lat, lon = lax.axis_index("lat"), lax.axis_index("lon")
    core, x_hi, z, y, x_lo = reduce_partners(lat, lon, z_count, y_count)
    x = 2 * x_hi + x_lo

    def at_x(step):
        other = lax.rem(x + step + 4, 4)
        return 4 * z + 2 * (other // 2) + core, lax.rem(other, 2) * y_count + y

    def at_y(step):
        return lat, x_lo * y_count + lax.rem(y + step, y_count)

    def at_z(step, row):
        return 4 * lax.rem(z + step + z_count, z_count) + 2 * row + core, lon

    partner = (lat + 1 - 2 * core, lon)
    far_steps = [near_count * i for i in range(1, far_count)]
    near_steps = [i if 2 * i <= near_count else i - near_count for i in range(1, near_count)]

    loads = [
        pltpu.make_async_copy(src, dst, load_sem.at[i])
        for i, (src, dst) in enumerate(
            (
                (exps_hbm, exps),
                (codes_hbm, codes),
                (cot_hbm, cot),
                (up_hbm, up_kernel),
                (mix_hbm, mix_kernel),
                (bias_hbm, bias),
            )
        )
    ]
    barrier = pltpu.get_barrier_semaphore()
    up, down, left, right = partners = halo_partners(lat, lon, lat_count, lon_count)
    greeted = [(a, b) for a in (up, down) for b in (left, lon, right)] + [(lat, left), (lat, right)]
    greeted += [partner, at_x(1), at_x(2), at_x(-1)]
    greeted += [at_y(step) for step in range(1, y_count)]
    far_all = sorted({step % z_count for base in far_steps for step in (base, -base)})
    near_all = sorted({step % z_count for base in near_steps for step in (base, -base)})
    greeted += [at_z(step, x_hi) for step in far_all + near_all]
    greeted += [at_z(step, 1 - x_hi) for step in [0] + near_all]
    for to in greeted:
        pl.semaphore_signal(barrier, inc=1, device_id=to, device_id_type=MESH)
    for load in loads:
        load.start()
    for load in loads[:3]:
        load.wait()
    halo_fill(codes, exps, cot, grid, own, cot_wide, row_out, col_out, corner_out)
    pl.semaphore_wait(barrier, len(greeted))
    halo = halo_copies(
        partners, lat, lon, row_out, col_out, corner_out, row_in, col_in, corner_in, halo_send, halo_recv
    )
    for copy in reversed(halo):
        copy.start()
    for load in loads[3:]:
        load.wait()
    halo_place(halo, lat, lat_count, grid, row_in, col_in, corner_in)

    def core_start(part):
        fetch(sums.at[1 - core, part], core_in.at[part], core_sem.at[0, part], core_sem.at[1, part], partner)

    y_steps = sorted(range(1, y_count), key=lambda step: -min(step, y_count - step))

    def core_end(part):
        await_bytes(core_in.at[part], core_sem.at[1, part])
        merged = sums[core, part].astype(F32) + core_in[part].astype(F32)
        x_out[part] = merged.astype(BF16).reshape(x_out.shape[1:])

    def mix_first():
        await_bytes(mix_core_in, core_sem.at[1, MIX])
        mix_y_out[...] = (mix_sums[core].astype(F32) + mix_core_in[...].astype(F32)).astype(BF16)
        for step in y_steps:
            fetch(
                mix_y_out.at[:, lax.rem(y + step, y_count)],
                mix_y_in.at[step - 1],
                mix_sem.at[0],
                mix_sem.at[1],
                at_y(step),
            )

    def mix_second():
        await_bytes(mix_y_in, mix_sem.at[1])
        total = mix_y_out[:, y].astype(F32)
        for step in range(y_count - 1):
            total = total + mix_y_in[step].astype(F32)
        mix_x_out[...] = total.astype(BF16)
        for step in (2, 1, 3):
            fetch(
                mix_x_out.at[lax.rem(x + step, 2)], mix_x_in.at[x], mix_sem.at[2], mix_sem.at[3], at_x(step)
            )
        mix_x_in[x] = mix_x_out[x_lo]

    def summed(ref, count):
        total = ref[0].astype(F32)
        for i in range(1, count):
            total = total + ref[i].astype(F32)
        return total

    def mix_third():
        await_bytes(mix_x_in.at[pl.ds(0, 3)], mix_sem.at[3])
        mix_far[far_at] = summed(mix_x_in, 4).astype(BF16)
        for step in far_steps:
            fetch(mix_far.at[far_at], mix_far.at[far_at], far_sem.at[0, MIX], far_sem.at[1, MIX], at_z(step, x_hi))

    def mix_fourth():
        await_bytes(mix_far.at[pl.ds(0, far_count - 1)], far_sem.at[1, MIX])
        mix_near[near_at] = summed(mix_far, far_count).astype(BF16)
        for step in near_steps:
            fetch(
                mix_near.at[near_at], mix_near.at[near_at], near_sem.at[0, MIX], near_sem.at[1, MIX], at_z(step, x_hi)
            )

    def mix_fifth():
        await_bytes(mix_near.at[pl.ds(0, near_count - 1)], near_sem.at[1, MIX])
        mix_final[core] = summed(mix_near, near_count) * scale
        fetch(mix_final.at[core], mix_final.at[core], final_sem.at[0, MIX], final_sem.at[1, MIX], partner)

    def mix_finish():
        await_bytes(mix_final.at[0], final_sem.at[1, MIX])
        tap = 0
        for owner, count in enumerate(MIX_TAPS):
            for i in range(count):
                mix_out[tap] = mix_final[owner, i * 8 : i * 8 + 8, :]
                tap += 1

    def x_start(part):
        core_end(part)
        for step in (2, 1, 3):
            fetch(
                x_out.at[part, lax.rem(x + step, 4)],
                x_in.at[part, step - 1],
                x_sem.at[0, part],
                x_sem.at[1, part],
                at_x(step),
            )

    def y_start(part):
        await_bytes(x_in.at[part], x_sem.at[1, part])
        total = x_out[part, x].astype(F32)
        for step in range(3):
            total = total + x_in[part, step].astype(F32)
        y_out[part] = total.astype(BF16)
        for step in y_steps:
            fetch(
                y_out.at[part, lax.rem(y + step, y_count)],
                y_in.at[part, step - 1],
                y_sem.at[0, part],
                y_sem.at[1, part],
                at_y(step),
            )

    far_at, near_at = z // near_count, lax.rem(z, near_count)

    def far_start(part):
        await_bytes(y_in.at[part], y_sem.at[1, part])
        total = y_out[part, y].astype(F32)
        for step in range(y_count - 1):
            total = total + y_in[part, step].astype(F32)
        far_send(part, total)

    def far_send(part, total):
        far[part, far_at] = total.astype(BF16)
        for step in far_steps:
            fetch(far.at[part, far_at], far.at[part, far_at], far_sem.at[0, part], far_sem.at[1, part], at_z(step, x_hi))

    def near_start(part):
        await_bytes(far.at[part, pl.ds(0, far_count - 1)], far_sem.at[1, part])
        total = far[part, 0].astype(F32)
        for i in range(1, far_count):
            total = total + far[part, i].astype(F32)
        slot = 2 * near_at + x_hi
        near[part, slot] = total.astype(BF16)
        for to in [at_z(step, 1 - x_hi) for step in [0] + near_steps] + [at_z(step, x_hi) for step in near_steps]:
            fetch(near.at[part, slot], near.at[part, slot], near_sem.at[0, part], near_sem.at[1, part], to)

    def final_start(part):
        await_bytes(near.at[part, pl.ds(0, 2 * near_count - 1)], near_sem.at[1, part])
        for row in range(2):
            total = near[part, row].astype(F32)
            for i in range(1, near_count):
                total = total + near[part, 2 * i + row].astype(F32)
            final[part, core, row] = total * scale
        fetch(
            final.at[part, core], final.at[part, core], final_sem.at[0, part], final_sem.at[1, part], partner
        )

    def finish(part):
        await_bytes(final.at[part, 0], final_sem.at[1, part])
        for w in range(4):
            for i in range(2):
                up_out[w, 2 * part + i] = final[part, w // 2, w % 2, :, i * COUT : (i + 1) * COUT]

    slope, outside = forward_part(lat, lat_count, grid, up_kernel, bias, act)
    act_patches = patches(positions(act, INNER, 0), False)
    mix_part_sums(grid, act_patches, mix_sums)
    fetch(mix_sums.at[1 - core], mix_core_in, core_sem.at[0, MIX], core_sem.at[1, MIX], partner)
    backward_part(grid, mix_kernel, slope, outside, pre_grad)
    up_part_sums(grid, pre_grad, 0, sums)
    core_start(0)
    up_part_sums(grid, pre_grad, 1, sums)
    core_start(1)
    mix_first()
    for part in UP:
        x_start(part)
    for part in UP:
        y_start(part)
    mix_second()
    section_part(act_patches, mix_kernel, staged, out_wide, section)
    mix_third()
    for part in UP:
        far_start(part)
    input_part(pre_grad, up_kernel, act, input_grad)
    mix_fourth()
    for part in UP:
        near_start(part)
    mix_fifth()
    for part in UP:
        final_start(part)
    mix_finish()
    for copy in halo:
        copy.wait_send()
    await_bytes(mix_y_in, mix_sem.at[0])
    await_bytes(mix_x_in.at[pl.ds(0, 3)], mix_sem.at[2])
    await_bytes(mix_core_in, core_sem.at[0, MIX])
    await_bytes(mix_far.at[pl.ds(0, far_count - 1)], far_sem.at[0, MIX])
    await_bytes(mix_near.at[pl.ds(0, near_count - 1)], near_sem.at[0, MIX])
    await_bytes(mix_final.at[0], final_sem.at[0, MIX])
    for part in UP:
        await_bytes(x_in.at[part], x_sem.at[0, part])
        await_bytes(y_in.at[part], y_sem.at[0, part])
        await_bytes(core_in.at[part], core_sem.at[0, part])
        await_bytes(far.at[part, pl.ds(0, far_count - 1)], far_sem.at[0, part])
        await_bytes(near.at[part, pl.ds(0, 2 * near_count - 1)], near_sem.at[0, part])
        await_bytes(final.at[part, 0], final_sem.at[0, part])
    for part in UP:
        finish(part)


def write_kernel(*refs):
    copies = [pltpu.make_async_copy(refs[i], refs[4 + i], refs[8].at[i]) for i in range(4)]
    for copy in copies:
        copy.start()
    for copy in copies:
        copy.wait()


def shards(elem_codes, block_exps, up_kernel, up_bias, mix_kernel, cotangent):
    lat_count, lon_count = lax.axis_size("lat"), lax.axis_size("lon")
    y_count, z_count = lon_count // 2, lat_count // 4
    far_count, near_count = z_plan(z_count)
    out_cells = 4 * CELLS * lat_count * lon_count
    operands = (
        elem_codes.reshape(CELLS, CIN),
        block_exps.transpose(1, 2, 0).reshape(COLS * CIN // BLOCK, ROWS),
        cotangent.reshape(4 * CELLS, COUT),
        up_kernel.reshape(16, CIN, COUT),
        up_bias.reshape(1, COUT),
        mix_kernel.reshape(9, COUT, COUT),
    )
    dma = pltpu.SemaphoreType.DMA
    results = pl.pallas_call(
        functools.partial(section_kernel, lat_count, lon_count, 1.0 / math.sqrt(out_cells)),
        out_shape=(
            pltpu.VMEM((4 * CELLS, COUT), BF16),
            pltpu.VMEM((CELLS, CIN), F32),
            pltpu.VMEM((4, 4, LON_ALL, COUT), F32),
            pltpu.VMEM((9, 8, COUT), F32),
        ),
        in_specs=[pl.BlockSpec(memory_space=pltpu.HBM)] * 6,
        out_specs=[pl.BlockSpec(memory_space=pltpu.VMEM)] * 4,
        scratch_shapes=[pltpu.VMEM(operand.shape, operand.dtype) for operand in operands]
        + [
            dma((6,)),
            pltpu.VMEM((TALL, FLAT, COUT), F32),
            pltpu.VMEM((TALL, CELLS, COUT), F32),
            pltpu.VMEM((4 * CELLS, COUT), F32),
            pltpu.VMEM((2, TALL // 2, 2 * COLS, COUT), BF16),
            pltpu.VMEM((2, TALL, ROWS, COUT), BF16),
            pltpu.VMEM((4, 8, COUT), F32),
            pltpu.VMEM((2, TALL // 2, 2 * COLS, COUT), BF16),
            pltpu.VMEM((2, TALL, ROWS, COUT), BF16),
            pltpu.VMEM((4, 8, COUT), F32),
            dma((8,)),
            dma((8,)),
            pltpu.VMEM((4, FLAT, COUT), F32),
            pltpu.VMEM((4, FLAT, COUT), F32),
            pltpu.VMEM((4 * INNER, COUT), F32),
            pltpu.VMEM((4 * CELLS, COUT), F32),
            pltpu.VMEM((2, 2, 2, CIN, SPAN), BF16),
            pltpu.VMEM((2, 2, CIN, SPAN), BF16),
            pltpu.VMEM((2, 4, y_count, 16, SPAN), BF16),
            pltpu.VMEM((2, 3, y_count, 16, SPAN), BF16),
            pltpu.VMEM((2, y_count, 16, SPAN), BF16),
            pltpu.VMEM((2, y_count - 1, 16, SPAN), BF16),
            pltpu.VMEM((2, 2, y_count, MIX_ROWS, COUT), BF16),
            pltpu.VMEM((2, y_count, MIX_ROWS, COUT), BF16),
            pltpu.VMEM((2, y_count, MIX_ROWS, COUT), BF16),
            pltpu.VMEM((y_count - 1, 2, MIX_ROWS, COUT), BF16),
            pltpu.VMEM((2, MIX_ROWS, COUT), BF16),
            pltpu.VMEM((4, MIX_ROWS, COUT), BF16),
            pltpu.VMEM((far_count, MIX_ROWS, COUT), BF16),
            pltpu.VMEM((near_count, MIX_ROWS, COUT), BF16),
            pltpu.VMEM((2, MIX_ROWS, COUT), F32),
            pltpu.VMEM((2, far_count, 16, SPAN), BF16),
            pltpu.VMEM((2, 2 * near_count, 16, SPAN), BF16),
            pltpu.VMEM((2, 2, 2, 16, SPAN), F32),
            dma((2, PARTS)),
            dma((2, 2)),
            dma((2, 2)),
            dma((2, PARTS)),
            dma((2, PARTS)),
            dma((2, PARTS)),
            dma((4,)),
        ],
        compiler_params=pltpu.CompilerParams(
            collective_id=0, has_side_effects=True, vmem_limit_bytes=40 * 2**20
        ),
    )(*[pltpu.with_memory_space_constraint(operand, pltpu.HBM) for operand in operands])
    section, input_grad, up_part, mix_part = pl.pallas_call(
        write_kernel,
        out_shape=tuple(jax.ShapeDtypeStruct(result.shape, result.dtype) for result in results),
        in_specs=[pl.BlockSpec(memory_space=pltpu.VMEM)] * 4,
        out_specs=[pl.BlockSpec(memory_space=pltpu.HBM)] * 4,
        scratch_shapes=[dma((4,))],
        compiler_params=pltpu.CompilerParams(vmem_limit_bytes=8 * 2**20),
    )(*results)
    return (
        section.reshape(2 * ROWS, 2 * COLS, COUT),
        input_grad.reshape(ROWS, COLS, CIN),
        up_part,
        mix_part.reshape(3, 3, 8, COUT),
    )


def solution(mesh):
    placed = (P("lat", "lon", None), P("lat", "lon", None), P(), P(), P(), P("lat", "lon", None))
    return jax.shard_map(
        shards,
        mesh=mesh,
        in_specs=placed,
        out_specs=(
            P("lat", "lon", None),
            P("lat", "lon", None),
            P(None, None, "lon", None),
            P(None, None, "lon", None),
        ),
        check_vma=False,
    )
```

```python
import functools
import math

import jax
import jax.numpy as jnp
from jax import lax
from jax.experimental import pallas as pl
from jax.experimental.pallas import tpu as pltpu
from jax.sharding import PartitionSpec as P

CIN = 256
COUT = 128
BLOCK = 32
ROWS = 16
COLS = 8
PITCH = 10
CELLS = ROWS * COLS
TALL = CIN // COUT + 4
FLAT = 192
OUTER = 176
INNER = ROWS * PITCH
PARTS = 3
SPAN = 2 * COUT
MIX = 2
MIX_TAPS = (5, 4)
MIX_ROWS = 48
UP = (0, 1)
LON_ALL = 16
MESH = pl.DeviceIdType.MESH
F32 = jnp.float32
BF16 = jnp.bfloat16


def power_bits(value, bits):
    total = jnp.where(value & 1 != 0, 2.0, 1.0)
    for bit in range(1, bits):
        total = total * jnp.where(value & (1 << bit) != 0, float(1 << (1 << bit)), 1.0)
    return total


def decode(codes, factor):
    sign = jnp.where(codes >= 128, -(2.0**-9), 2.0**-9)
    fraction = (8 + (codes & 7)).astype(F32) * 0.125
    return sign * power_bits((codes >> 3) & 15, 4) * fraction * factor


def block_factors(exps, own):
    factor = power_bits(exps + 2, 2).astype(BF16)
    count = exps.shape[0]
    lane = lax.broadcasted_iota(jnp.int32, (count, COLS * CIN), 1)
    row = lax.broadcasted_iota(jnp.int32, (count, COLS * CIN), 0)
    spread = jnp.where(lane // BLOCK == row, 1.0, 0.0).astype(BF16)
    wide = lax.dot_general(factor, spread, (((0,), (0,)), ((), ())), preferred_element_type=F32)
    for c in range(COLS):
        for i in range(CIN // COUT):
            at = c * CIN + i * COUT
            own[i, pl.ds(c, ROWS, stride=COLS), :] = wide[:, at : at + COUT]


def halo_partners(lat, lon, lat_count, lon_count):
    up, down = lax.rem(lat + lat_count - 1, lat_count), lax.rem(lat + 1, lat_count)
    left, right = lax.rem(lon + lon_count - 1, lon_count), lax.rem(lon + 1, lon_count)
    return up, down, left, right


def halo_fill(codes, exps, cot, grid, own, cot_wide, row_out, col_out, corner_out):
    block_factors(exps[...], own)
    for i in range(CIN // COUT):
        own[i] = decode(codes[:, i * COUT : (i + 1) * COUT], own[i])
    cot_wide[...] = cot[...].astype(F32)
    for r in range(ROWS):
        for s in range(2):
            for t in range(2):
                own[2 + 2 * s + t, r * COLS : (r + 1) * COLS, :] = cot_wide[
                    pl.ds((2 * r + s) * 2 * COLS + t, COLS, stride=2), :
                ]
    for side, r in enumerate((ROWS - 1, 0)):
        for i in range(TALL // 2):
            row_out[side, i] = jnp.concatenate(
                [own[j, r * COLS : (r + 1) * COLS, :] for j in (2 * i, 2 * i + 1)], axis=0
            ).astype(BF16)
    for side, c in enumerate((COLS - 1, 0)):
        for i in range(TALL):
            col_out[side, i] = own[i, pl.ds(c, ROWS, stride=COLS), :].astype(BF16)
    for corner, (r, c) in enumerate(((ROWS - 1, COLS - 1), (ROWS - 1, 0), (0, COLS - 1), (0, 0))):
        cell = r * COLS + c
        corner_out[corner] = jnp.zeros((8, COUT), F32)
        for i in range(TALL):
            corner_out[corner, i : i + 1, :] = own[i, cell : cell + 1, :]
    for r in range(ROWS):
        at = (r + 1) * PITCH + 1
        for i in range(TALL):
            grid[i, at : at + COLS, :] = own[i, r * COLS : (r + 1) * COLS, :]
    tail = (ROWS + 2) * PITCH
    for i in range(TALL):
        grid[i, tail:FLAT, :] = jnp.zeros((FLAT - tail, COUT), F32)


def halo_copies(partners, lat, lon, row_out, col_out, corner_out, row_in, col_in, corner_in, send, recv):
    up, down, left, right = partners
    plan = [
        (row_out.at[0], row_in.at[0], down, lon),
        (row_out.at[1], row_in.at[1], up, lon),
        (col_out.at[0], col_in.at[0], lat, right),
        (col_out.at[1], col_in.at[1], lat, left),
        (corner_out.at[0], corner_in.at[0], down, right),
        (corner_out.at[1], corner_in.at[1], down, left),
        (corner_out.at[2], corner_in.at[2], up, right),
        (corner_out.at[3], corner_in.at[3], up, left),
    ]
    return [
        pltpu.make_async_remote_copy(
            src_ref=src,
            dst_ref=dst,
            send_sem=send.at[i],
            recv_sem=recv.at[i],
            device_id=(to_lat, to_lon),
            device_id_type=MESH,
        )
        for i, (src, dst, to_lat, to_lon) in enumerate(plan)
    ]


def halo_place(copies, lat, lat_count, grid, row_in, col_in, corner_in):
    above = (lat > 0).astype(F32)
    below = (lat < lat_count - 1).astype(F32)
    for side, (r, keep) in enumerate(((0, above), (ROWS + 1, below))):
        copies[side].wait_recv()
        at = r * PITCH + 1
        for i in range(TALL // 2):
            part = row_in[side, i].astype(F32) * keep
            grid[2 * i, at : at + COLS, :] = part[:COLS]
            grid[2 * i + 1, at : at + COLS, :] = part[COLS:]
    for side, c in enumerate((0, COLS + 1)):
        copies[2 + side].wait_recv()
        for i in range(TALL):
            grid[i, pl.ds(PITCH + c, ROWS, stride=PITCH), :] = col_in[side, i].astype(F32)
    places = ((0, 0, above), (0, COLS + 1, above), (ROWS + 1, 0, below), (ROWS + 1, COLS + 1, below))
    for corner, (r, c, keep) in enumerate(places):
        copies[4 + corner].wait_recv()
        cell = r * PITCH + c
        for i in range(TALL):
            grid[i, cell : cell + 1, :] = corner_in[corner, i : i + 1, :] * keep


OFFSETS = ((0, 0), (0, 1), (1, 0), (1, 1))


def positions(ref, length, low):
    found = {}
    for dr, dc in OFFSETS:
        for pr in range(2):
            for pc in range(2):
                found[2 * dr + pr, 2 * dc + pc] = ref[
                    low + 2 * pr + pc, pl.ds(dr * PITCH + dc, length), :
                ].astype(BF16)
    return found


def window(ref, start, length, low, high):
    return jnp.concatenate([ref[i, pl.ds(start, length), :] for i in range(low, high)], axis=1)


def keep_wide(ref, value):
    for i in range(4):
        ref[i, :OUTER, :] = value[:, i * COUT : (i + 1) * COUT]
        ref[i, OUTER:, :] = jnp.zeros((FLAT - OUTER, COUT), F32)


def patches(found, flipped):
    stacked = []
    for s in range(2):
        for t in range(2):
            pieces = []
            for ky in range(3):
                for kx in range(3):
                    at = (s - ky + 2, t - kx + 2) if flipped else (s + ky, t + kx)
                    pieces.append(found[at])
            stacked.append(jnp.concatenate(pieces, axis=1))
    return jnp.concatenate(stacked, axis=0)


def beside(array, rows):
    return jnp.concatenate([array[i * rows : (i + 1) * rows] for i in range(4)], axis=1)


def inner_mask(lanes):
    cell = lax.broadcasted_iota(jnp.int32, (INNER, lanes), 0)
    return lax.rem(cell, PITCH) < COLS


def forward_part(lat, lat_count, grid, up_kernel, bias, act):
    windows = [window(grid, dr * PITCH + dc, OUTER, 0, 2).astype(BF16) for dr, dc in OFFSETS]
    forward = jnp.concatenate(
        [
            jnp.concatenate(
                [
                    up_kernel[(2 * (1 - dr) + pr) * 4 + 2 * (1 - dc) + pc]
                    for pr in range(2)
                    for pc in range(2)
                ],
                axis=1,
            )
            for dr, dc in OFFSETS
        ],
        axis=0,
    )
    raw = jnp.dot(jnp.concatenate(windows, axis=1), forward, preferred_element_type=F32)
    plain = (raw + jnp.concatenate([bias[...]] * 4, axis=1)).astype(BF16).astype(F32)
    sigmoid = jax.nn.sigmoid(plain)
    activated = (plain * sigmoid).astype(BF16).astype(F32)
    cell = lax.broadcasted_iota(jnp.int32, (OUTER, 4 * COUT), 0)
    lane = lax.broadcasted_iota(jnp.int32, (OUTER, 4 * COUT), 1)
    outside = ((cell < PITCH) & (lane < 2 * COUT) & (lat == 0)) | (
        (cell >= ROWS * PITCH) & (lane >= 2 * COUT) & (lat == lat_count - 1)
    )
    keep_wide(act, jnp.where(outside, 0.0, activated))
    return sigmoid * (1.0 + plain * (1.0 - sigmoid)), outside


def mix_part_sums(grid, act_patches, mix_sums):
    cot_own = window(grid, PITCH + 1, INNER, 2, TALL)
    cot_own = jnp.where(inner_mask(4 * COUT), cot_own, 0.0).astype(BF16)
    cot_stacked = jnp.concatenate([cot_own[:, i * COUT : (i + 1) * COUT] for i in range(4)], axis=0)
    mix_sum = lax.dot_general(
        act_patches, cot_stacked, (((0,), (0,)), ((), ())), preferred_element_type=F32
    )
    empty = jnp.zeros((LON_ALL, 8, COUT), F32)
    tap = 0
    for core, count in enumerate(MIX_TAPS):
        rows = [empty] * (MIX_ROWS // 8)
        for i in range(count):
            rows[i] = mix_sum[tap * COUT : (tap + 1) * COUT].reshape(LON_ALL, 8, COUT)
            tap += 1
        mix_sums[core] = jnp.concatenate(rows, axis=1).astype(BF16).reshape(mix_sums.shape[1:])


def backward_part(grid, back_mix, slope, outside, pre_grad):
    act_grad = jnp.dot(
        patches(positions(grid, OUTER, 2), True), back_mix[...], preferred_element_type=F32
    )
    graded = (beside(act_grad, OUTER) * slope).astype(BF16).astype(F32)
    keep_wide(pre_grad, jnp.where(outside, 0.0, graded))


def grad_window(pre_grad, dr, dc):
    return window(pre_grad, dr * PITCH + dc, INNER, 0, 4).astype(BF16)


def up_part_sums(grid, pre_grad, dc, sums):
    in_own = window(grid, PITCH + 1, INNER, 0, 2)
    in_own = jnp.where(inner_mask(CIN), in_own, 0.0).astype(BF16)
    for dr in range(2):
        up_sum = lax.dot_general(
            in_own,
            grad_window(pre_grad, dr, dc),
            (((0,), (0,)), ((), ())),
            preferred_element_type=F32,
        ).astype(BF16)
        for pr in range(2):
            sums[dr, dc, pr] = up_sum[:, pr * SPAN : (pr + 1) * SPAN]


def section_part(act_patches, mix_kernel, staged, out_wide, section):
    flat_mix = mix_kernel[...].reshape(9 * COUT, COUT)
    staged[...] = jnp.dot(act_patches, flat_mix, preferred_element_type=F32)
    for s in range(2):
        for t in range(2):
            for r in range(ROWS):
                out_wide[pl.ds((2 * r + s) * 2 * COLS + t, COLS, stride=2), :] = staged[
                    pl.ds((2 * s + t) * INNER + r * PITCH, COLS), :
                ]
    section[...] = out_wide[...].astype(BF16)


def input_part(pre_grad, up_kernel, act, input_grad):
    back_up = jnp.concatenate(
        [
            up_kernel[(2 * dr + pr) * 4 + 2 * dc + pc]
            for dr, dc in OFFSETS
            for pr in range(2)
            for pc in range(2)
        ],
        axis=1,
    )
    grad_windows = jnp.concatenate([grad_window(pre_grad, dr, dc) for dr, dc in OFFSETS], axis=1)
    spread = lax.dot_general(
        grad_windows, back_up, (((1,), (1,)), ((), ())), preferred_element_type=F32
    )
    for i in range(2):
        act[i, :INNER, :] = spread[:, i * COUT : (i + 1) * COUT]
        for r in range(ROWS):
            input_grad[r * COLS : (r + 1) * COLS, i * COUT : (i + 1) * COUT] = act[
                i, pl.ds(r * PITCH, COLS), :
            ]


def reduce_partners(lat, lon, z_count, y_count):
    core, x_hi, z = lax.rem(lat, 2), lax.rem(lat // 2, 2), lat // 4
    y, x_lo = lax.rem(lon, y_count), lon // y_count
    return core, x_hi, z, y, x_lo


def fetch(src, dst, send, recv, to):
    copy = pltpu.make_async_remote_copy(
        src_ref=src, dst_ref=dst, send_sem=send, recv_sem=recv, device_id=to, device_id_type=MESH
    )
    copy.start()


def await_bytes(ref, sem):
    pltpu.make_async_copy(ref, ref, sem).wait()


def z_plan(z_count):
    return 3, z_count // 3


def section_kernel(
    lat_count,
    lon_count,
    scale,
    codes_hbm,
    exps_hbm,
    cot_hbm,
    up_hbm,
    bias_hbm,
    mix_hbm,
    section,
    input_grad,
    up_out,
    mix_out,
    codes,
    exps,
    cot,
    up_kernel,
    bias,
    mix_kernel,
    load_sem,
    back_mix,
    grid,
    own,
    cot_wide,
    row_out,
    col_out,
    corner_out,
    row_in,
    col_in,
    corner_in,
    halo_send,
    halo_recv,
    act,
    pre_grad,
    staged,
    out_wide,
    sums,
    core_in,
    x_out,
    x_in,
    y_out,
    y_in,
    mix_sums,
    mix_core_in,
    mix_y_out,
    mix_y_in,
    mix_x_out,
    mix_x_in,
    mix_far,
    mix_near,
    mix_final,
    far,
    near,
    final,
    core_sem,
    x_sem,
    y_sem,
    far_sem,
    near_sem,
    final_sem,
    mix_sem,
):
    z_count, y_count = lat_count // 4, lon_count // 2
    far_count, near_count = z_plan(z_count)
    lat, lon = lax.axis_index("lat"), lax.axis_index("lon")
    core, x_hi, z, y, x_lo = reduce_partners(lat, lon, z_count, y_count)
    x = 2 * x_hi + x_lo

    def at_x(step):
        other = lax.rem(x + step + 4, 4)
        return 4 * z + 2 * (other // 2) + core, lax.rem(other, 2) * y_count + y

    def at_y(step):
        return lat, x_lo * y_count + lax.rem(y + step, y_count)

    def at_z(step, row):
        return 4 * lax.rem(z + step + z_count, z_count) + 2 * row + core, lon

    partner = (lat + 1 - 2 * core, lon)
    far_steps = [near_count * i for i in range(1, far_count)]
    near_steps = [i if 2 * i <= near_count else i - near_count for i in range(1, near_count)]

    loads = [
        pltpu.make_async_copy(src, dst, load_sem.at[i])
        for i, (src, dst) in enumerate(
            (
                (exps_hbm, exps),
                (codes_hbm, codes),
                (cot_hbm, cot),
                (up_hbm, up_kernel),
                (mix_hbm, mix_kernel),
                (bias_hbm, bias),
            )
        )
    ]
    barrier = pltpu.get_barrier_semaphore()
    up, down, left, right = partners = halo_partners(lat, lon, lat_count, lon_count)
    greeted = [(a, b) for a in (up, down) for b in (left, lon, right)] + [(lat, left), (lat, right)]
    greeted += [partner, at_x(1), at_x(2), at_x(-1)]
    greeted += [at_y(step) for step in range(1, y_count)]
    far_all = sorted({step % z_count for base in far_steps for step in (base, -base)})
    near_all = sorted({step % z_count for base in near_steps for step in (base, -base)})
    greeted += [at_z(step, x_hi) for step in far_all + near_all]
    greeted += [at_z(step, 1 - x_hi) for step in [0] + near_all]
    for to in greeted[:8]:
        pl.semaphore_signal(barrier, inc=1, device_id=to, device_id_type=MESH)
    for load in loads:
        load.start()
    for to in greeted[8:]:
        pl.semaphore_signal(barrier, inc=1, device_id=to, device_id_type=MESH)
    for load in loads[:3]:
        load.wait()
    halo_fill(codes, exps, cot, grid, own, cot_wide, row_out, col_out, corner_out)
    pl.semaphore_wait(barrier, len(greeted))
    halo = halo_copies(
        partners, lat, lon, row_out, col_out, corner_out, row_in, col_in, corner_in, halo_send, halo_recv
    )
    for copy in reversed(halo):
        copy.start()
    for load in loads[3:]:
        load.wait()
    for i in range(9):
        back_mix[i * COUT : (i + 1) * COUT, :] = mix_kernel[i].astype(F32).T.astype(BF16)
    halo_place(halo, lat, lat_count, grid, row_in, col_in, corner_in)

    def core_start(part):
        fetch(sums.at[1 - core, part], core_in.at[part], core_sem.at[0, part], core_sem.at[1, part], partner)

    y_steps = sorted(range(1, y_count), key=lambda step: -min(step, y_count - step))

    def core_end(part):
        await_bytes(core_in.at[part], core_sem.at[1, part])
        merged = sums[core, part].astype(F32) + core_in[part].astype(F32)
        x_out[part] = merged.astype(BF16).reshape(x_out.shape[1:])

    def mix_first():
        await_bytes(mix_core_in, core_sem.at[1, MIX])
        mix_y_out[...] = (mix_sums[core].astype(F32) + mix_core_in[...].astype(F32)).astype(BF16)
        for step in y_steps:
            fetch(
                mix_y_out.at[:, lax.rem(y + step, y_count)],
                mix_y_in.at[step - 1],
                mix_sem.at[0],
                mix_sem.at[1],
                at_y(step),
            )

    def mix_second():
        await_bytes(mix_y_in, mix_sem.at[1])
        total = mix_y_out[:, y].astype(F32)
        for step in range(y_count - 1):
            total = total + mix_y_in[step].astype(F32)
        mix_x_out[...] = total.astype(BF16)
        for step in (2, 1, 3):
            fetch(
                mix_x_out.at[lax.rem(x + step, 2)], mix_x_in.at[x], mix_sem.at[2], mix_sem.at[3], at_x(step)
            )
        mix_x_in[x] = mix_x_out[x_lo]

    def summed(ref, count):
        total = ref[0].astype(F32)
        for i in range(1, count):
            total = total + ref[i].astype(F32)
        return total

    def mix_third():
        await_bytes(mix_x_in.at[pl.ds(0, 3)], mix_sem.at[3])
        mix_far[far_at] = summed(mix_x_in, 4).astype(BF16)
        for step in far_steps:
            fetch(mix_far.at[far_at], mix_far.at[far_at], far_sem.at[0, MIX], far_sem.at[1, MIX], at_z(step, x_hi))

    def mix_fourth():
        await_bytes(mix_far.at[pl.ds(0, far_count - 1)], far_sem.at[1, MIX])
        mix_near[near_at] = summed(mix_far, far_count).astype(BF16)
        for step in near_steps:
            fetch(
                mix_near.at[near_at], mix_near.at[near_at], near_sem.at[0, MIX], near_sem.at[1, MIX], at_z(step, x_hi)
            )

    def mix_fifth():
        await_bytes(mix_near.at[pl.ds(0, near_count - 1)], near_sem.at[1, MIX])
        mix_final[core] = summed(mix_near, near_count) * scale
        fetch(mix_final.at[core], mix_final.at[core], final_sem.at[0, MIX], final_sem.at[1, MIX], partner)

    def mix_finish():
        await_bytes(mix_final.at[0], final_sem.at[1, MIX])
        tap = 0
        for owner, count in enumerate(MIX_TAPS):
            for i in range(count):
                mix_out[tap] = mix_final[owner, i * 8 : i * 8 + 8, :]
                tap += 1

    def x_start(part):
        core_end(part)
        for step in (2, 1, 3):
            fetch(
                x_out.at[part, lax.rem(x + step, 4)],
                x_in.at[part, step - 1],
                x_sem.at[0, part],
                x_sem.at[1, part],
                at_x(step),
            )

    def y_start(part):
        await_bytes(x_in.at[part], x_sem.at[1, part])
        total = x_out[part, x].astype(F32)
        for step in range(3):
            total = total + x_in[part, step].astype(F32)
        y_out[part] = total.astype(BF16)
        for step in y_steps:
            fetch(
                y_out.at[part, lax.rem(y + step, y_count)],
                y_in.at[part, step - 1],
                y_sem.at[0, part],
                y_sem.at[1, part],
                at_y(step),
            )

    far_at, near_at = z // near_count, lax.rem(z, near_count)

    def far_start(part):
        await_bytes(y_in.at[part], y_sem.at[1, part])
        total = y_out[part, y].astype(F32)
        for step in range(y_count - 1):
            total = total + y_in[part, step].astype(F32)
        far_send(part, total)

    def far_send(part, total):
        far[part, far_at] = total.astype(BF16)
        for step in far_steps:
            fetch(far.at[part, far_at], far.at[part, far_at], far_sem.at[0, part], far_sem.at[1, part], at_z(step, x_hi))

    def near_start(part):
        await_bytes(far.at[part, pl.ds(0, far_count - 1)], far_sem.at[1, part])
        total = far[part, 0].astype(F32)
        for i in range(1, far_count):
            total = total + far[part, i].astype(F32)
        slot = 2 * near_at + x_hi
        near[part, slot] = total.astype(BF16)
        for to in [at_z(step, 1 - x_hi) for step in [0] + near_steps] + [at_z(step, x_hi) for step in near_steps]:
            fetch(near.at[part, slot], near.at[part, slot], near_sem.at[0, part], near_sem.at[1, part], to)

    def final_start(part):
        await_bytes(near.at[part, pl.ds(0, 2 * near_count - 1)], near_sem.at[1, part])
        for row in range(2):
            total = near[part, row].astype(F32)
            for i in range(1, near_count):
                total = total + near[part, 2 * i + row].astype(F32)
            final[part, core, row] = total * scale
        fetch(
            final.at[part, core], final.at[part, core], final_sem.at[0, part], final_sem.at[1, part], partner
        )

    def finish(part):
        await_bytes(final.at[part, 0], final_sem.at[1, part])
        for w in range(4):
            for i in range(2):
                up_out[w, 2 * part + i] = final[part, w // 2, w % 2, :, i * COUT : (i + 1) * COUT]

    slope, outside = forward_part(lat, lat_count, grid, up_kernel, bias, act)
    act_patches = patches(positions(act, INNER, 0), False)
    mix_part_sums(grid, act_patches, mix_sums)
    fetch(mix_sums.at[1 - core], mix_core_in, core_sem.at[0, MIX], core_sem.at[1, MIX], partner)
    backward_part(grid, back_mix, slope, outside, pre_grad)
    up_part_sums(grid, pre_grad, 0, sums)
    core_start(0)
    up_part_sums(grid, pre_grad, 1, sums)
    core_start(1)
    mix_first()
    for part in UP:
        x_start(part)
    for part in UP:
        y_start(part)
    mix_second()
    section_part(act_patches, mix_kernel, staged, out_wide, section)
    mix_third()
    for part in UP:
        far_start(part)
    input_part(pre_grad, up_kernel, act, input_grad)
    mix_fourth()
    for part in UP:
        near_start(part)
    mix_fifth()
    for part in UP:
        final_start(part)
    mix_finish()
    for copy in halo:
        copy.wait_send()
    await_bytes(mix_y_in, mix_sem.at[0])
    await_bytes(mix_x_in.at[pl.ds(0, 3)], mix_sem.at[2])
    await_bytes(mix_core_in, core_sem.at[0, MIX])
    await_bytes(mix_far.at[pl.ds(0, far_count - 1)], far_sem.at[0, MIX])
    await_bytes(mix_near.at[pl.ds(0, near_count - 1)], near_sem.at[0, MIX])
    await_bytes(mix_final.at[0], final_sem.at[0, MIX])
    for part in UP:
        await_bytes(x_in.at[part], x_sem.at[0, part])
        await_bytes(y_in.at[part], y_sem.at[0, part])
        await_bytes(core_in.at[part], core_sem.at[0, part])
        await_bytes(far.at[part, pl.ds(0, far_count - 1)], far_sem.at[0, part])
        await_bytes(near.at[part, pl.ds(0, 2 * near_count - 1)], near_sem.at[0, part])
        await_bytes(final.at[part, 0], final_sem.at[0, part])
    for part in UP:
        finish(part)


def write_kernel(*refs):
    copies = [pltpu.make_async_copy(refs[i], refs[4 + i], refs[8].at[i]) for i in range(4)]
    for copy in copies:
        copy.start()
    for copy in copies:
        copy.wait()


def shards(elem_codes, block_exps, up_kernel, up_bias, mix_kernel, cotangent):
    lat_count, lon_count = lax.axis_size("lat"), lax.axis_size("lon")
    y_count, z_count = lon_count // 2, lat_count // 4
    far_count, near_count = z_plan(z_count)
    out_cells = 4 * CELLS * lat_count * lon_count
    operands = (
        elem_codes.reshape(CELLS, CIN),
        block_exps.transpose(1, 2, 0).reshape(COLS * CIN // BLOCK, ROWS),
        cotangent.reshape(4 * CELLS, COUT),
        up_kernel.reshape(16, CIN, COUT),
        up_bias.reshape(1, COUT),
        mix_kernel.reshape(9, COUT, COUT),
    )
    dma = pltpu.SemaphoreType.DMA
    results = pl.pallas_call(
        functools.partial(section_kernel, lat_count, lon_count, 1.0 / math.sqrt(out_cells)),
        out_shape=(
            pltpu.VMEM((4 * CELLS, COUT), BF16),
            pltpu.VMEM((CELLS, CIN), F32),
            pltpu.VMEM((4, 4, LON_ALL, COUT), F32),
            pltpu.VMEM((9, 8, COUT), F32),
        ),
        in_specs=[pl.BlockSpec(memory_space=pltpu.HBM)] * 6,
        out_specs=[pl.BlockSpec(memory_space=pltpu.VMEM)] * 4,
        scratch_shapes=[pltpu.VMEM(operand.shape, operand.dtype) for operand in operands]
        + [
            dma((6,)),
            pltpu.VMEM((9 * COUT, COUT), BF16),
            pltpu.VMEM((TALL, FLAT, COUT), F32),
            pltpu.VMEM((TALL, CELLS, COUT), F32),
            pltpu.VMEM((4 * CELLS, COUT), F32),
            pltpu.VMEM((2, TALL // 2, 2 * COLS, COUT), BF16),
            pltpu.VMEM((2, TALL, ROWS, COUT), BF16),
            pltpu.VMEM((4, 8, COUT), F32),
            pltpu.VMEM((2, TALL // 2, 2 * COLS, COUT), BF16),
            pltpu.VMEM((2, TALL, ROWS, COUT), BF16),
            pltpu.VMEM((4, 8, COUT), F32),
            dma((8,)),
            dma((8,)),
            pltpu.VMEM((4, FLAT, COUT), F32),
            pltpu.VMEM((4, FLAT, COUT), F32),
            pltpu.VMEM((4 * INNER, COUT), F32),
            pltpu.VMEM((4 * CELLS, COUT), F32),
            pltpu.VMEM((2, 2, 2, CIN, SPAN), BF16),
            pltpu.VMEM((2, 2, CIN, SPAN), BF16),
            pltpu.VMEM((2, 4, y_count, 16, SPAN), BF16),
            pltpu.VMEM((2, 3, y_count, 16, SPAN), BF16),
            pltpu.VMEM((2, y_count, 16, SPAN), BF16),
            pltpu.VMEM((2, y_count - 1, 16, SPAN), BF16),
            pltpu.VMEM((2, 2, y_count, MIX_ROWS, COUT), BF16),
            pltpu.VMEM((2, y_count, MIX_ROWS, COUT), BF16),
            pltpu.VMEM((2, y_count, MIX_ROWS, COUT), BF16),
            pltpu.VMEM((y_count - 1, 2, MIX_ROWS, COUT), BF16),
            pltpu.VMEM((2, MIX_ROWS, COUT), BF16),
            pltpu.VMEM((4, MIX_ROWS, COUT), BF16),
            pltpu.VMEM((far_count, MIX_ROWS, COUT), BF16),
            pltpu.VMEM((near_count, MIX_ROWS, COUT), BF16),
            pltpu.VMEM((2, MIX_ROWS, COUT), F32),
            pltpu.VMEM((2, far_count, 16, SPAN), BF16),
            pltpu.VMEM((2, 2 * near_count, 16, SPAN), BF16),
            pltpu.VMEM((2, 2, 2, 16, SPAN), F32),
            dma((2, PARTS)),
            dma((2, 2)),
            dma((2, 2)),
            dma((2, PARTS)),
            dma((2, PARTS)),
            dma((2, PARTS)),
            dma((4,)),
        ],
        compiler_params=pltpu.CompilerParams(
            collective_id=0, has_side_effects=True, vmem_limit_bytes=40 * 2**20
        ),
    )(*[pltpu.with_memory_space_constraint(operand, pltpu.HBM) for operand in operands])
    section, input_grad, up_part, mix_part = pl.pallas_call(
        write_kernel,
        out_shape=tuple(jax.ShapeDtypeStruct(result.shape, result.dtype) for result in results),
        in_specs=[pl.BlockSpec(memory_space=pltpu.VMEM)] * 4,
        out_specs=[pl.BlockSpec(memory_space=pltpu.HBM)] * 4,
        scratch_shapes=[dma((4,))],
        compiler_params=pltpu.CompilerParams(vmem_limit_bytes=8 * 2**20),
    )(*results)
    return (
        section.reshape(2 * ROWS, 2 * COLS, COUT),
        input_grad.reshape(ROWS, COLS, CIN),
        up_part,
        mix_part.reshape(3, 3, 8, COUT),
    )


def solution(mesh):
    placed = (P("lat", "lon", None), P("lat", "lon", None), P(), P(), P(), P("lat", "lon", None))
    return jax.shard_map(
        shards,
        mesh=mesh,
        in_specs=placed,
        out_specs=(
            P("lat", "lon", None),
            P("lat", "lon", None),
            P(None, None, "lon", None),
            P(None, None, "lon", None),
        ),
        check_vma=False,
    )
```

```python
import functools
import math

import jax
import jax.numpy as jnp
from jax import lax
from jax.experimental import pallas as pl
from jax.experimental.pallas import tpu as pltpu
from jax.sharding import PartitionSpec as P

CIN = 256
COUT = 128
BLOCK = 32
ROWS = 16
COLS = 8
PITCH = 10
CELLS = ROWS * COLS
TALL = CIN // COUT + 4
FLAT = 192
OUTER = 176
INNER = ROWS * PITCH
PARTS = 3
SPAN = 2 * COUT
MIX = 2
MIX_TAPS = (5, 4)
MIX_ROWS = 48
UP = (0, 1)
LON_ALL = 16
MESH = pl.DeviceIdType.MESH
F32 = jnp.float32
BF16 = jnp.bfloat16


def power_bits(value, bits):
    total = jnp.where(value & 1 != 0, 2.0, 1.0)
    for bit in range(1, bits):
        total = total * jnp.where(value & (1 << bit) != 0, float(1 << (1 << bit)), 1.0)
    return total


def decode(codes, factor):
    sign = jnp.where(codes >= 128, -(2.0**-9), 2.0**-9)
    fraction = (8 + (codes & 7)).astype(F32) * 0.125
    return sign * power_bits((codes >> 3) & 15, 4) * fraction * factor


def block_factors(exps, own):
    factor = power_bits(exps + 2, 2).astype(BF16)
    count = exps.shape[0]
    lane = lax.broadcasted_iota(jnp.int32, (count, COLS * CIN), 1)
    row = lax.broadcasted_iota(jnp.int32, (count, COLS * CIN), 0)
    spread = jnp.where(lane // BLOCK == row, 1.0, 0.0).astype(BF16)
    wide = lax.dot_general(factor, spread, (((0,), (0,)), ((), ())), preferred_element_type=F32)
    for c in range(COLS):
        for i in range(CIN // COUT):
            at = c * CIN + i * COUT
            own[i, pl.ds(c, ROWS, stride=COLS), :] = wide[:, at : at + COUT]


def halo_partners(lat, lon, lat_count, lon_count):
    up, down = lax.rem(lat + lat_count - 1, lat_count), lax.rem(lat + 1, lat_count)
    left, right = lax.rem(lon + lon_count - 1, lon_count), lax.rem(lon + 1, lon_count)
    return up, down, left, right


def halo_fill(codes, exps, cot, grid, own, cot_wide, row_out, col_out, corner_out):
    block_factors(exps[...], own)
    for i in range(CIN // COUT):
        own[i] = decode(codes[:, i * COUT : (i + 1) * COUT], own[i])
    cot_wide[...] = cot[...].astype(F32)
    for r in range(ROWS):
        for s in range(2):
            for t in range(2):
                own[2 + 2 * s + t, r * COLS : (r + 1) * COLS, :] = cot_wide[
                    pl.ds((2 * r + s) * 2 * COLS + t, COLS, stride=2), :
                ]
    for side, r in enumerate((ROWS - 1, 0)):
        for i in range(TALL // 2):
            row_out[side, i] = jnp.concatenate(
                [own[j, r * COLS : (r + 1) * COLS, :] for j in (2 * i, 2 * i + 1)], axis=0
            ).astype(BF16)
    for side, c in enumerate((COLS - 1, 0)):
        for i in range(TALL):
            col_out[side, i] = own[i, pl.ds(c, ROWS, stride=COLS), :].astype(BF16)
    for corner, (r, c) in enumerate(((ROWS - 1, COLS - 1), (ROWS - 1, 0), (0, COLS - 1), (0, 0))):
        cell = r * COLS + c
        corner_out[corner] = jnp.zeros((8, COUT), F32)
        for i in range(TALL):
            corner_out[corner, i : i + 1, :] = own[i, cell : cell + 1, :]
    for r in range(ROWS):
        at = (r + 1) * PITCH + 1
        for i in range(TALL):
            grid[i, at : at + COLS, :] = own[i, r * COLS : (r + 1) * COLS, :]
    tail = (ROWS + 2) * PITCH
    for i in range(TALL):
        grid[i, tail:FLAT, :] = jnp.zeros((FLAT - tail, COUT), F32)


def halo_copies(partners, lat, lon, row_out, col_out, corner_out, row_in, col_in, corner_in, send, recv):
    up, down, left, right = partners
    plan = [
        (row_out.at[0], row_in.at[0], down, lon),
        (row_out.at[1], row_in.at[1], up, lon),
        (col_out.at[0], col_in.at[0], lat, right),
        (col_out.at[1], col_in.at[1], lat, left),
        (corner_out.at[0], corner_in.at[0], down, right),
        (corner_out.at[1], corner_in.at[1], down, left),
        (corner_out.at[2], corner_in.at[2], up, right),
        (corner_out.at[3], corner_in.at[3], up, left),
    ]
    return [
        pltpu.make_async_remote_copy(
            src_ref=src,
            dst_ref=dst,
            send_sem=send.at[i],
            recv_sem=recv.at[i],
            device_id=(to_lat, to_lon),
            device_id_type=MESH,
        )
        for i, (src, dst, to_lat, to_lon) in enumerate(plan)
    ]


def halo_place(copies, lat, lat_count, grid, row_in, col_in, corner_in):
    above = (lat > 0).astype(F32)
    below = (lat < lat_count - 1).astype(F32)
    for side, (r, keep) in enumerate(((0, above), (ROWS + 1, below))):
        copies[side].wait_recv()
        at = r * PITCH + 1
        for i in range(TALL // 2):
            part = row_in[side, i].astype(F32) * keep
            grid[2 * i, at : at + COLS, :] = part[:COLS]
            grid[2 * i + 1, at : at + COLS, :] = part[COLS:]
    for side, c in enumerate((0, COLS + 1)):
        copies[2 + side].wait_recv()
        for i in range(TALL):
            grid[i, pl.ds(PITCH + c, ROWS, stride=PITCH), :] = col_in[side, i].astype(F32)
    places = ((0, 0, above), (0, COLS + 1, above), (ROWS + 1, 0, below), (ROWS + 1, COLS + 1, below))
    for corner, (r, c, keep) in enumerate(places):
        copies[4 + corner].wait_recv()
        cell = r * PITCH + c
        for i in range(TALL):
            grid[i, cell : cell + 1, :] = corner_in[corner, i : i + 1, :] * keep


OFFSETS = ((0, 0), (0, 1), (1, 0), (1, 1))


def positions(ref, length, low):
    found = {}
    for dr, dc in OFFSETS:
        for pr in range(2):
            for pc in range(2):
                found[2 * dr + pr, 2 * dc + pc] = ref[
                    low + 2 * pr + pc, pl.ds(dr * PITCH + dc, length), :
                ].astype(BF16)
    return found


def window(ref, start, length, low, high):
    return jnp.concatenate([ref[i, pl.ds(start, length), :] for i in range(low, high)], axis=1)


def keep_wide(ref, value):
    for i in range(4):
        ref[i, :OUTER, :] = value[:, i * COUT : (i + 1) * COUT]
        ref[i, OUTER:, :] = jnp.zeros((FLAT - OUTER, COUT), F32)


def patches(found, flipped):
    stacked = []
    for s in range(2):
        for t in range(2):
            pieces = []
            for ky in range(3):
                for kx in range(3):
                    at = (s - ky + 2, t - kx + 2) if flipped else (s + ky, t + kx)
                    pieces.append(found[at])
            stacked.append(jnp.concatenate(pieces, axis=1))
    return jnp.concatenate(stacked, axis=0)


def beside(array, rows):
    return jnp.concatenate([array[i * rows : (i + 1) * rows] for i in range(4)], axis=1)


def inner_mask(lanes):
    cell = lax.broadcasted_iota(jnp.int32, (INNER, lanes), 0)
    return lax.rem(cell, PITCH) < COLS


def forward_part(lat, lat_count, grid, up_kernel, bias, act):
    windows = [window(grid, dr * PITCH + dc, OUTER, 0, 2).astype(BF16) for dr, dc in OFFSETS]
    forward = jnp.concatenate(
        [
            jnp.concatenate(
                [
                    up_kernel[(2 * (1 - dr) + pr) * 4 + 2 * (1 - dc) + pc]
                    for pr in range(2)
                    for pc in range(2)
                ],
                axis=1,
            )
            for dr, dc in OFFSETS
        ],
        axis=0,
    )
    raw = jnp.dot(jnp.concatenate(windows, axis=1), forward, preferred_element_type=F32)
    plain = (raw + jnp.concatenate([bias[...]] * 4, axis=1)).astype(BF16).astype(F32)
    sigmoid = jax.nn.sigmoid(plain)
    activated = (plain * sigmoid).astype(BF16).astype(F32)
    cell = lax.broadcasted_iota(jnp.int32, (OUTER, 4 * COUT), 0)
    lane = lax.broadcasted_iota(jnp.int32, (OUTER, 4 * COUT), 1)
    outside = ((cell < PITCH) & (lane < 2 * COUT) & (lat == 0)) | (
        (cell >= ROWS * PITCH) & (lane >= 2 * COUT) & (lat == lat_count - 1)
    )
    keep_wide(act, jnp.where(outside, 0.0, activated))
    return sigmoid * (1.0 + plain * (1.0 - sigmoid)), outside


def mix_part_sums(grid, act_patches, mix_sums):
    cot_own = window(grid, PITCH + 1, INNER, 2, TALL)
    cot_own = jnp.where(inner_mask(4 * COUT), cot_own, 0.0).astype(BF16)
    cot_stacked = jnp.concatenate([cot_own[:, i * COUT : (i + 1) * COUT] for i in range(4)], axis=0)
    mix_sum = lax.dot_general(
        act_patches, cot_stacked, (((0,), (0,)), ((), ())), preferred_element_type=F32
    )
    empty = jnp.zeros((LON_ALL, 8, COUT), F32)
    tap = 0
    for core, count in enumerate(MIX_TAPS):
        rows = [empty] * (MIX_ROWS // 8)
        for i in range(count):
            rows[i] = mix_sum[tap * COUT : (tap + 1) * COUT].reshape(LON_ALL, 8, COUT)
            tap += 1
        mix_sums[core] = jnp.concatenate(rows, axis=1).astype(BF16).reshape(mix_sums.shape[1:])


def backward_part(grid, back_mix, slope, outside, pre_grad):
    act_grad = jnp.dot(
        patches(positions(grid, OUTER, 2), True), back_mix[...], preferred_element_type=F32
    )
    graded = (beside(act_grad, OUTER) * slope).astype(BF16).astype(F32)
    keep_wide(pre_grad, jnp.where(outside, 0.0, graded))


def grad_window(pre_grad, dr, dc):
    return window(pre_grad, dr * PITCH + dc, INNER, 0, 4).astype(BF16)


def up_part_sums(grid, pre_grad, dc, sums):
    in_own = window(grid, PITCH + 1, INNER, 0, 2)
    in_own = jnp.where(inner_mask(CIN), in_own, 0.0).astype(BF16)
    for dr in range(2):
        up_sum = lax.dot_general(
            in_own,
            grad_window(pre_grad, dr, dc),
            (((0,), (0,)), ((), ())),
            preferred_element_type=F32,
        ).astype(BF16)
        for pr in range(2):
            sums[dr, dc, pr] = up_sum[:, pr * SPAN : (pr + 1) * SPAN]


def section_part(act_patches, mix_kernel, staged, out_wide, section):
    flat_mix = mix_kernel[...].reshape(9 * COUT, COUT)
    staged[...] = jnp.dot(act_patches, flat_mix, preferred_element_type=F32)
    for s in range(2):
        for t in range(2):
            for r in range(ROWS):
                out_wide[pl.ds((2 * r + s) * 2 * COLS + t, COLS, stride=2), :] = staged[
                    pl.ds((2 * s + t) * INNER + r * PITCH, COLS), :
                ]
    section[...] = out_wide[...].astype(BF16)


def input_part(pre_grad, up_kernel, act, input_grad):
    back_up = jnp.concatenate(
        [
            up_kernel[(2 * dr + pr) * 4 + 2 * dc + pc]
            for dr, dc in OFFSETS
            for pr in range(2)
            for pc in range(2)
        ],
        axis=1,
    )
    grad_windows = jnp.concatenate([grad_window(pre_grad, dr, dc) for dr, dc in OFFSETS], axis=1)
    spread = lax.dot_general(
        grad_windows, back_up, (((1,), (1,)), ((), ())), preferred_element_type=F32
    )
    for i in range(2):
        act[i, :INNER, :] = spread[:, i * COUT : (i + 1) * COUT]
        for r in range(ROWS):
            input_grad[r * COLS : (r + 1) * COLS, i * COUT : (i + 1) * COUT] = act[
                i, pl.ds(r * PITCH, COLS), :
            ]


def reduce_partners(lat, lon, z_count, y_count):
    core, x_hi, z = lax.rem(lat, 2), lax.rem(lat // 2, 2), lat // 4
    y, x_lo = lax.rem(lon, y_count), lon // y_count
    return core, x_hi, z, y, x_lo


def fetch(src, dst, send, recv, to):
    copy = pltpu.make_async_remote_copy(
        src_ref=src, dst_ref=dst, send_sem=send, recv_sem=recv, device_id=to, device_id_type=MESH
    )
    copy.start()


def await_bytes(ref, sem):
    pltpu.make_async_copy(ref, ref, sem).wait()


def z_plan(z_count):
    return 3, z_count // 3


def section_kernel(
    lat_count,
    lon_count,
    scale,
    codes_hbm,
    exps_hbm,
    cot_hbm,
    up_hbm,
    bias_hbm,
    mix_hbm,
    section,
    input_grad,
    up_out,
    mix_out,
    codes,
    exps,
    cot,
    up_kernel,
    bias,
    mix_kernel,
    load_sem,
    back_mix,
    grid,
    own,
    cot_wide,
    row_out,
    col_out,
    corner_out,
    row_in,
    col_in,
    corner_in,
    halo_send,
    halo_recv,
    act,
    pre_grad,
    staged,
    out_wide,
    sums,
    core_in,
    x_out,
    x_in,
    y_out,
    y_in,
    mix_sums,
    mix_core_in,
    mix_y_out,
    mix_y_in,
    mix_x_out,
    mix_x_in,
    mix_far,
    mix_near,
    mix_final,
    far,
    near,
    final,
    core_sem,
    x_sem,
    y_sem,
    far_sem,
    near_sem,
    final_sem,
    mix_sem,
):
    z_count, y_count = lat_count // 4, lon_count // 2
    far_count, near_count = z_plan(z_count)
    lat, lon = lax.axis_index("lat"), lax.axis_index("lon")
    core, x_hi, z, y, x_lo = reduce_partners(lat, lon, z_count, y_count)
    x = 2 * x_hi + x_lo

    def at_x(step):
        other = lax.rem(x + step + 4, 4)
        return 4 * z + 2 * (other // 2) + core, lax.rem(other, 2) * y_count + y

    def at_y(step):
        return lat, x_lo * y_count + lax.rem(y + step, y_count)

    def at_z(step, row):
        return 4 * lax.rem(z + step + z_count, z_count) + 2 * row + core, lon

    partner = (lat + 1 - 2 * core, lon)
    far_steps = [near_count * i for i in range(1, far_count)]
    near_steps = [i if 2 * i <= near_count else i - near_count for i in range(1, near_count)]

    loads = [
        pltpu.make_async_copy(src, dst, load_sem.at[i])
        for i, (src, dst) in enumerate(
            (
                (exps_hbm, exps),
                (codes_hbm, codes),
                (cot_hbm, cot),
                (up_hbm, up_kernel),
                (mix_hbm, mix_kernel),
                (bias_hbm, bias),
            )
        )
    ]
    barrier = pltpu.get_barrier_semaphore()
    up, down, left, right = partners = halo_partners(lat, lon, lat_count, lon_count)
    greeted = [(a, b) for a in (up, down) for b in (left, lon, right)] + [(lat, left), (lat, right)]
    greeted += [partner, at_x(1), at_x(2), at_x(-1)]
    greeted += [at_y(step) for step in range(1, y_count)]
    far_all = sorted({step % z_count for base in far_steps for step in (base, -base)})
    near_all = sorted({step % z_count for base in near_steps for step in (base, -base)})
    greeted += [at_z(step, x_hi) for step in far_all + near_all]
    greeted += [at_z(step, 1 - x_hi) for step in [0] + near_all]
    for to in greeted[:8]:
        pl.semaphore_signal(barrier, inc=1, device_id=to, device_id_type=MESH)
    for load in loads:
        load.start()
    for to in greeted[8:]:
        pl.semaphore_signal(barrier, inc=1, device_id=to, device_id_type=MESH)
    for load in loads[:3]:
        load.wait()
    halo_fill(codes, exps, cot, grid, own, cot_wide, row_out, col_out, corner_out)
    pl.semaphore_wait(barrier, len(greeted))
    halo = halo_copies(
        partners, lat, lon, row_out, col_out, corner_out, row_in, col_in, corner_in, halo_send, halo_recv
    )
    for copy in reversed(halo):
        copy.start()
    for load in loads[3:]:
        load.wait()
    for i in range(9):
        back_mix[i * COUT : (i + 1) * COUT, :] = mix_kernel[i].astype(F32).T.astype(BF16)
    halo_place(halo, lat, lat_count, grid, row_in, col_in, corner_in)

    def core_start(part):
        fetch(sums.at[1 - core, part], core_in.at[part], core_sem.at[0, part], core_sem.at[1, part], partner)

    y_steps = sorted(range(1, y_count), key=lambda step: -min(step, y_count - step))

    def core_end(part):
        await_bytes(core_in.at[part], core_sem.at[1, part])
        merged = sums[core, part].astype(F32) + core_in[part].astype(F32)
        x_out[part] = merged.astype(BF16).reshape(x_out.shape[1:])

    def mix_first():
        await_bytes(mix_core_in, core_sem.at[1, MIX])
        mix_y_out[...] = (mix_sums[core].astype(F32) + mix_core_in[...].astype(F32)).astype(BF16)
        for step in y_steps:
            fetch(
                mix_y_out.at[:, lax.rem(y + step, y_count)],
                mix_y_in.at[step - 1],
                mix_sem.at[0],
                mix_sem.at[1],
                at_y(step),
            )

    def mix_second():
        await_bytes(mix_y_in, mix_sem.at[1])
        total = mix_y_out[:, y].astype(F32)
        for step in range(y_count - 1):
            total = total + mix_y_in[step].astype(F32)
        mix_x_out[...] = total.astype(BF16)
        for step in (2, 1, 3):
            fetch(
                mix_x_out.at[lax.rem(x + step, 2)], mix_x_in.at[x], mix_sem.at[2], mix_sem.at[3], at_x(step)
            )
        mix_x_in[x] = mix_x_out[x_lo]

    def summed(ref, count):
        total = ref[0].astype(F32)
        for i in range(1, count):
            total = total + ref[i].astype(F32)
        return total

    def mix_third():
        await_bytes(mix_x_in.at[pl.ds(0, 3)], mix_sem.at[3])
        mix_far[far_at] = summed(mix_x_in, 4).astype(BF16)
        for step in far_steps:
            fetch(mix_far.at[far_at], mix_far.at[far_at], far_sem.at[0, MIX], far_sem.at[1, MIX], at_z(step, x_hi))

    def mix_fourth():
        await_bytes(mix_far.at[pl.ds(0, far_count - 1)], far_sem.at[1, MIX])
        mix_near[near_at] = summed(mix_far, far_count).astype(BF16)
        for step in near_steps:
            fetch(
                mix_near.at[near_at], mix_near.at[near_at], near_sem.at[0, MIX], near_sem.at[1, MIX], at_z(step, x_hi)
            )

    def mix_fifth():
        await_bytes(mix_near.at[pl.ds(0, near_count - 1)], near_sem.at[1, MIX])
        mix_final[core] = summed(mix_near, near_count) * scale
        fetch(mix_final.at[core], mix_final.at[core], final_sem.at[0, MIX], final_sem.at[1, MIX], partner)

    def mix_finish():
        await_bytes(mix_final.at[0], final_sem.at[1, MIX])
        tap = 0
        for owner, count in enumerate(MIX_TAPS):
            for i in range(count):
                mix_out[tap] = mix_final[owner, i * 8 : i * 8 + 8, :]
                tap += 1

    def x_start(part):
        core_end(part)
        for step in (2, 1, 3):
            fetch(
                x_out.at[part, lax.rem(x + step, 4)],
                x_in.at[part, step - 1],
                x_sem.at[0, part],
                x_sem.at[1, part],
                at_x(step),
            )

    def y_start(part):
        await_bytes(x_in.at[part], x_sem.at[1, part])
        total = x_out[part, x].astype(F32)
        for step in range(3):
            total = total + x_in[part, step].astype(F32)
        y_out[part] = total.astype(BF16)
        for step in y_steps:
            fetch(
                y_out.at[part, lax.rem(y + step, y_count)],
                y_in.at[part, step - 1],
                y_sem.at[0, part],
                y_sem.at[1, part],
                at_y(step),
            )

    far_at, near_at = z // near_count, lax.rem(z, near_count)

    def far_start(part):
        await_bytes(y_in.at[part], y_sem.at[1, part])
        total = y_out[part, y].astype(F32)
        for step in range(y_count - 1):
            total = total + y_in[part, step].astype(F32)
        far_send(part, total)

    def far_send(part, total):
        far[part, far_at] = total.astype(BF16)
        for step in far_steps:
            fetch(far.at[part, far_at], far.at[part, far_at], far_sem.at[0, part], far_sem.at[1, part], at_z(step, x_hi))

    def near_start(part):
        await_bytes(far.at[part, pl.ds(0, far_count - 1)], far_sem.at[1, part])
        total = far[part, 0].astype(F32)
        for i in range(1, far_count):
            total = total + far[part, i].astype(F32)
        slot = 2 * near_at + x_hi
        near[part, slot] = total.astype(BF16)
        for to in [at_z(step, 1 - x_hi) for step in [0] + near_steps] + [at_z(step, x_hi) for step in near_steps]:
            fetch(near.at[part, slot], near.at[part, slot], near_sem.at[0, part], near_sem.at[1, part], to)

    def final_start(part):
        await_bytes(near.at[part, pl.ds(0, 2 * near_count - 1)], near_sem.at[1, part])
        for row in range(2):
            total = near[part, row].astype(F32)
            for i in range(1, near_count):
                total = total + near[part, 2 * i + row].astype(F32)
            final[part, core, row] = total * scale
        fetch(
            final.at[part, core], final.at[part, core], final_sem.at[0, part], final_sem.at[1, part], partner
        )

    def finish(part):
        await_bytes(final.at[part, 0], final_sem.at[1, part])
        for w in range(4):
            for i in range(2):
                up_out[w, 2 * part + i] = final[part, w // 2, w % 2, :, i * COUT : (i + 1) * COUT]

    slope, outside = forward_part(lat, lat_count, grid, up_kernel, bias, act)
    act_patches = patches(positions(act, INNER, 0), False)
    mix_part_sums(grid, act_patches, mix_sums)
    fetch(mix_sums.at[1 - core], mix_core_in, core_sem.at[0, MIX], core_sem.at[1, MIX], partner)
    backward_part(grid, back_mix, slope, outside, pre_grad)
    up_part_sums(grid, pre_grad, 0, sums)
    core_start(0)
    up_part_sums(grid, pre_grad, 1, sums)
    core_start(1)
    for part in UP:
        x_start(part)
    mix_first()
    for part in UP:
        y_start(part)
    mix_second()
    section_part(act_patches, mix_kernel, staged, out_wide, section)
    mix_third()
    for part in UP:
        far_start(part)
    input_part(pre_grad, up_kernel, act, input_grad)
    mix_fourth()
    for part in UP:
        near_start(part)
    mix_fifth()
    for part in UP:
        final_start(part)
    mix_finish()
    for copy in halo:
        copy.wait_send()
    await_bytes(mix_y_in, mix_sem.at[0])
    await_bytes(mix_x_in.at[pl.ds(0, 3)], mix_sem.at[2])
    await_bytes(mix_core_in, core_sem.at[0, MIX])
    await_bytes(mix_far.at[pl.ds(0, far_count - 1)], far_sem.at[0, MIX])
    await_bytes(mix_near.at[pl.ds(0, near_count - 1)], near_sem.at[0, MIX])
    await_bytes(mix_final.at[0], final_sem.at[0, MIX])
    for part in UP:
        await_bytes(x_in.at[part], x_sem.at[0, part])
        await_bytes(y_in.at[part], y_sem.at[0, part])
        await_bytes(core_in.at[part], core_sem.at[0, part])
        await_bytes(far.at[part, pl.ds(0, far_count - 1)], far_sem.at[0, part])
        await_bytes(near.at[part, pl.ds(0, 2 * near_count - 1)], near_sem.at[0, part])
        await_bytes(final.at[part, 0], final_sem.at[0, part])
    for part in UP:
        finish(part)


def write_kernel(*refs):
    copies = [pltpu.make_async_copy(refs[i], refs[4 + i], refs[8].at[i]) for i in range(4)]
    for copy in copies:
        copy.start()
    for copy in copies:
        copy.wait()


def shards(elem_codes, block_exps, up_kernel, up_bias, mix_kernel, cotangent):
    lat_count, lon_count = lax.axis_size("lat"), lax.axis_size("lon")
    y_count, z_count = lon_count // 2, lat_count // 4
    far_count, near_count = z_plan(z_count)
    out_cells = 4 * CELLS * lat_count * lon_count
    operands = (
        elem_codes.reshape(CELLS, CIN),
        block_exps.transpose(1, 2, 0).reshape(COLS * CIN // BLOCK, ROWS),
        cotangent.reshape(4 * CELLS, COUT),
        up_kernel.reshape(16, CIN, COUT),
        up_bias.reshape(1, COUT),
        mix_kernel.reshape(9, COUT, COUT),
    )
    dma = pltpu.SemaphoreType.DMA
    results = pl.pallas_call(
        functools.partial(section_kernel, lat_count, lon_count, 1.0 / math.sqrt(out_cells)),
        out_shape=(
            pltpu.VMEM((4 * CELLS, COUT), BF16),
            pltpu.VMEM((CELLS, CIN), F32),
            pltpu.VMEM((4, 4, LON_ALL, COUT), F32),
            pltpu.VMEM((9, 8, COUT), F32),
        ),
        in_specs=[pl.BlockSpec(memory_space=pltpu.HBM)] * 6,
        out_specs=[pl.BlockSpec(memory_space=pltpu.VMEM)] * 4,
        scratch_shapes=[pltpu.VMEM(operand.shape, operand.dtype) for operand in operands]
        + [
            dma((6,)),
            pltpu.VMEM((9 * COUT, COUT), BF16),
            pltpu.VMEM((TALL, FLAT, COUT), F32),
            pltpu.VMEM((TALL, CELLS, COUT), F32),
            pltpu.VMEM((4 * CELLS, COUT), F32),
            pltpu.VMEM((2, TALL // 2, 2 * COLS, COUT), BF16),
            pltpu.VMEM((2, TALL, ROWS, COUT), BF16),
            pltpu.VMEM((4, 8, COUT), F32),
            pltpu.VMEM((2, TALL // 2, 2 * COLS, COUT), BF16),
            pltpu.VMEM((2, TALL, ROWS, COUT), BF16),
            pltpu.VMEM((4, 8, COUT), F32),
            dma((8,)),
            dma((8,)),
            pltpu.VMEM((4, FLAT, COUT), F32),
            pltpu.VMEM((4, FLAT, COUT), F32),
            pltpu.VMEM((4 * INNER, COUT), F32),
            pltpu.VMEM((4 * CELLS, COUT), F32),
            pltpu.VMEM((2, 2, 2, CIN, SPAN), BF16),
            pltpu.VMEM((2, 2, CIN, SPAN), BF16),
            pltpu.VMEM((2, 4, y_count, 16, SPAN), BF16),
            pltpu.VMEM((2, 3, y_count, 16, SPAN), BF16),
            pltpu.VMEM((2, y_count, 16, SPAN), BF16),
            pltpu.VMEM((2, y_count - 1, 16, SPAN), BF16),
            pltpu.VMEM((2, 2, y_count, MIX_ROWS, COUT), BF16),
            pltpu.VMEM((2, y_count, MIX_ROWS, COUT), BF16),
            pltpu.VMEM((2, y_count, MIX_ROWS, COUT), BF16),
            pltpu.VMEM((y_count - 1, 2, MIX_ROWS, COUT), BF16),
            pltpu.VMEM((2, MIX_ROWS, COUT), BF16),
            pltpu.VMEM((4, MIX_ROWS, COUT), BF16),
            pltpu.VMEM((far_count, MIX_ROWS, COUT), BF16),
            pltpu.VMEM((near_count, MIX_ROWS, COUT), BF16),
            pltpu.VMEM((2, MIX_ROWS, COUT), F32),
            pltpu.VMEM((2, far_count, 16, SPAN), BF16),
            pltpu.VMEM((2, 2 * near_count, 16, SPAN), BF16),
            pltpu.VMEM((2, 2, 2, 16, SPAN), F32),
            dma((2, PARTS)),
            dma((2, 2)),
            dma((2, 2)),
            dma((2, PARTS)),
            dma((2, PARTS)),
            dma((2, PARTS)),
            dma((4,)),
        ],
        compiler_params=pltpu.CompilerParams(
            collective_id=0, has_side_effects=True, vmem_limit_bytes=40 * 2**20
        ),
    )(*[pltpu.with_memory_space_constraint(operand, pltpu.HBM) for operand in operands])
    section, input_grad, up_part, mix_part = pl.pallas_call(
        write_kernel,
        out_shape=tuple(jax.ShapeDtypeStruct(result.shape, result.dtype) for result in results),
        in_specs=[pl.BlockSpec(memory_space=pltpu.VMEM)] * 4,
        out_specs=[pl.BlockSpec(memory_space=pltpu.HBM)] * 4,
        scratch_shapes=[dma((4,))],
        compiler_params=pltpu.CompilerParams(vmem_limit_bytes=8 * 2**20),
    )(*results)
    return (
        section.reshape(2 * ROWS, 2 * COLS, COUT),
        input_grad.reshape(ROWS, COLS, CIN),
        up_part,
        mix_part.reshape(3, 3, 8, COUT),
    )


def solution(mesh):
    placed = (P("lat", "lon", None), P("lat", "lon", None), P(), P(), P(), P("lat", "lon", None))
    return jax.shard_map(
        shards,
        mesh=mesh,
        in_specs=placed,
        out_specs=(
            P("lat", "lon", None),
            P("lat", "lon", None),
            P(None, None, "lon", None),
            P(None, None, "lon", None),
        ),
        check_vma=False,
    )
```
